32 devices in a mesh: dp: 4 (over y, x), section: 2 (over core), seq: 4 (over z).
Axes of the slice: x: 2, y: 2, z: 4, core: 2. Of those that a mesh axis runs over, the one named last changes fastest.
Arguments:
- source: bfloat16 [16, 512, 256], P('dp', 'seq'), may hold values from -6 to 6
- position: bfloat16 [16, 512, 256], P('dp', 'seq'), may hold values from -6 to 6
- lengths: int32 [16], P('dp'), may hold values from 128 to 512, as said below
- target: float32 [16, 300, 256], P('dp'), may hold values from -6 to 6
- points: float32 [16, 300, 2], P('dp'), may hold values from 0.05 to 0.95
- grad_output: float32 [16, 300, 256], P('dp'), may hold values from -6 to 6
- attn: bfloat16 [2, 3, 256, 256], replicated, may hold values from -0.375 to 0.375
- attn_out: bfloat16 [3, 256, 256], replicated, may hold values from -1.5 to 1.5
- attn_bias: float32 [3, 3, 256], replicated, may hold values from -2 to 2
- cross: bfloat16 [5, 256, 256], replicated, may hold values from -0.5 to 0.5
- ffn_in: bfloat16 [2, 256, 2048], replicated, may hold values from -0.375 to 0.375
- ffn_in_bias: float32 [2, 2048], replicated, may hold values from -2 to 2
- ffn_out: bfloat16 [2, 2048, 256], replicated, may hold values from -0.125 to 0.125
- ffn_out_bias: float32 [2, 256], replicated, may hold values from -2 to 2
- norm_gain: float32 [5, 256], replicated, may hold values from 0.25 to 1.75
- norm_bias: float32 [5, 256], replicated, may hold values from -2 to 2
- query_embed: float32 [300, 256], replicated, may hold values from -6 to 6
Outputs:
- decoder_output: float32 [16, 300, 256], P(('dp', 'section'))
- grad_source: float32 [16, 512, 256], P(('dp', 'section'), 'seq')
- grad_target: float32 [16, 300, 256], P(('dp', 'section'))
- grad_attn: float32 [2, 3, 256, 256], replicated
- grad_attn_out: float32 [3, 256, 256], replicated
- grad_attn_bias: float32 [3, 3, 256], replicated
- grad_cross: float32 [5, 256, 256], replicated
- grad_ffn_in: float32 [2, 256, 2048], replicated
- grad_ffn_in_bias: float32 [2, 2048], replicated
- grad_ffn_out: float32 [2, 2048, 256], replicated
- grad_ffn_out_bias: float32 [2, 256], replicated
- grad_norm_gain: float32 [5, 256], replicated
- grad_norm_bias: float32 [5, 256], replicated
- grad_query_embed: float32 [300, 256], replicated
The draws below stay inside these ranges and needn't reach their ends.
Inputs may be any that keep to these rules, and one draw needn't show every extreme that they name: `lengths`: in each aligned block of 4 images (those of one index of dp) at least one image, which one drawn from the seed, has length 512.
All inputs are finite; a program needn't handle non-finite values.
Results may differ from the reference program's by a relative error of at most 0.024.
The reference program's roundings to bfloat16 on the way count: a program that leaves them out, or rounds other values in their place, can miss the bound.
Values may be sent and summed in bfloat16 or wider, within the bound.
No kernel may reach another device: no remote copies, remote signals or barrier semaphores. Data moves between devices by JAX's collectives and lax.ppermute only.
A program may use at most 320 MiB of HBM per device.

```python
import math
import jax
import jax.numpy as jnp
from jax import lax

D = 256
HEADS = 8
FF = 2048
NQ = 300
MB = 4
SEQ_LEN = 512
IMAGES = 16


def draw_lengths(key, part):
    key = jax.random.fold_in(key, 7)
    spread_key, pick_key = jax.random.split(key)
    spread = jax.random.randint(spread_key, (IMAGES,), SEQ_LEN // 4, SEQ_LEN + 1)
    picked = jax.random.randint(pick_key, (IMAGES // MB,), 0, MB)
    place = jnp.arange(IMAGES) % MB
    full = place == jnp.repeat(picked, MB)
    return jnp.where(full, SEQ_LEN, spread).astype(jnp.int32)


def block_scale(rng, extent, cuts, low, top_value):
    def one(dim, blocks):
        draws = jax.random.uniform(jax.random.fold_in(jax.random.fold_in(rng, 6), dim), (blocks,), jnp.float32, low / len(cuts), top_value / len(cuts))
        return jnp.repeat(jnp.exp(draws), extent[dim] // blocks).reshape((-1,) + (1,) * (len(extent) - dim - 1))

    factor_of = one(*cuts[0])
    for cut in cuts[1:]:
        factor_of = factor_of * one(*cut)
    return factor_of


def noise(key, dims, scale, bound, cuts=(), held_as=jnp.bfloat16):
    values = jax.random.normal(key, dims, jnp.float32) * scale
    if len(cuts) > 0:
        values = block_scale(key, dims, cuts, -0.22, 0.18) * values
    return jnp.clip(values, min=-bound, max=bound).astype(held_as)


def setup_inputs(seed: int = 0) -> dict:
    splits = jax.random.split(jax.random.key(seed), 18)
    source = noise(splits[0], (IMAGES, SEQ_LEN, D), 1.0, 6.0, ((0, 4), (1, 4)))
    position = noise(splits[1], (IMAGES, SEQ_LEN, D), 1.0, 6.0, ((0, 4), (1, 4)))
    lengths = draw_lengths(jax.random.fold_in(splits[17], 71), 0)
    target = noise(splits[3], (IMAGES, NQ, D), 1.0, 6.0, ((0, 4),), jnp.float32)
    points = jnp.clip(0.05 + 0.9 * jax.random.uniform(splits[4], (IMAGES, NQ, 2), jnp.float32) ** block_scale(splits[4], (IMAGES, NQ, 2), ((0, 4),), -0.2, 0.2), 0.05, 0.95)
    grad_output = noise(splits[5], (IMAGES, NQ, D), 1.0, 6.0, ((0, 4),), jnp.float32)
    attn = noise(splits[6], (2, 3, D, D), D ** -0.5, 0.375)
    attn_out = noise(splits[7], (3, D, D), 16 ** -0.5, 1.5)
    attn_bias = noise(splits[8], (3, 3, D), 0.3, 2.0, (), jnp.float32)
    cross = noise(splits[9], (5, D, D), (D // 2) ** -0.5, 0.5)
    ffn_in = noise(splits[10], (2, D, FF), D ** -0.5, 0.375)
    ffn_in_bias = noise(splits[11], (2, FF), 0.3, 2.0, (), jnp.float32)
    ffn_out = noise(splits[12], (2, FF, D), FF ** -0.5, 0.125)
    ffn_out_bias = noise(splits[13], (2, D), 0.3, 2.0, (), jnp.float32)
    norm_gain = jnp.clip(1.0 + 0.15 * jax.random.normal(splits[14], (5, D), jnp.float32), 0.25, 1.75)
    norm_bias = noise(splits[15], (5, D), 0.3, 2.0, (), jnp.float32)
    query_embed = noise(splits[16], (NQ, D), 1.0, 6.0, (), jnp.float32)
    return {"source": source, "position": position, "lengths": lengths, "target": target, "points": points, "grad_output": grad_output, "attn": attn, "attn_out": attn_out, "attn_bias": attn_bias, "cross": cross, "ffn_in": ffn_in, "ffn_in_bias": ffn_in_bias, "ffn_out": ffn_out, "ffn_out_bias": ffn_out_bias, "norm_gain": norm_gain, "norm_bias": norm_bias, "query_embed": query_embed}


HIGHEST_PRECISION = lax.Precision.HIGHEST
EPSILON = 1e-05
NEGATIVE = -1e+30

@jax.custom_vjp
def low(v):
    return lax.optimization_barrier(v.astype(jnp.bfloat16)).astype(jnp.float32)

@jax.custom_vjp
def low_back(v):
    return v

def low_keep(v):
    return (low(v), None)

def low_pass(kept, grad):
    return (grad,)

def back_keep(v):
    return (v, None)

def back_low(kept, grad):
    return (low(grad),)
low.defvjp(low_keep, low_pass)
low_back.defvjp(back_keep, back_low)

def product(left, right):
    return jnp.dot(left, right, precision=HIGHEST_PRECISION)

def norm_apply(value, gain, shift):
    center = value - lax.optimization_barrier(jnp.mean(value, axis=-1, keepdims=True))
    scale = lax.rsqrt(lax.optimization_barrier(jnp.mean(center * center, axis=-1, keepdims=True)) + EPSILON)
    return center * scale * gain + shift

def sine_embed(points, width):
    half_width = width // 2
    column = jnp.arange(half_width)
    period = 10000.0 ** ((2 * (column // 2)).astype(jnp.float32) / half_width)

    def embed(coordinate):
        angle = coordinate[..., None] * (2.0 * math.pi) / period
        return jnp.where(column % 2 == 0, jnp.sin(angle), jnp.cos(angle))
    return jnp.concatenate([embed(points[..., 1]), embed(points[..., 0])], axis=-1)

def split_heads(value, heads):
    return value.reshape(value.shape[0], heads, value.shape[1] // heads)

def join_heads(first, second, heads):
    joined = jnp.concatenate([split_heads(first, heads), split_heads(second, heads)], axis=2)
    return joined.reshape(first.shape[0], 2 * first.shape[1])

@jax.checkpoint
def attention_block(queries, keys, values, valid):
    scores = low_back(jnp.einsum('qhd,khd->hqk', split_heads(queries, HEADS), split_heads(keys, HEADS), precision=HIGHEST_PRECISION))
    masked = jnp.where(valid, scores, NEGATIVE)
    highest = lax.optimization_barrier(jnp.max(masked, axis=-1, keepdims=True))
    weights = jnp.where(valid, jnp.exp(masked - highest), 0.0)
    probs = low(weights / lax.optimization_barrier(jnp.sum(weights, axis=-1, keepdims=True)))
    mixed = jnp.einsum('hqk,khd->qhd', probs, split_heads(values, HEADS), precision=HIGHEST_PRECISION)
    return mixed.reshape(mixed.shape[0], -1)

def feed_forward(value, w_in, b_in, w_out, b_out):
    inner = low_back(product(low(value), w_in) + b_in)
    return low_back(product(low(jax.nn.gelu(inner)), w_out) + b_out)

def image_forward(weights, source, position, length, target, points):
    attn, attn_out, attn_bias, cross, ffn_in, ffn_in_bias, ffn_out, ffn_out_bias, norm_gain, norm_bias, query_embed = weights
    width = source.shape[1]
    head = width // HEADS
    scale = head ** (-0.5)
    cross_scale = (2 * head) ** (-0.5)
    valid = jnp.arange(source.shape[0]) < length
    everyone = jnp.arange(target.shape[0]) >= 0
    mixed_in = low(source + position)
    query = low(low_back((product(mixed_in, attn[0, 0]) + attn_bias[0, 0]) * scale))
    key = low(low_back(product(mixed_in, attn[0, 1])))
    value = low(low_back(product(source, attn[0, 2]) + attn_bias[0, 1]))
    mixed = low(low_back(attention_block(query, key, value, valid)))
    first = norm_apply(source + low_back(product(mixed, attn_out[0]) + attn_bias[0, 2]), norm_gain[0], norm_bias[0])
    second = norm_apply(first + feed_forward(first, ffn_in[0], ffn_in_bias[0], ffn_out[0], ffn_out_bias[0]), norm_gain[1], norm_bias[1])
    memory = low(low_back(second))
    self_in = low(target + query_embed)
    target_low = low(target)
    dec_query = low(low_back((product(self_in, attn[1, 0]) + attn_bias[1, 0]) * scale))
    dec_key = low(low_back(product(self_in, attn[1, 1])))
    dec_value = low(low_back(product(target_low, attn[1, 2]) + attn_bias[1, 1]))
    dec_mixed = low(low_back(attention_block(dec_query, dec_key, dec_value, everyone)))
    dec_first = norm_apply(target + low_back(product(dec_mixed, attn_out[1]) + attn_bias[1, 2]), norm_gain[2], norm_bias[2])
    first_low = low(dec_first)
    content_key = low(low_back(product(memory, cross[2])))
    place_key = low(low_back(product(position, cross[3])))
    cross_value = low(low_back(product(memory, cross[4]) + attn_bias[2, 1]))
    content_query = low(low_back((product(first_low, cross[0]) + attn_bias[2, 0]) * cross_scale))
    place_query = low(low_back(product(low(sine_embed(points, width)), cross[1]) * cross_scale))
    joined_query = join_heads(content_query, place_query, HEADS)
    joined_key = join_heads(content_key, place_key, HEADS)
    cross_mixed = low(low_back(attention_block(joined_query, joined_key, cross_value, valid)))
    dec_second = norm_apply(dec_first + low_back(product(cross_mixed, attn_out[2]) + attn_bias[2, 2]), norm_gain[3], norm_bias[3])
    return norm_apply(dec_second + feed_forward(dec_second, ffn_in[1], ffn_in_bias[1], ffn_out[1], ffn_out_bias[1]), norm_gain[4], norm_bias[4])

def reference(source, position, lengths, target, points, grad_output, attn, attn_out, attn_bias, cross, ffn_in, ffn_in_bias, ffn_out, ffn_out_bias, norm_gain, norm_bias, query_embed):
    weights = tuple((item.astype(jnp.float32) for item in (attn, attn_out, attn_bias, cross, ffn_in, ffn_in_bias, ffn_out, ffn_out_bias, norm_gain, norm_bias, query_embed)))
    position_f = position.astype(jnp.float32)

    def forward(source_f, target_f, weight_set):

        @jax.checkpoint
        def one_image(source_i, position_i, length_i, target_i, points_i):
            return image_forward(weight_set, source_i, position_i, length_i, target_i, points_i)

        def scan_step(carry, item):
            return (carry, one_image(*item))
        _, outputs = lax.scan(scan_step, jnp.zeros((), jnp.float32), (source_f, position_f, lengths, target_f, points))
        return outputs
    outputs, backward = jax.vjp(forward, source.astype(jnp.float32), target, weights)
    grad_source, grad_target, grad_weights = backward(grad_output)
    return (outputs, grad_source, grad_target, grad_weights[0], grad_weights[1], grad_weights[2], grad_weights[3], grad_weights[4], grad_weights[5], grad_weights[6], grad_weights[7], grad_weights[8], grad_weights[9], grad_weights[10])
```

```python
import functools
import math
from types import SimpleNamespace

import jax
import jax.numpy as jnp
import numpy as np
from jax import lax
from jax.experimental import pallas as pl
from jax.experimental.pallas import tpu as pltpu
from jax.sharding import PartitionSpec as P

HEADS = 8


EPSILON = 1e-05
NEGATIVE = -1e30


def swapped(block, axis, bit):
    count = lax.axis_size(axis)
    route = []
    for low in range(count):
        high = low | 1 << bit
        if high != low and high < count:
            route += [(low, high), (high, low)]
    return lax.ppermute(block, axis, route)


def lower(value):
    return value.astype(jnp.bfloat16)


def product(left, right):
    return jnp.dot(left, right, preferred_element_type=jnp.float32)


def left_transposed(left, right):
    return lax.dot_general(
        left, right, (((0,), (0,)), ((), ())), preferred_element_type=jnp.float32
    )


def right_transposed(left, right):
    return lax.dot_general(
        left, right, (((1,), (1,)), ((), ())), preferred_element_type=jnp.float32
    )


def column_sum(value):
    return jnp.sum(value.astype(jnp.float32), axis=0)


def norm_apply(value, gain, shift):
    center = value - jnp.mean(value, axis=-1, keepdims=True)
    scale = lax.rsqrt(jnp.mean(center * center, axis=-1, keepdims=True) + EPSILON)
    return center * scale * gain + shift


def activate(value):
    return jax.nn.gelu(value)


def sine_embed(points, width):
    half_width = width // 2
    column = jnp.arange(half_width)
    period = 10000.0 ** ((2 * (column // 2)).astype(jnp.float32) / half_width)

    def embed(coordinate):
        angle = coordinate[..., None] * (2.0 * math.pi) / period
        return jnp.where(column % 2 == 0, jnp.sin(angle), jnp.cos(angle))

    return jnp.concatenate([embed(points[..., 1]), embed(points[..., 0])], axis=-1)


def split_heads(value, heads):
    return value.reshape(value.shape[0], heads, value.shape[1] // heads)


def join_heads(first, second, heads):
    joined = jnp.concatenate([split_heads(first, heads), split_heads(second, heads)], axis=2)
    return joined.reshape(first.shape[0], 2 * first.shape[1])


def part_heads(value, heads):
    count = value.shape[0]
    split = split_heads(value, heads)
    middle = split.shape[2] // 2
    return (split[:, :, :middle].reshape(count, -1), split[:, :, middle:].reshape(count, -1))


def column_block(value, start, count):
    return lax.dynamic_slice_in_dim(value, start, count, 2)


def score_heads(queries, keys, heads):
    return jnp.einsum(
        "qhd,khd->hqk",
        split_heads(queries, heads),
        split_heads(keys, heads),
        preferred_element_type=jnp.float32,
    )


def mix_heads(probs, values, heads):
    mixed = jnp.einsum(
        "hqk,khd->qhd", probs, split_heads(values, heads), preferred_element_type=jnp.float32
    )
    return mixed.reshape(mixed.shape[0], -1)


def attend(queries, keys, values, valid, heads):
    masked = jnp.where(valid, score_heads(queries, keys, heads), NEGATIVE)
    highest = jnp.max(masked, axis=-1, keepdims=True)
    weights = jnp.where(valid, jnp.exp(masked - highest), 0.0)
    totals = jnp.sum(weights, axis=-1, keepdims=True)
    return (mix_heads(lower(weights / totals), values, heads), highest + jnp.log(totals))


def attend_back(queries, keys, values, valid, heads, log_total, grad_mixed):
    probs = jnp.where(valid, jnp.exp(score_heads(queries, keys, heads) - log_total), 0.0)
    grad_probs = score_heads(grad_mixed, values, heads)
    inner = jnp.sum(probs * grad_probs, axis=-1, keepdims=True)
    grad_scores = lower(probs * (grad_probs - inner))
    return (lower(probs), grad_scores, mix_heads(grad_scores, keys, heads))


def key_terms(grad_scores, probs, queries, grad_mixed, heads):
    grad_keys = jnp.einsum(
        "hqk,qhd->khd", grad_scores, split_heads(queries, heads), preferred_element_type=jnp.float32
    )
    grad_values = jnp.einsum(
        "hqk,qhd->khd", probs, split_heads(grad_mixed, heads), preferred_element_type=jnp.float32
    )
    count = grad_keys.shape[0]
    return jnp.concatenate([grad_keys.reshape(count, -1), grad_values.reshape(count, -1)], axis=1)


def encoder_forward(source, position, valid, params, heads, scale):
    width = source.shape[1]
    source_f = source.astype(jnp.float32)
    mixed_in = lower(source_f + position.astype(jnp.float32))
    query = lower((product(mixed_in, params.attn[0, 0]) + params.attn_bias[0, 0]) * scale)
    key = lower(product(mixed_in, params.attn[0, 1]))
    value = lower(product(source, params.attn[0, 2]) + params.attn_bias[0, 1])
    pairs = lax.all_gather(jnp.concatenate([key, value], axis=1), "seq", axis=0, tiled=True)
    mixed, log_total = attend(query, pairs[:, :width], pairs[:, width:], valid, heads)
    mixed = lower(mixed)
    first_sum = source_f + product(mixed, params.attn_out[0]) + params.attn_bias[0, 2]
    first = norm_apply(first_sum, params.norm_gain[0], params.norm_bias[0])
    inner = product(lower(first), params.ffn_in[0]) + params.ffn_in_bias[0]
    second_sum = (
        first + product(lower(activate(inner)), params.ffn_out[0]) + params.ffn_out_bias[0]
    )
    memory = norm_apply(second_sum, params.norm_gain[1], params.norm_bias[1])
    stash = dict(
        query=query,
        pairs=pairs,
        log_total=log_total,
        mixed=mixed,
        first_sum=first_sum,
        inner=inner,
        second_sum=second_sum,
    )
    return (lower(memory), stash)


def encoder_backward(kept, source, position, valid, grad_memory, params, heads, scale):
    stash = SimpleNamespace(**kept)
    width = source.shape[1]
    rows = source.shape[0]
    query = stash.query
    pairs = stash.pairs
    _, last_back = jax.vjp(
        norm_apply, stash.second_sum, params.norm_gain[1], params.norm_bias[1]
    )
    grad_second, gain_two, bias_two = last_back(grad_memory)
    first, first_back = jax.vjp(
        norm_apply, stash.first_sum, params.norm_gain[0], params.norm_bias[0]
    )
    activated, gelu_back = jax.vjp(activate, stash.inner)
    grad_branch = lower(grad_second)
    grad_inner = lower(gelu_back(right_transposed(grad_branch, params.ffn_out[0]))[0])
    grad_first_sum, gain_one, bias_one = first_back(
        grad_second + right_transposed(grad_inner, params.ffn_in[0])
    )
    grad_attention = lower(grad_first_sum)
    grad_mixed = lower(right_transposed(grad_attention, params.attn_out[0]))
    probs, grad_scores, grad_query = attend_back(
        query, pairs[:, :width], pairs[:, width:], valid, heads, stash.log_total, grad_mixed
    )
    start = jnp.int32(0)
    own = lax.psum_scatter(
        key_terms(
            column_block(grad_scores, start, lax.axis_size("seq") * rows),
            column_block(probs, start, lax.axis_size("seq") * rows),
            query,
            grad_mixed,
            heads,
        ).astype(jnp.bfloat16),
        "seq",
        scatter_dimension=0,
        tiled=True,
    ).astype(jnp.float32)
    grad_key = lower(own[:, :width])
    grad_value = lower(own[:, width:])
    grad_query = lower(grad_query)
    mixed_in = lower(source.astype(jnp.float32) + position.astype(jnp.float32))
    grad_source = (
        grad_first_sum
        + scale * right_transposed(grad_query, params.attn[0, 0])
        + right_transposed(grad_key, params.attn[0, 1])
        + right_transposed(grad_value, params.attn[0, 2])
    )
    grads = dict(
        attn=jnp.stack(
            [
                scale * left_transposed(mixed_in, grad_query),
                left_transposed(mixed_in, grad_key),
                left_transposed(source, grad_value),
            ]
        ),
        attn_out=left_transposed(stash.mixed, grad_attention),
        attn_bias=jnp.stack(
            [scale * column_sum(grad_query), column_sum(grad_value), column_sum(grad_attention)]
        ),
        ffn_in=left_transposed(lower(first), grad_inner),
        ffn_in_bias=column_sum(grad_inner),
        ffn_out=left_transposed(lower(activated), grad_branch),
        ffn_out_bias=column_sum(grad_branch),
        norm_gain=jnp.stack([gain_one, gain_two]),
        norm_bias=jnp.stack([bias_one, bias_two]),
    )
    return (grad_source, grads)


def decoder_step(
    target, points, memory, position, valid, grad_output, params, heads, scale, cross_scale
):
    width = target.shape[1]
    rows = memory.shape[0]
    attn = params.attn
    attn_bias = params.attn_bias
    cross = params.cross
    sine = lower(sine_embed(points, width))
    target_low = lower(target)
    self_in = lower(target + params.query_embed)
    query = lower((product(self_in, attn[1, 0]) + attn_bias[1, 0]) * scale)
    key = lower(product(self_in, attn[1, 1]))
    value = lower(product(target_low, attn[1, 2]) + attn_bias[1, 1])
    everyone = jnp.arange(target.shape[0]) >= 0
    mixed, log_self = attend(query, key, value, everyone, heads)
    mixed = lower(mixed)
    first_sum = target + product(mixed, params.attn_out[1]) + attn_bias[1, 2]
    first, first_back = jax.vjp(
        norm_apply, first_sum, params.norm_gain[2], params.norm_bias[2]
    )
    first_low = lower(first)
    content_key = lower(product(memory, cross[2]))
    place_key = lower(product(position, cross[3]))
    cross_value = lower(product(memory, cross[4]) + attn_bias[2, 1])
    triple = lax.all_gather(
        jnp.concatenate([content_key, place_key, cross_value], axis=1), "seq", axis=0, tiled=True
    )
    content_key = triple[:, :width]
    place_key = triple[:, width : 2 * width]
    cross_value = triple[:, 2 * width :]
    content_query = lower((product(first_low, cross[0]) + attn_bias[2, 0]) * cross_scale)
    place_query = lower(product(sine, cross[1]) * cross_scale)
    joined_query = join_heads(content_query, place_query, heads)
    joined_key = join_heads(content_key, place_key, heads)
    own_start = lax.axis_index("seq") * rows
    cross_mixed, log_cross = attend(joined_query, joined_key, cross_value, valid, heads)
    cross_mixed = lower(cross_mixed)
    second_sum = first + product(cross_mixed, params.attn_out[2]) + attn_bias[2, 2]
    second, second_back = jax.vjp(
        norm_apply, second_sum, params.norm_gain[3], params.norm_bias[3]
    )
    second_low = lower(second)
    inner = product(second_low, params.ffn_in[1]) + params.ffn_in_bias[1]
    activated, gelu_back = jax.vjp(activate, inner)
    activated_low = lower(activated)
    third_sum = second + product(activated_low, params.ffn_out[1]) + params.ffn_out_bias[1]
    output, third_back = jax.vjp(
        norm_apply, third_sum, params.norm_gain[4], params.norm_bias[4]
    )
    grad_third, gain_five, bias_five = third_back(grad_output)
    grad_branch = lower(grad_third)
    grad_inner = lower(gelu_back(right_transposed(grad_branch, params.ffn_out[1]))[0])
    grad_second_sum, gain_four, bias_four = second_back(
        grad_third + right_transposed(grad_inner, params.ffn_in[1])
    )
    grad_cross_out = lower(grad_second_sum)
    grad_cross_mixed = lower(right_transposed(grad_cross_out, params.attn_out[2]))
    cross_probs, cross_scores, grad_joined = attend_back(
        joined_query, joined_key, cross_value, valid, heads, log_cross, grad_cross_mixed
    )
    own = key_terms(
        column_block(cross_scores, own_start, rows),
        column_block(cross_probs, own_start, rows),
        joined_query,
        grad_cross_mixed,
        heads,
    )
    grad_content_key, grad_place_key = part_heads(own[:, : 2 * width], heads)
    grad_content_key = lower(grad_content_key)
    grad_place_key = lower(grad_place_key)
    grad_cross_value = lower(own[:, 2 * width :])
    grad_memory = right_transposed(grad_content_key, cross[2]) + right_transposed(
        grad_cross_value, cross[4]
    )
    grad_content_query, grad_place_query = part_heads(grad_joined, heads)
    grad_content_query = lower(grad_content_query)
    grad_place_query = lower(grad_place_query)
    grad_first = grad_second_sum + cross_scale * right_transposed(grad_content_query, cross[0])
    grad_first_sum, gain_three, bias_three = first_back(grad_first)
    grad_self_out = lower(grad_first_sum)
    grad_mixed = lower(right_transposed(grad_self_out, params.attn_out[1]))
    self_probs, self_scores, grad_query = attend_back(
        query, key, value, everyone, heads, log_self, grad_mixed
    )
    pair = key_terms(self_scores, self_probs, query, grad_mixed, heads)
    grad_key = lower(pair[:, :width])
    grad_value = lower(pair[:, width:])
    grad_query = lower(grad_query)
    grad_self_in = scale * right_transposed(grad_query, attn[1, 0]) + right_transposed(
        grad_key, attn[1, 1]
    )
    grad_target = grad_first_sum + grad_self_in + right_transposed(grad_value, attn[1, 2])
    grads = dict(
        attn=jnp.stack(
            [
                scale * left_transposed(self_in, grad_query),
                left_transposed(self_in, grad_key),
                left_transposed(target_low, grad_value),
            ]
        ),
        attn_out=jnp.stack(
            [left_transposed(mixed, grad_self_out), left_transposed(cross_mixed, grad_cross_out)]
        ),
        attn_bias=jnp.stack(
            [
                jnp.stack(
                    [
                        scale * column_sum(grad_query),
                        column_sum(grad_value),
                        column_sum(grad_self_out),
                    ]
                ),
                jnp.stack(
                    [
                        cross_scale * column_sum(grad_content_query),
                        column_sum(grad_cross_value),
                        column_sum(grad_cross_out),
                    ]
                ),
            ]
        ),
        cross=jnp.stack(
            [
                cross_scale * left_transposed(first_low, grad_content_query),
                cross_scale * left_transposed(sine, grad_place_query),
                left_transposed(memory, grad_content_key),
                left_transposed(position, grad_place_key),
                left_transposed(memory, grad_cross_value),
            ]
        ),
        ffn_in=left_transposed(second_low, grad_inner),
        ffn_in_bias=column_sum(grad_inner),
        ffn_out=left_transposed(activated_low, grad_branch),
        ffn_out_bias=column_sum(grad_branch),
        norm_gain=jnp.stack([gain_three, gain_four, gain_five]),
        norm_bias=jnp.stack([bias_three, bias_four, bias_five]),
        query_embed=grad_self_in,
    )
    return (output, grad_target, lower(grad_memory), grads)


def encoder_zeros(width, inner_width):
    return dict(
        attn=jnp.zeros((3, width, width), jnp.float32),
        attn_out=jnp.zeros((width, width), jnp.float32),
        attn_bias=jnp.zeros((3, width), jnp.float32),
        ffn_in=jnp.zeros((width, inner_width), jnp.float32),
        ffn_in_bias=jnp.zeros((inner_width,), jnp.float32),
        ffn_out=jnp.zeros((inner_width, width), jnp.float32),
        ffn_out_bias=jnp.zeros((width,), jnp.float32),
        norm_gain=jnp.zeros((2, width), jnp.float32),
        norm_bias=jnp.zeros((2, width), jnp.float32),
    )


def decoder_zeros(width, inner_width, queries):
    return dict(
        attn=jnp.zeros((3, width, width), jnp.float32),
        attn_out=jnp.zeros((2, width, width), jnp.float32),
        attn_bias=jnp.zeros((2, 3, width), jnp.float32),
        cross=jnp.zeros((5, width, width), jnp.float32),
        ffn_in=jnp.zeros((width, inner_width), jnp.float32),
        ffn_in_bias=jnp.zeros((inner_width,), jnp.float32),
        ffn_out=jnp.zeros((inner_width, width), jnp.float32),
        ffn_out_bias=jnp.zeros((width,), jnp.float32),
        norm_gain=jnp.zeros((3, width), jnp.float32),
        norm_bias=jnp.zeros((3, width), jnp.float32),
        query_embed=jnp.zeros((queries, width), jnp.float32),
    )


def share_decoder(grads, share, key_share):
    scaled = {name: grads[name] * share for name in grads}
    factor = jnp.array([share, share, key_share, key_share, key_share], jnp.float32)
    scaled["cross"] = grads["cross"] * factor[:, None, None]
    bias_factor = jnp.array([[share, share, share], [share, key_share, share]], jnp.float32)
    scaled["attn_bias"] = grads["attn_bias"] * bias_factor[:, :, None]
    return scaled


def assemble(encoder, decoder):
    encoder = SimpleNamespace(**encoder)
    decoder = SimpleNamespace(**decoder)
    return (
        jnp.stack([encoder.attn, decoder.attn]),
        jnp.concatenate([encoder.attn_out[None], decoder.attn_out]),
        jnp.concatenate([encoder.attn_bias[None], decoder.attn_bias]),
        decoder.cross,
        jnp.stack([encoder.ffn_in, decoder.ffn_in]),
        jnp.stack([encoder.ffn_in_bias, decoder.ffn_in_bias]),
        jnp.stack([encoder.ffn_out, decoder.ffn_out]),
        jnp.stack([encoder.ffn_out_bias, decoder.ffn_out_bias]),
        jnp.concatenate([encoder.norm_gain, decoder.norm_gain]),
        jnp.concatenate([encoder.norm_bias, decoder.norm_bias]),
        decoder.query_embed,
    )


def select_tree(flag, chosen, other):
    return jax.tree.map(lambda first, second: jnp.where(flag, first, second), chosen, other)


def per_device(
    source,
    position,
    lengths,
    target,
    points,
    grad_output,
    attn,
    attn_out,
    attn_bias,
    cross,
    ffn_in,
    ffn_in_bias,
    ffn_out,
    ffn_out_bias,
    norm_gain,
    norm_bias,
    query_embed,
):
    params = SimpleNamespace(
        attn=attn,
        attn_out=attn_out,
        attn_bias=attn_bias,
        cross=cross,
        ffn_in=ffn_in,
        ffn_in_bias=ffn_in_bias,
        ffn_out=ffn_out,
        ffn_out_bias=ffn_out_bias,
        norm_gain=norm_gain,
        norm_bias=norm_bias,
        query_embed=query_embed,
    )
    batches, rows, width = source.shape
    heads = HEADS
    head = width // heads
    scale = head ** (-0.5)
    cross_scale = (2 * head) ** (-0.5)
    queries = target.shape[1]
    inner_width = ffn_in.shape[2]
    seq_count = lax.axis_size("seq")
    positions = jnp.arange(rows * seq_count)
    section = lax.axis_index("section")
    state = dict(
        enc=encoder_zeros(width, inner_width),
        dec=decoder_zeros(width, inner_width, queries),
        stash=dict(
            query=jnp.zeros((batches, rows, width), jnp.bfloat16),
            pairs=jnp.zeros((batches, rows * seq_count, 2 * width), jnp.bfloat16),
            log_total=jnp.zeros((batches, heads, rows, 1), jnp.float32),
            mixed=jnp.zeros((batches, rows, width), jnp.bfloat16),
            first_sum=jnp.zeros((batches, rows, width), jnp.float32),
            inner=jnp.zeros((batches, rows, inner_width), jnp.float32),
            second_sum=jnp.zeros((batches, rows, width), jnp.float32),
        ),
        source=jnp.zeros((batches, rows, width), jnp.float32),
        decoded=jnp.zeros((batches, 2, queries, width), jnp.float32),
    )
    arrived_start = jnp.zeros((rows, width), jnp.bfloat16)
    stored_start = jnp.zeros((batches, rows, width), jnp.bfloat16)

    def tick_step(carry, tick):
        current, incoming, stored = carry
        enc_batch = jnp.minimum(tick, batches - 1)
        dec_batch = jnp.maximum(tick - 1, 0)
        enc_active = jnp.logical_and(section == 0, tick < batches)
        dec_active = jnp.logical_and(section == 1, tick > 0)
        enc_valid = positions < lengths[enc_batch]
        memory, stash = encoder_forward(
            source[enc_batch], position[enc_batch], enc_valid, params, heads, scale
        )
        new_stash = {
            name: lax.dynamic_update_index_in_dim(current["stash"][name], stash[name], enc_batch, 0)
            for name in stash
        }
        dec_valid = positions < lengths[dec_batch]
        output, grad_target, grad_memory, grads = decoder_step(
            target[dec_batch],
            points[dec_batch],
            incoming,
            position[dec_batch],
            dec_valid,
            grad_output[dec_batch],
            params,
            heads,
            scale,
            cross_scale,
        )
        new_dec = jax.tree.map(jnp.add, current["dec"], grads)
        new_decoded = lax.dynamic_update_index_in_dim(
            current["decoded"], jnp.stack([output, grad_target]), dec_batch, 0
        )
        updated = dict(current)
        updated["stash"] = select_tree(enc_active, new_stash, current["stash"])
        updated["dec"] = select_tree(dec_active, new_dec, current["dec"])
        updated["decoded"] = jnp.where(dec_active, new_decoded, current["decoded"])
        outgoing = jnp.where(
            enc_active, memory, jnp.where(dec_active, grad_memory, jnp.zeros_like(memory))
        )
        arrived = swapped(outgoing, "section", 0)
        stored = jnp.where(
            tick > 0, lax.dynamic_update_index_in_dim(stored, arrived, dec_batch, 0), stored
        )
        return ((updated, arrived, stored), None)

    (state, _, stored), _ = lax.scan(
        tick_step, (state, arrived_start, stored_start), jnp.arange(batches + 1)
    )

    def back_step(current, batch):
        valid = positions < lengths[batch]
        stash = {name: current["stash"][name][batch] for name in current["stash"]}
        grad_source, grads = encoder_backward(
            stash,
            source[batch],
            position[batch],
            valid,
            stored[batch].astype(jnp.float32),
            params,
            heads,
            scale,
        )
        active = section == 0
        updated = dict(current)
        updated["enc"] = select_tree(
            active, jax.tree.map(jnp.add, current["enc"], grads), current["enc"]
        )
        updated["source"] = jnp.where(
            active,
            lax.dynamic_update_index_in_dim(current["source"], grad_source, batch, 0),
            current["source"],
        )
        return (updated, None)

    state, _ = lax.scan(back_step, state, jnp.arange(batches))
    share = 1.0 / seq_count
    key_share = 1.0
    encoder = state["enc"]
    decoder = share_decoder(state["dec"], share, key_share)
    half = batches // 2
    source_upper = state["source"][half:]
    decoded_lower = state["decoded"][:half]
    parts = assemble(encoder, decoder)
    summed = lax.psum(
        (
            parts[0],
            parts[1],
            parts[2],
            parts[3],
            parts[4],
            parts[5],
            parts[6],
            parts[7],
            parts[8],
            parts[9],
            parts[10],
        ),
        ("dp", "section", "seq"),
    )
    other_source, other_decoded = (
        swapped(source_upper.astype(jnp.bfloat16), "section", 0).astype(source_upper.dtype),
        swapped(decoded_lower.astype(jnp.bfloat16), "section", 0).astype(decoded_lower.dtype),
    )
    grad_source = jnp.where(section == 0, state["source"][:half], other_source)
    decoded = jnp.where(section == 0, other_decoded, state["decoded"][half:])
    return (
        decoded[:, 0],
        grad_source,
        decoded[:, 1],
        summed[0],
        summed[1],
        summed[2],
        summed[3],
        summed[4],
        summed[5],
        summed[6],
        summed[7],
        summed[8],
        summed[9],
        summed[10],
    )


BF16 = jnp.bfloat16
F32 = jnp.float32


def dot_nn(left, right):
    return lax.dot_general(left, right, (((1,), (0,)), ((), ())), preferred_element_type=F32)


def dot_nt(left, right):
    return lax.dot_general(left, right, (((1,), (1,)), ((), ())), preferred_element_type=F32)


def dot_tn(left, right):
    return lax.dot_general(left, right, (((0,), (0,)), ((), ())), preferred_element_type=F32)


def rows_sum(value):
    return jnp.sum(value.astype(F32), axis=0, keepdims=True)


def norm_parts(value):
    center = value - jnp.mean(value, axis=-1, keepdims=True)
    scale = lax.rsqrt(jnp.mean(center * center, axis=-1, keepdims=True) + EPSILON)
    return center * scale, scale


def norm_back(grad, unit, scale, gain):
    scaled = grad * gain
    inner = jnp.mean(scaled * unit, axis=-1, keepdims=True)
    back = scale * (scaled - jnp.mean(scaled, axis=-1, keepdims=True) - unit * inner)
    return back, rows_sum(grad * unit), rows_sum(grad)


def gelu_parts(value):
    root = math.sqrt(2.0 / math.pi)
    square = value * value
    bend = jnp.tanh(root * value * (1.0 + 0.044715 * square))
    half = 0.5 * (1.0 + bend)
    slope = half + 0.5 * value * (1.0 - bend * bend) * (root * (1.0 + 3.0 * 0.044715 * square))
    return value * half, slope


def head_mask(width, index):
    lane = lax.broadcasted_iota(jnp.int32, (1, width), 1)
    size = width // HEADS
    inside = jnp.logical_and(lane >= index * size, lane < (index + 1) * size)
    return jnp.where(inside, 1.0, 0.0).astype(BF16)


def attend_heads(pairs, values, bias):
    width = values.shape[1]
    count = pairs[0][0].shape[0]
    column = lax.broadcasted_iota(jnp.int32, (count, 128), 1)
    mixed = jnp.zeros((count, width), F32)
    logs = jnp.zeros((count, 128), F32)
    for head in range(HEADS):
        mask = head_mask(width, head)
        scores = bias
        for queries, keys in pairs:
            scores = scores + dot_nt(queries * mask, keys)
        highest = jnp.max(scores, axis=-1, keepdims=True)
        weights = jnp.exp(scores - highest)
        total = jnp.sum(weights, axis=-1, keepdims=True)
        probs = (weights * (1.0 / total)).astype(BF16)
        mixed = mixed + dot_nn(probs, values * mask)
        logs = jnp.where(column == head, highest + jnp.log(total), logs)
    return mixed, logs


def attend_heads_back(pairs, values, bias, logs, grad_mixed, key_refs, value_ref):
    width = values.shape[1]
    size = width // HEADS
    turned_grad = grad_mixed.T
    turned_queries = [queries.T for queries, _ in pairs]
    grads = [jnp.zeros(queries.shape, F32) for queries, _ in pairs]
    for head in range(HEADS):
        mask = head_mask(width, head)
        log = logs[:, head : head + 1]
        scores = bias
        for queries, keys in pairs:
            scores = scores + dot_nt(queries * mask, keys)
        probs = jnp.exp(scores - log)
        grad_probs = dot_nt(grad_mixed * mask, values)
        inner = jnp.sum(probs * grad_probs, axis=-1, keepdims=True)
        grad_scores = (probs * (grad_probs - inner)).astype(BF16)
        part = slice(head * size, (head + 1) * size)
        value_ref[part, :] = dot_nn(turned_grad[part, :], probs.astype(BF16))
        for index, (queries, keys) in enumerate(pairs):
            key_refs[index][part, :] = dot_nn(turned_queries[index][part, :], grad_scores)
            grads[index] = grads[index] + dot_nn(grad_scores, keys * mask)
    return grads


def place_in_pair():
    return lax.axis_index("section"), lax.axis_index("seq")


def rows_at(half, count):
    return pl.ds(pl.multiple_of(half * count, count), count)


def token_bias(lengths, image, rows):
    seq = lax.axis_index("seq")
    lane = lax.broadcasted_iota(jnp.int32, (1, rows), 1)
    length = lengths[image]
    parts = [jnp.where((seq ^ bit) * rows + lane < length, 0.0, NEGATIVE) for bit in range(4)]
    return jnp.concatenate(parts, axis=1)


def query_bias(queries, padded):
    lane = lax.broadcasted_iota(jnp.int32, (1, padded), 1)
    return jnp.where(lane < queries, 0.0, NEGATIVE)


def put_halves(scratch, own, other):
    half = place_in_pair()[0]
    size = scratch.shape[0] // 2
    scratch[rows_at(half, size)] = own
    scratch[rows_at(1 - half, size)] = other
    return scratch[...]


def fetch(source, target, semaphore):
    copy = pltpu.make_async_copy(source, target, semaphore)
    copy.start()
    return copy


ENTERED, TARGET, KEY, VALUE, MINE, QUERY, MIXED = ((0, 2), (2, 4), (4, 6), (6, 8), (8, 9), (9, 10), (10, 11))
SUM, FIRST, LOGS = ((0, 1), (1, 2), (2, 3))


def kept_part(ref, part, own):
    return ref.at[part[0] * own : part[1] * own, :]


def pack_kernel(source, position, mine_o, near_o, far_o, farthest_o):
    width = source.shape[2]
    rows = near_o.shape[0]
    half, image = place_in_pair()
    part = rows_at(half, rows)
    for array, columns in ((source, slice(0, width)), (position, slice(width, 2 * width))):
        mine_o[:, columns] = array[image]
        for bit, out in ((1, near_o), (2, far_o), (3, farthest_o)):
            out[:, columns] = array[image ^ bit, part, :]


def stack_kernel(*refs):
    size = refs[0].shape[0]
    for index, ref in enumerate(refs[:-1]):
        refs[-1][index * size : (index + 1) * size, :] = ref[...]


def self_forward_kernel(
    scale, own, target, embed, attn, attn_bias, attn_out, gain, shift,
    low_o, full_o,
    arrived_s, target_s, embed_s, semaphore,
):
    width = embed.shape[1]
    padded = 2 * own
    queries = embed.shape[0]
    half, image = place_in_pair()
    copy = fetch(target.at[image], arrived_s, semaphore)
    embed_s[:queries] = embed[...]
    for scratch in (embed_s, target_s):
        scratch[queries:] = jnp.zeros((padded - queries, width), F32)
    copy.wait()
    target_s[:queries] = arrived_s[...]
    mine = rows_at(half, own)
    whole = target_s[...]
    own_target = target_s[mine]
    entered = (whole + embed_s[...]).astype(BF16)
    low = whole.astype(BF16)
    own_entered = (own_target + embed_s[mine]).astype(BF16)
    query = ((dot_nn(own_entered, attn[0]) + attn_bias[3:4]) * scale).astype(BF16)
    key = dot_nn(entered, attn[1]).astype(BF16)
    value = (dot_nn(low, attn[2]) + attn_bias[4:5]).astype(BF16)
    mixed, logs = attend_heads([(query, key)], value, query_bias(queries, padded))
    mixed = mixed.astype(BF16)
    first_sum = own_target + dot_nn(mixed, attn_out[...]) + attn_bias[5:6]
    unit, _ = norm_parts(first_sum)
    parts = ((ENTERED, entered), (TARGET, low), (KEY, key), (VALUE, value), (MINE, own_entered), (QUERY, query), (MIXED, mixed))
    for part, values in parts:
        kept_part(low_o, part, own)[...] = values
    kept_part(full_o, SUM, own)[...] = first_sum
    kept_part(full_o, FIRST, own)[...] = unit * gain[2:3] + shift[2:3]
    full_o[LOGS[0] * own :, :128] = logs
    full_o[LOGS[0] * own :, 128:] = jnp.zeros((own, width - 128), F32)


def cross_query_kernel(
    cross_scale, own, points, full_d, tokens, period, cross, attn_bias,
    sine_o, content_o, place_o, place_key_o,
    points_s, spots_s,
):
    width = full_d.shape[1]
    first = kept_part(full_d, FIRST, own)
    half, image = place_in_pair()
    points_s[...] = jnp.zeros(points_s.shape, F32)
    points_s[: points.shape[1], : points.shape[2]] = points[image]
    spots_s[...] = points_s[...].T
    place_key_o[...] = dot_nn(tokens[:, width:], cross[3]).astype(BF16)
    content_o[...] = ((dot_nn(first[...].astype(BF16), cross[0]) + attn_bias[6:7]) * cross_scale).astype(BF16)
    spots = spots_s[rows_at(half, own)]
    lane = lax.broadcasted_iota(jnp.int32, (1, width), 1)
    angle = jnp.where(lane < width // 2, spots[:, 1:2], spots[:, 0:1]) * (2.0 * math.pi) / period[...]
    sine = jnp.where(lane % 2 == 0, jnp.sin(angle), jnp.cos(angle)).astype(BF16)
    sine_o[...] = sine
    place_o[...] = (dot_nn(sine, cross[1]) * cross_scale).astype(BF16)


def encoder_forward_kernel(
    scale, lengths, chunk, arrived, others, attn, attn_bias, attn_out, ffn_in, ffn_in_bias, ffn_out, ffn_out_bias, gain, shift,
    query_o, key_o, value_o, mixed_o, logs_o, sum_o, second_o, memory_o, tokens_o,
):
    own, width = query_o.shape
    rows = chunk.shape[0]
    half = place_in_pair()[0]
    tokens_o[:rows, :] = chunk[...]
    part = rows // 2
    for index in range(3):
        source_rows = slice(index * part, (index + 1) * part)
        for place, ref in ((half, arrived), (1 - half, others)):
            tokens_o[pl.ds(pl.multiple_of((index + 1) * rows + place * part, part), part), :] = ref[source_rows, :]
    tokens = tokens_o[...]
    mine = tokens_o[rows_at(half, own)].astype(F32)
    own_source = mine[:, :width]
    own_entered = (own_source + mine[:, width:]).astype(BF16)
    source = tokens[:, :width]
    position = tokens[:, width:]
    bias = token_bias(lengths, place_in_pair()[1], rows)
    entered = (source.astype(F32) + position.astype(F32)).astype(BF16)
    query = ((dot_nn(own_entered, attn[0]) + attn_bias[0:1]) * scale).astype(BF16)
    key = dot_nn(entered, attn[1]).astype(BF16)
    value = (dot_nn(source, attn[2]) + attn_bias[1:2]).astype(BF16)
    mixed, logs = attend_heads([(query, key)], value, bias)
    mixed = mixed.astype(BF16)
    first_sum = own_source + dot_nn(mixed, attn_out[...]) + attn_bias[2:3]
    unit, _ = norm_parts(first_sum)
    first = unit * gain[0:1] + shift[0:1]
    first_low = first.astype(BF16)
    second_sum = first + ffn_out_bias[0:1]
    inner_width = ffn_in.shape[1]
    for start in range(0, inner_width, width):
        part = slice(start, start + width)
        active, _ = gelu_parts(dot_nn(first_low, ffn_in[:, part]) + ffn_in_bias[0:1, part])
        second_sum = second_sum + dot_nn(active.astype(BF16), ffn_out[part, :])
    unit, _ = norm_parts(second_sum)
    query_o[...] = query
    key_o[...] = key
    value_o[...] = value
    mixed_o[...] = mixed
    logs_o[...] = logs
    sum_o[...] = first_sum
    second_o[...] = second_sum
    memory_o[...] = (unit * gain[1:2] + shift[1:2]).astype(BF16)


def cross_forward_kernel(
    lengths, memory_own, memory_other, place_key, full_d, content, place, grad_output,
    cross, attn_bias, attn_out, ffn_in, ffn_in_bias, ffn_out, ffn_out_bias, gain, shift,
    output_o, key_o, value_o, logs_o, grad_o, grad_mixed_o, keep_o, send_o, out_o, small_o,
    active_s, slope_s, piece_s, grad_s, arrived_s, memory_s, semaphore,
):
    own, width = content.shape
    first = kept_part(full_d, FIRST, own)
    queries = arrived_s.shape[0]
    half, image = place_in_pair()
    copy = fetch(grad_output.at[image], arrived_s, semaphore)
    bias = token_bias(lengths, image, memory_own.shape[0] // 2)
    memory = put_halves(memory_s, memory_own[...], memory_other[...])
    key = dot_nn(memory, cross[2]).astype(BF16)
    value = (dot_nn(memory, cross[4]) + attn_bias[7:8]).astype(BF16)
    mixed, logs = attend_heads([(content[...], key), (place[...], place_key[...])], value, bias)
    mixed = mixed.astype(BF16)
    key_o[...] = key
    value_o[...] = value
    logs_o[...] = logs
    second_sum = first[...] + dot_nn(mixed, attn_out[...]) + attn_bias[8:9]
    second_unit, second_scale = norm_parts(second_sum)
    second = second_unit * gain[3:4] + shift[3:4]
    second_low = second.astype(BF16)
    third_sum = second + ffn_out_bias[1:2]
    inner_width = ffn_in.shape[1]
    for start in range(0, inner_width, width):
        part = slice(start, start + width)
        active, slope = gelu_parts(dot_nn(second_low, ffn_in[:, part]) + ffn_in_bias[1:2, part])
        active = active.astype(BF16)
        active_s[:, part] = active
        slope_s[:, part] = slope
        third_sum = third_sum + dot_nn(active, ffn_out[part, :])
    unit, scale = norm_parts(third_sum)
    output_o[...] = (unit * gain[4:5] + shift[4:5]).astype(output_o.dtype)
    copy.wait()
    grad_s[:queries] = arrived_s[...]
    grad_s[queries:] = jnp.zeros((grad_s.shape[0] - queries, width), F32)
    grad_third, gain_five, shift_five = norm_back(grad_s[rows_at(half, own)], unit, scale, gain[4:5])
    branch = grad_third.astype(BF16)
    grad_second = grad_third
    for index, start in enumerate(range(0, inner_width, width)):
        part = slice(start, start + width)
        grad_inner = (dot_nt(branch, ffn_out[part, :]) * slope_s[:, part]).astype(BF16)
        grad_second = grad_second + dot_nt(grad_inner, ffn_in[:, part])
        piece_s[part, :] = dot_tn(second_low, grad_inner).astype(BF16)
        piece_s[inner_width + start : inner_width + start + width, :] = dot_tn(active_s[:, part], branch).astype(BF16)
        small_o[index : index + 1, :] = rows_sum(grad_inner)
    spread(piece_s, keep_o, send_o)
    grad_second_sum, gain_four, shift_four = norm_back(grad_second, second_unit, second_scale, gain[3:4])
    cross_out = grad_second_sum.astype(BF16)
    grad_o[...] = grad_second_sum
    grad_mixed_o[...] = dot_nt(cross_out, attn_out[...]).astype(BF16)
    out_o[...] = dot_tn(mixed, cross_out).astype(BF16)
    base = inner_width // width
    rest = [rows_sum(branch), gain_four, gain_five, shift_four, shift_five, rows_sum(cross_out)]
    for index, row in enumerate(rest):
        small_o[base + index : base + index + 1, :] = row
    small_o[base + len(rest) :, :] = jnp.zeros((small_o.shape[0] - base - len(rest), width), F32)


def cross_back_kernel(
    lengths, key, value, place_key, content, place, logs, grad_mixed, cross,
    memory_own_o, memory_other_o, grad_key_o, grad_place_key_o, grad_value_o, grad_content_o, grad_place_o,
    key_s, place_s, value_s, grad_s,
):
    own = memory_own_o.shape[0]
    bias = token_bias(lengths, place_in_pair()[1], own // 2)
    grad_content, grad_place = attend_heads_back(
        [(content[...], key[...]), (place[...], place_key[...])],
        value[...], bias, logs[...], grad_mixed[...], [key_s, place_s], value_s,
    )
    grad_key = key_s[...].T.astype(BF16)
    grad_value = value_s[...].T.astype(BF16)
    grad_memory = dot_nt(grad_key, cross[2]) + dot_nt(grad_value, cross[4])
    grad_s[...] = grad_memory
    half = place_in_pair()[0]
    memory_own_o[...] = grad_s[rows_at(half, own)]
    memory_other_o[...] = grad_s[rows_at(1 - half, own)].astype(BF16)
    grad_key_o[...] = grad_key
    grad_value_o[...] = grad_value
    grad_place_key_o[...] = place_s[...].T.astype(BF16)
    grad_content_o[...] = grad_content.astype(BF16)
    grad_place_o[...] = grad_place.astype(BF16)


def self_back_kernel(
    scale, cross_scale, queries,
    low_d, full_d, sine, grad_second_sum,
    memory_own, memory_other, tokens, grad_key, grad_place_key, grad_value, grad_content, grad_place, cross_out, small_c,
    attn, attn_out, cross, gain, shift,
    target_own_o, target_other_o, grads_o,
    key_s, value_s, rows_s, memory_s,
):
    own, width = sine.shape
    padded = 2 * own
    low = lambda part: kept_part(low_d, part, own)[...]
    logs = full_d[LOGS[0] * own :, :128]
    half = place_in_pair()[0]
    mine, other = rows_at(half, own), rows_at(1 - half, own)
    unit, norm_scale = norm_parts(kept_part(full_d, SUM, own)[...])
    first_low = (unit * gain[2:3] + shift[2:3]).astype(BF16)
    grad_first = grad_second_sum[...] + cross_scale * dot_nt(grad_content[...], cross[...])
    grad_first_sum, gain_three, shift_three = norm_back(grad_first, unit, norm_scale, gain[2:3])
    branch = grad_first_sum.astype(BF16)
    grad_mixed = dot_nt(branch, attn_out[...]).astype(BF16)
    (grad_query,) = attend_heads_back(
        [(low(QUERY), low(KEY))], low(VALUE), query_bias(queries, padded), logs, grad_mixed, [key_s], value_s
    )
    grad_query = grad_query.astype(BF16)
    self_key = key_s[...].T.astype(BF16)
    self_value = value_s[...].T.astype(BF16)
    from_query = scale * dot_nt(grad_query, attn[0])
    from_key = dot_nt(self_key, attn[1])
    from_value = dot_nt(self_value, attn[2])
    rows_s[...] = from_key + from_value
    target_own_o[...] = rows_s[mine] + grad_first_sum + from_query
    target_other_o[...] = rows_s[other].astype(BF16)
    rows_s[...] = from_key
    rows_s[mine] += from_query
    position = tokens[:, width:]
    memory = put_halves(memory_s, memory_own[...], memory_other[...])
    small = [
        scale * rows_sum(grad_query),
        rows_sum(self_value),
        rows_sum(branch),
        cross_scale * rows_sum(grad_content[...]),
        rows_sum(grad_value[...]),
        gain_three,
        shift_three,
        jnp.zeros((9, width), F32),
    ]
    grads = [
        scale * dot_tn(low(MINE), grad_query),
        dot_tn(low(ENTERED), self_key),
        dot_tn(low(TARGET), self_value),
        dot_tn(low(MIXED), branch),
        cross_scale * dot_tn(first_low, grad_content[...]),
        cross_scale * dot_tn(sine[...], grad_place[...]),
        dot_tn(memory, grad_key[...]),
        dot_tn(position, grad_place_key[...]),
        dot_tn(memory, grad_value[...]),
        cross_out[...],
        rows_s[...],
        small_c[...],
        jnp.concatenate(small, axis=0),
    ]
    fill(grads_o, grads)


def encoder_ffn_back_kernel(
    grad_own, grad_other, first_sum, second_sum, mixed, attn_out, ffn_in, ffn_in_bias, ffn_out, gain, shift,
    grad_o, grad_mixed_o, keep_o, send_o, out_o, small_o,
    piece_s,
):
    width = first_sum.shape[1]
    inner_width = ffn_in.shape[1]
    grad_memory = (grad_own[...] + grad_other[...].astype(F32)).astype(BF16).astype(F32)
    second_unit, second_scale = norm_parts(second_sum[...])
    grad_second, gain_two, shift_two = norm_back(grad_memory, second_unit, second_scale, gain[1:2])
    branch = grad_second.astype(BF16)
    unit, scale = norm_parts(first_sum[...])
    first_low = (unit * gain[0:1] + shift[0:1]).astype(BF16)
    grad_first = grad_second
    for index, start in enumerate(range(0, inner_width, width)):
        part = slice(start, start + width)
        active, slope = gelu_parts(dot_nn(first_low, ffn_in[:, part]) + ffn_in_bias[0:1, part])
        grad_inner = (dot_nt(branch, ffn_out[part, :]) * slope).astype(BF16)
        grad_first = grad_first + dot_nt(grad_inner, ffn_in[:, part])
        piece_s[part, :] = dot_tn(first_low, grad_inner).astype(BF16)
        piece_s[inner_width + start : inner_width + start + width, :] = dot_tn(active.astype(BF16), branch).astype(BF16)
        small_o[index : index + 1, :] = rows_sum(grad_inner)
    spread(piece_s, keep_o, send_o)
    grad_first_sum, gain_one, shift_one = norm_back(grad_first, unit, scale, gain[0:1])
    attention = grad_first_sum.astype(BF16)
    out_o[...] = dot_tn(mixed[...], attention).astype(BF16)
    grad_o[...] = grad_first_sum
    grad_mixed_o[...] = dot_nt(attention, attn_out[...]).astype(BF16)
    base = inner_width // width
    rest = [rows_sum(branch), gain_one, gain_two, shift_one, shift_two, rows_sum(attention)]
    for index, row in enumerate(rest):
        small_o[base + index : base + index + 1, :] = row
    small_o[base + len(rest) :, :] = jnp.zeros((small_o.shape[0] - base - len(rest), width), F32)


def encoder_attention_back_kernel(
    scale, lengths, tokens, query, key, value, logs, grad_first_sum, grad_mixed, encoder_out, small_e, decoder_grads, attn,
    source_o, source_low_o, keep_o, send_o,
    key_s, value_s, piece_s, source_s, tokens_s,
):
    own, width = query.shape
    rows = tokens.shape[0] // 4
    bias = token_bias(lengths, place_in_pair()[1], rows)
    (grad_query,) = attend_heads_back(
        [(query[...], key[...])], value[...], bias, logs[...], grad_mixed[...], [key_s], value_s
    )
    grad_query = grad_query.astype(BF16)
    grad_key = key_s[...].T.astype(BF16)
    grad_value = value_s[...].T.astype(BF16)
    from_query = grad_first_sum[...] + scale * dot_nt(grad_query, attn[0])
    grad_source = dot_nt(grad_key, attn[1]) + dot_nt(grad_value, attn[2])
    mine = rows_at(place_in_pair()[0], own)
    source_s[...] = grad_source
    source_s[mine] += from_query
    source_o[...] = source_s[...]
    source_low_o[...] = source_s[...].astype(BF16)
    source = tokens[:, :width]
    entered = (source.astype(F32) + tokens[:, width:].astype(F32)).astype(BF16)
    tokens_s[...] = entered
    grads = [
        scale * dot_tn(tokens_s[mine], grad_query),
        dot_tn(entered, grad_key),
        dot_tn(source, grad_value),
        encoder_out[...],
        small_e[...],
        jnp.concatenate([scale * rows_sum(grad_query), rows_sum(grad_value), jnp.zeros((14, width), F32)], axis=0),
        decoder_grads[...],
    ]
    fill(piece_s, grads)
    spread(piece_s, keep_o, send_o)


PARTS = 16


def place_code(core):
    spot = lax.axis_index("dp")
    low, high = spot % 2, spot // 2
    swap = core == 1
    first, second = jnp.where(swap, high, low), jnp.where(swap, low, high)
    return first * 4 + second * 2 + lax.axis_index("seq") % 2


def fill(piece, grads):
    start = 0
    for grad in grads:
        piece[start : start + grad.shape[0], :] = grad.astype(BF16)
        start += grad.shape[0]
    if start < piece.shape[0]:
        piece[start:, :] = jnp.zeros((piece.shape[0] - start, piece.shape[1]), BF16)


def spread(piece, keep_o, send_o):
    half = PARTS // 2
    count = piece.shape[0] // PARTS
    me = lax.axis_index("section")
    for core, out in ((me, keep_o), (1 - me, send_o)):
        code = place_code(core)
        for slot in range(half):
            out[slot * count : (slot + 1) * count, :] = piece[rows_at(core * half + (slot ^ code), count), :]


def added(first, second):
    return (first.astype(F32) + second.astype(F32)).astype(BF16)


def add_whole_kernel(own, arrived, out):
    out[...] = added(own[...], arrived[...])


def add_split_kernel(own, arrived, keep_o, send_o):
    size = keep_o.shape[0]
    keep_o[...] = added(own[:size, :], arrived[:size, :])
    send_o[...] = added(own[size:, :], arrived[size:, :])


def join_kernel(near, far, out):
    size = near.shape[0]
    out[:size, :] = near[...]
    out[size:, :] = far[...]


def crossed(block, axis, bit):
    return lax.ppermute(block, axis, [(index, index ^ bit) for index in range(lax.axis_size(axis))])


def crossed_plane(block, step):
    pairs = []
    for spot in range(lax.axis_size("dp")):
        for core in range(2):
            pairs.append((spot * 2 + core, (spot ^ (1 if core == step else 2)) * 2 + core))
    return lax.ppermute(block, ("dp", "section"), pairs)


def reduce_steps(keep, send):
    size, width = keep.shape
    low = lambda rows: ((rows, width), BF16)
    moves = [
        lambda block: crossed(block, "section", 1),
        lambda block: crossed_plane(block, 0),
        lambda block: crossed_plane(block, 1),
        lambda block: crossed(block, "seq", 1),
        lambda block: crossed(block, "seq", 2),
    ]
    for move in moves[:3]:
        after, micros = yield keep
        size //= 2
        keep, send = run(add_split_kernel, [low(size)] * 2, [keep, move(send)], after=after, micros=micros)
    after, micros = yield keep
    (total,) = run(add_whole_kernel, [low(size)], [keep, moves[3](send)], after=after, micros=micros)
    after, micros = yield total
    (total,) = run(add_whole_kernel, [low(size)], [total, moves[4](total)], after=after, micros=micros)
    for move in reversed(moves[1:4]):
        after, micros = yield total
        size *= 2
        (total,) = run(join_kernel, [low(size)], [total, move(total)], after=after, micros=micros)
    yield total, moves[0](total)


class Piece:
    def __init__(self, keep, send):
        self.steps = reduce_steps(keep, send)
        next(self.steps)

    def step(self, *after, micros=0.1):
        return self.steps.send((after, micros))

    def finish(self, *after, micros=0.1):
        result = self.step(*after, micros=micros)
        while not isinstance(result, tuple):
            result = self.step(micros=micros)
        return result


def part_rows(near, far, start, rows, write):
    half = PARTS // 2
    count = near.shape[0] // half
    me = lax.axis_index("section")
    for part in range(start // count, -(-(start + rows) // count)):
        core = part // half
        slot = (part % half) ^ place_code(core)
        for ref, here in ((near, me == core), (far, me != core)):

            @pl.when(here)
            def _():
                write(part * count - start, ref[rows_at(slot, count), :].astype(F32))


def ffn_result_kernel(*refs):
    near, far = refs[:2]
    in_o, out_o = refs[-2:]
    inner_width, width = out_o.shape

    def write_in(offset, values):
        for start in range(0, values.shape[0], width):
            block = (offset + start) // width
            row = (offset + start) % width
            part = values[start : start + width]
            in_o[row : row + part.shape[0], block * width : (block + 1) * width] = part

    def write_out(offset, values):
        out_o[offset : offset + values.shape[0], :] = values

    part_rows(near, far, 0, inner_width, write_in)
    part_rows(near, far, inner_width, inner_width, write_out)


def rest_result_kernel(
    padded, near, far, attn_o, out_o, attn_bias_o, cross_o, ffn_in_bias_o, ffn_out_bias_o, gain_o, shift_o, embed_o, piece_s
):
    width = gain_o.shape[1]

    def write(offset, values):
        piece_s[offset : offset + values.shape[0], :] = values

    part_rows(near, far, 0, piece_s.shape[0], write)
    encoder = 4 * width
    decoder = encoder + 32
    late = decoder + 10 * width + padded
    block = lambda start, index: piece_s[start + index * width : start + (index + 1) * width, :]
    for index in range(3):
        attn_o[0, index] = block(0, index)
        attn_o[1, index] = block(decoder, index)
    out_o[0] = block(0, 3)
    out_o[1] = block(decoder, 3)
    out_o[2] = block(decoder, 9)
    for index in range(5):
        cross_o[index] = block(decoder, 4 + index)
    embed_o[...] = piece_s[decoder + 10 * width : decoder + 10 * width + embed_o.shape[0], :]
    row = lambda start: piece_s[start : start + 1, :]
    blocks = ffn_in_bias_o.shape[1] // width
    row_e = lambda index: row(encoder + index)
    row_a = lambda index: row(encoder + 16 + index)
    row_c = lambda index: row(late + index)
    row_d = lambda index: row(late + 16 + index)
    bias = [
        row_a(0), row_a(1), row_e(blocks + 5),
        row_d(0), row_d(1), row_d(2),
        row_d(3), row_d(4), row_c(blocks + 5),
    ]
    for index, values in enumerate(bias):
        attn_bias_o[index // 3, index % 3 : index % 3 + 1, :] = values
    for index in range(blocks):
        part = slice(index * width, (index + 1) * width)
        ffn_in_bias_o[0:1, part] = row_e(index)
        ffn_in_bias_o[1:2, part] = row_c(index)
    ffn_out_bias_o[0:1, :] = row_e(blocks)
    ffn_out_bias_o[1:2, :] = row_c(blocks)
    for index, out in ((1, gain_o), (3, shift_o)):
        rows = [row_e(blocks + index), row_e(blocks + index + 1), row_d(5 + index // 2)]
        rows += [row_c(blocks + index), row_c(blocks + index + 1)]
        for place, values in enumerate(rows):
            out[place : place + 1, :] = values


def is_home():
    return lax.axis_index("seq") // 2 == lax.axis_index("section")


def sent_far(block):
    pairs = []
    for core in range(2):
        for spot in range(4):
            if spot // 2 == core:
                pairs.append((core * 4 + spot, core * 4 + (spot ^ 2)))
    return lax.ppermute(block, ("section", "seq"), pairs)


def queries_pack_kernel(output, target_own, target_arrived, out):
    own = output.shape[0]
    out[:own, :] = output[...]
    out[own:, :] = (target_own[...] + target_arrived[...].astype(F32)).astype(BF16)


def chosen_kernel(home, arrived, out):
    @pl.when(is_home())
    def _():
        out[...] = home[...]

    @pl.when(jnp.logical_not(is_home()))
    def _():
        out[...] = arrived[...]


def queries_result_kernel(mine, near, output_o, target_o, rows_s):
    own = mine.shape[0] // 4
    core = lax.axis_index("section")
    spot = lax.axis_index("seq") % 2
    for index, out in enumerate((output_o, target_o)):
        for image, ref in ((spot, mine), (1 - spot, near)):
            for half in range(2):
                start = (2 * half + index) * own
                place = core if half == 0 else 1 - core
                rows_s[image, rows_at(place, own), :] = ref[start : start + own, :].astype(F32)
        out[...] = rows_s[:, : out.shape[1], :]


def source_sum_kernel(own, arrived, keep_o, send_o):
    size = keep_o.shape[0]
    total = own[...] + arrived[...].astype(F32)
    keep_o[...] = total[:size]
    send_o[...] = total[size:].astype(BF16)


def source_pair_kernel(home, arrived, keep_o, send_o):
    rows = keep_o.shape[0]

    @pl.when(is_home())
    def _():
        keep_o[...] = home[:rows, :]
        send_o[...] = home[rows:, :].astype(BF16)

    @pl.when(jnp.logical_not(is_home()))
    def _():
        keep_o[...] = arrived[:rows, :].astype(F32)
        send_o[...] = arrived[rows:, :]


def source_result_kernel(mine, near, out_o):
    spot = lax.axis_index("seq") % 2
    out_o[spot] = mine[...]
    out_o[1 - spot] = near[...].astype(F32)


def whole_spec(shape):
    return pl.BlockSpec(shape, lambda step: (0,) * len(shape))


def part_spec(shape, index):
    return pl.BlockSpec((None,) + shape[1:], lambda step: (index,) + (0,) * (len(shape) - 1))


def run(kernel, outs, operands, scratch=(), micros=1.0, limit=16, after=(), hold=()):
    arrays, specs, places = [], [], []
    for operand in operands:
        array, extra = operand if isinstance(operand, tuple) else (operand, None)
        spec = extra if isinstance(extra, pl.BlockSpec) else pl.BlockSpec(memory_space=pltpu.VMEM)
        arrays.append(array)
        specs.append(spec)
        places.append(extra if isinstance(extra, int) else None)

    def body(*refs):
        parts = [ref if place is None else ref.at[place] for ref, place in zip(refs, places)]
        kernel(*parts, *refs[len(places) + len(after) + len(hold) :])

    return pl.pallas_call(
        body,
        name=getattr(kernel, "func", kernel).__name__,
        out_shape=[jax.ShapeDtypeStruct(shape, dtype) for shape, dtype in outs],
        in_specs=specs + [pl.BlockSpec(memory_space=pl.ANY)] * len(after) + [pl.BlockSpec(memory_space=pltpu.VMEM)] * len(hold),
        out_specs=[pl.BlockSpec(memory_space=pltpu.VMEM) for _ in outs],
        scratch_shapes=[pltpu.VMEM(*item) if isinstance(item, tuple) else item for item in scratch],
        compiler_params=pltpu.CompilerParams(vmem_limit_bytes=limit * 1024 * 1024),
        cost_estimate=pl.CostEstimate(flops=int(micros * 1.15e9), bytes_accessed=1024, transcendentals=0),
    )(*arrays, *after, *hold)


def run_parts(kernel, outs, operands, scratch=(), aliases=None, micros=2.0, after=()):
    arrays, specs = [], []
    for operand in operands:
        array, spec = operand if isinstance(operand, tuple) else (operand, whole_spec(operand.shape))
        arrays.append(array)
        specs.append(spec)
    count = len(specs) + len(after)

    def body(*refs):
        kernel(*refs[: len(specs)], *refs[count : count + len(outs)], *refs[count + len(outs) + 1 :])
        refs[count + len(outs)][...] = jnp.zeros((8, 128), F32)

    return pl.pallas_call(
        body,
        name=getattr(kernel, "func", kernel).__name__,
        grid=(1,),
        out_shape=[jax.ShapeDtypeStruct(out[0], out[1]) for out in outs] + [jax.ShapeDtypeStruct((8, 128), F32)],
        in_specs=specs + [pl.BlockSpec(memory_space=pl.ANY)] * len(after),
        out_specs=[out[2] if len(out) > 2 else whole_spec(out[0]) for out in outs] + [whole_spec((8, 128))],
        scratch_shapes=[pltpu.VMEM(shape, dtype) for shape, dtype in scratch],
        input_output_aliases=aliases or {},
        compiler_params=pltpu.CompilerParams(vmem_limit_bytes=24 * 1024 * 1024),
        cost_estimate=pl.CostEstimate(flops=int(micros * 1.15e9), bytes_accessed=1024, transcendentals=0),
    )(*arrays, *after)


def traded(block, bit):
    return crossed(block, "seq", bit)


def with_pair(block):
    return crossed(block, "section", 1)


BEFORE = "d"
AFTER = "edqwpewrdehwdeswtdewedweewDuEw"


def paired_device(
    source, position, lengths, target, points, grad_output,
    attn, attn_out, attn_bias, cross, ffn_in, ffn_in_bias, ffn_out, ffn_out_bias, norm_gain, norm_bias, query_embed,
):
    batches, rows, width = source.shape
    queries = target.shape[1]
    inner_width = ffn_in.shape[2]
    images = batches // lax.axis_size("section")
    tokens = rows * lax.axis_size("seq")
    half_tokens = tokens // 2
    half_queries = -(-queries // 32) * 16
    padded = 2 * half_queries
    head = width // HEADS
    scale = head ** (-0.5)
    cross_scale = (2 * head) ** (-0.5)
    wide = lambda count: ((count, 2 * width), BF16)
    chunk, *parts = run(pack_kernel, [wide(rows)] + [wide(rows // 2)] * 3, [source, position])
    parts = [traded(part, bit + 1) for bit, part in enumerate(parts)]

    column = np.arange(width) % (width // 2)
    period = (10000.0 ** ((2 * (column // 2)).astype(np.float32) / np.float32(width // 2))).astype(np.float32)[None]
    bias_rows = attn_bias.reshape(9, width)
    lengths = (lengths, pl.BlockSpec(memory_space=pltpu.SMEM))
    low = lambda count, columns=width: ((count, columns), BF16)
    full = lambda count, columns=width: ((count, columns), F32)
    part = lambda array, index: (array, index)

    elsewhere = lambda array: (array, pl.BlockSpec(memory_space=pl.ANY))
    copied = pltpu.SemaphoreType.DMA
    lanes = -(-padded // 128) * 128

    low_d, full_d = run(
        functools.partial(self_forward_kernel, scale, half_queries),
        [low(11 * half_queries), full(3 * half_queries)],
        [elsewhere(target), query_embed, part(attn, 1), bias_rows, part(attn_out, 1), norm_gain, norm_bias],
        [full(queries), full(padded), full(padded), copied], micros=12.0, hold=[ffn_in, ffn_out],
    )

    (arrived,) = run(stack_kernel, [wide(3 * rows // 2)], parts, after=[low_d])
    query_e, key_e, value_e, mixed_e, logs_e, sum_e, second_e, memory, token_rows = run(
        functools.partial(encoder_forward_kernel, scale),
        [low(half_tokens), low(tokens), low(tokens), low(half_tokens), full(half_tokens, 128),
         full(half_tokens), full(half_tokens), low(half_tokens), wide(tokens)],
        [lengths, chunk, arrived, with_pair(arrived), part(attn, 0), bias_rows, part(attn_out, 0),
         part(ffn_in, 0), ffn_in_bias, part(ffn_out, 0), ffn_out_bias, norm_gain, norm_bias], micros=21.0, after=[low_d],
    )

    sine, content, place_query, place_key = run(
        functools.partial(cross_query_kernel, cross_scale, half_queries),
        [low(half_queries), low(half_queries), low(half_queries), low(tokens)],
        [points.transpose(0, 2, 1), full_d, token_rows, jnp.asarray(period), cross, bias_rows],
        [full(8, lanes), full(lanes, 8)], micros=6.0, after=[mixed_e],
    )
    memory_other = with_pair(memory)
    piece = lambda rows: [low(rows // 2)] * 2
    output_half, cross_key, cross_value, logs_c, grad_second_sum, grad_cross_mixed, keep_d, send_d, out_c, small_c = run(
        cross_forward_kernel,
        [low(half_queries), low(tokens), low(tokens), full(half_queries, 128), full(half_queries), low(half_queries),
         *piece(2 * inner_width), low(width), full(16)],
        [lengths, memory, memory_other, place_key, full_d, content, place_query, elsewhere(grad_output),
         cross, bias_rows, part(attn_out, 2), part(ffn_in, 1), ffn_in_bias, part(ffn_out, 1), ffn_out_bias, norm_gain, norm_bias],
        [low(half_queries, inner_width), full(half_queries, inner_width), low(2 * inner_width), full(padded), full(queries), low(tokens), copied],
        micros=30.0,
    )
    piece_d = Piece(keep_d, send_d)

    memory_grad_own, memory_grad_other, grad_key, grad_place_key, grad_value, grad_content, grad_place = run(
        cross_back_kernel,
        [full(half_tokens), low(half_tokens), low(tokens), low(tokens), low(tokens), low(half_queries), low(half_queries)],
        [lengths, cross_key, cross_value, place_key, content, place_query, logs_c, grad_cross_mixed, cross],
        [full(width, tokens)] * 3 + [full(tokens)],
        micros=21.0,
    )
    memory_grad_partner = with_pair(memory_grad_other)

    count_d = 10 * width + padded + 32
    target_own, target_other, grads_d = run(
        functools.partial(self_back_kernel, scale, cross_scale, queries),
        [full(half_queries), low(half_queries), low(count_d)],
        [low_d, full_d, sine, grad_second_sum, memory, memory_other, token_rows,
         grad_key, grad_place_key, grad_value, grad_content, grad_place, out_c, small_c,
         part(attn, 1), part(attn_out, 1), part(cross, 0), norm_gain, norm_bias],
        [full(width, padded), full(width, padded), full(padded), low(tokens)], micros=18.0, after=[piece_d.step()],
    )

    grad_first_sum, grad_mixed, keep_e, send_e, out_e, small_e = run(
        encoder_ffn_back_kernel,
        [full(half_tokens), low(half_tokens), *piece(2 * inner_width), low(width), full(16)],
        [memory_grad_own, memory_grad_partner, sum_e, second_e, mixed_e, part(attn_out, 0),
         part(ffn_in, 0), ffn_in_bias, part(ffn_out, 0), norm_gain, norm_bias],
        [low(2 * inner_width)], micros=21.0, after=[grads_d, piece_d.step()],
    )
    piece_e = Piece(keep_e, send_e)

    count_w = -(-(4 * width + 32 + count_d) // (16 * PARTS)) * 16 * PARTS
    source_full, source_low, keep_w, send_w = run(
        functools.partial(encoder_attention_back_kernel, scale),
        [full(tokens), low(tokens), *piece(count_w)],
        [lengths, token_rows, query_e, key_e, value_e, logs_e, grad_first_sum, grad_mixed, out_e, small_e, grads_d, part(attn, 0)],
        [full(width, tokens), full(width, tokens), low(count_w), full(tokens), low(tokens)],
        micros=21.0, after=[{"d": piece_d, "e": piece_e}[step].step() for step in BEFORE],
    )
    piece_w = Piece(keep_w, send_w)

    def kept(shape, index):
        return (shape, F32, part_spec(shape, index))

    pieces = dict(d=piece_d, e=piece_e, w=piece_w)
    sums = {}
    packed_halves = [output_half, target_own, with_pair(target_other)]
    mark = keep_w
    for step in AFTER:
        if step in pieces:
            result = pieces[step].step(mark, micros=6.0)
            if isinstance(result, tuple):
                sums[step] = result
                result = result[0]
            mark = result
        elif step == "q":
            (halves,) = run(queries_pack_kernel, [low(2 * half_queries)], packed_halves, after=[mark], micros=6.0)
            mark = halves
        elif step == "r":
            (halves,) = run(join_kernel, [low(4 * half_queries)], [halves, with_pair(halves)], after=[mark], micros=6.0)
            mark = halves
        elif step == "h":
            (halves,) = run(chosen_kernel, [low(4 * half_queries)], [halves, sent_far(halves)], after=[mark], micros=6.0)
            mark = halves
        elif step == "u":
            decoder_output, grad_target, mark = run_parts(
                queries_result_kernel, [((images, queries, width), F32)] * 2, [halves, traded(halves, 1)],
                [((images, padded, width), F32)], after=[mark],
            )
        elif step == "p":
            source_home, source_far = run(
                source_sum_kernel, [full(half_tokens), low(half_tokens)], [source_full, with_pair(source_low)], after=[mark], micros=6.0
            )
            mark = source_home
        elif step == "s":
            source_mine, source_near = run(
                source_pair_kernel, [full(rows), low(rows)], [source_home, sent_far(source_far)], after=[mark], micros=6.0
            )
            mark = source_mine
        elif step == "t":
            grad_source, mark = run_parts(
                source_result_kernel, [((images, rows, width), F32)], [source_mine, traded(source_near, 1)], after=[mark]
            )
        elif step == "D":
            *grad_ffn, mark = run_parts(
                ffn_result_kernel, [kept(ffn_in.shape, 1), kept(ffn_out.shape, 1)], sums["d"], after=[mark]
            )
        elif step == "E":
            before = [(array, pl.BlockSpec(memory_space=pl.ANY)) for array in grad_ffn]
            *grad_ffn, mark = run_parts(
                ffn_result_kernel, [kept(ffn_in.shape, 0), kept(ffn_out.shape, 0)], [*sums["e"], *before], aliases={2: 0, 3: 1}, after=[mark]
            )
    grad_ffn_in, grad_ffn_out = grad_ffn
    rest = (attn, attn_out, attn_bias, cross, ffn_in_bias, ffn_out_bias, norm_gain, norm_bias, query_embed)
    *grads, _ = run_parts(
        functools.partial(rest_result_kernel, padded), [(array.shape, F32) for array in rest],
        sums["w"], [full(count_w)]
    )
    grad_attn, grad_attn_out, grad_attn_bias, grad_cross, grad_ffn_in_bias, grad_ffn_out_bias, grad_gain, grad_shift, grad_embed = grads
    return (
        decoder_output, grad_source, grad_target, grad_attn, grad_attn_out, grad_attn_bias, grad_cross,
        grad_ffn_in, grad_ffn_in_bias, grad_ffn_out, grad_ffn_out_bias, grad_gain, grad_shift, grad_embed,
    )


def chosen_plan(*args):
    batches = args[0].shape[0]
    sections = lax.axis_size("section")
    paired = sections == 2 and batches == lax.axis_size("seq") == lax.axis_size("dp") == 4
    return (paired_device if paired else per_device)(*args)


def solution(mesh):
    placed = (
        P("dp", "seq", None),
        P("dp", "seq", None),
        P("dp"),
        P("dp", None, None),
        P("dp", None, None),
        P("dp", None, None),
        P(),
        P(),
        P(),
        P(),
        P(),
        P(),
        P(),
        P(),
        P(),
        P(),
        P(),
    )
    return jax.shard_map(
        chosen_plan,
        mesh=mesh,
        in_specs=placed,
        out_specs=(
            P(("dp", "section"), None, None),
            P(("dp", "section"), "seq", None),
            P(("dp", "section"), None, None),
            P(),
            P(),
            P(),
            P(),
            P(),
            P(),
            P(),
            P(),
            P(),
            P(),
            P(),
        ),
        check_vma=False,
    )
```

```python
import functools
import math
from types import SimpleNamespace

import jax
import jax.numpy as jnp
import numpy as np
from jax import lax
from jax.experimental import pallas as pl
from jax.experimental.pallas import tpu as pltpu
from jax.sharding import PartitionSpec as P

HEADS = 8


EPSILON = 1e-05
NEGATIVE = -1e30


def swapped(block, axis, bit):
    count = lax.axis_size(axis)
    route = []
    for low in range(count):
        high = low | 1 << bit
        if high != low and high < count:
            route += [(low, high), (high, low)]
    return lax.ppermute(block, axis, route)


def lower(value):
    return value.astype(jnp.bfloat16)


def product(left, right):
    return jnp.dot(left, right, preferred_element_type=jnp.float32)


def left_transposed(left, right):
    return lax.dot_general(
        left, right, (((0,), (0,)), ((), ())), preferred_element_type=jnp.float32
    )


def right_transposed(left, right):
    return lax.dot_general(
        left, right, (((1,), (1,)), ((), ())), preferred_element_type=jnp.float32
    )


def column_sum(value):
    return jnp.sum(value.astype(jnp.float32), axis=0)


def norm_apply(value, gain, shift):
    center = value - jnp.mean(value, axis=-1, keepdims=True)
    scale = lax.rsqrt(jnp.mean(center * center, axis=-1, keepdims=True) + EPSILON)
    return center * scale * gain + shift


def activate(value):
    return jax.nn.gelu(value)


def sine_embed(points, width):
    half_width = width // 2
    column = jnp.arange(half_width)
    period = 10000.0 ** ((2 * (column // 2)).astype(jnp.float32) / half_width)

    def embed(coordinate):
        angle = coordinate[..., None] * (2.0 * math.pi) / period
        return jnp.where(column % 2 == 0, jnp.sin(angle), jnp.cos(angle))

    return jnp.concatenate([embed(points[..., 1]), embed(points[..., 0])], axis=-1)


def split_heads(value, heads):
    return value.reshape(value.shape[0], heads, value.shape[1] // heads)


def join_heads(first, second, heads):
    joined = jnp.concatenate([split_heads(first, heads), split_heads(second, heads)], axis=2)
    return joined.reshape(first.shape[0], 2 * first.shape[1])


def part_heads(value, heads):
    count = value.shape[0]
    split = split_heads(value, heads)
    middle = split.shape[2] // 2
    return (split[:, :, :middle].reshape(count, -1), split[:, :, middle:].reshape(count, -1))


def column_block(value, start, count):
    return lax.dynamic_slice_in_dim(value, start, count, 2)


def score_heads(queries, keys, heads):
    return jnp.einsum(
        "qhd,khd->hqk",
        split_heads(queries, heads),
        split_heads(keys, heads),
        preferred_element_type=jnp.float32,
    )


def mix_heads(probs, values, heads):
    mixed = jnp.einsum(
        "hqk,khd->qhd", probs, split_heads(values, heads), preferred_element_type=jnp.float32
    )
    return mixed.reshape(mixed.shape[0], -1)


def attend(queries, keys, values, valid, heads):
    masked = jnp.where(valid, score_heads(queries, keys, heads), NEGATIVE)
    highest = jnp.max(masked, axis=-1, keepdims=True)
    weights = jnp.where(valid, jnp.exp(masked - highest), 0.0)
    totals = jnp.sum(weights, axis=-1, keepdims=True)
    return (mix_heads(lower(weights / totals), values, heads), highest + jnp.log(totals))


def attend_back(queries, keys, values, valid, heads, log_total, grad_mixed):
    probs = jnp.where(valid, jnp.exp(score_heads(queries, keys, heads) - log_total), 0.0)
    grad_probs = score_heads(grad_mixed, values, heads)
    inner = jnp.sum(probs * grad_probs, axis=-1, keepdims=True)
    grad_scores = lower(probs * (grad_probs - inner))
    return (lower(probs), grad_scores, mix_heads(grad_scores, keys, heads))


def key_terms(grad_scores, probs, queries, grad_mixed, heads):
    grad_keys = jnp.einsum(
        "hqk,qhd->khd", grad_scores, split_heads(queries, heads), preferred_element_type=jnp.float32
    )
    grad_values = jnp.einsum(
        "hqk,qhd->khd", probs, split_heads(grad_mixed, heads), preferred_element_type=jnp.float32
    )
    count = grad_keys.shape[0]
    return jnp.concatenate([grad_keys.reshape(count, -1), grad_values.reshape(count, -1)], axis=1)


def encoder_forward(source, position, valid, params, heads, scale):
    width = source.shape[1]
    source_f = source.astype(jnp.float32)
    mixed_in = lower(source_f + position.astype(jnp.float32))
    query = lower((product(mixed_in, params.attn[0, 0]) + params.attn_bias[0, 0]) * scale)
    key = lower(product(mixed_in, params.attn[0, 1]))
    value = lower(product(source, params.attn[0, 2]) + params.attn_bias[0, 1])
    pairs = lax.all_gather(jnp.concatenate([key, value], axis=1), "seq", axis=0, tiled=True)
    mixed, log_total = attend(query, pairs[:, :width], pairs[:, width:], valid, heads)
    mixed = lower(mixed)
    first_sum = source_f + product(mixed, params.attn_out[0]) + params.attn_bias[0, 2]
    first = norm_apply(first_sum, params.norm_gain[0], params.norm_bias[0])
    inner = product(lower(first), params.ffn_in[0]) + params.ffn_in_bias[0]
    second_sum = (
        first + product(lower(activate(inner)), params.ffn_out[0]) + params.ffn_out_bias[0]
    )
    memory = norm_apply(second_sum, params.norm_gain[1], params.norm_bias[1])
    stash = dict(
        query=query,
        pairs=pairs,
        log_total=log_total,
        mixed=mixed,
        first_sum=first_sum,
        inner=inner,
        second_sum=second_sum,
    )
    return (lower(memory), stash)


def encoder_backward(kept, source, position, valid, grad_memory, params, heads, scale):
    stash = SimpleNamespace(**kept)
    width = source.shape[1]
    rows = source.shape[0]
    query = stash.query
    pairs = stash.pairs
    _, last_back = jax.vjp(
        norm_apply, stash.second_sum, params.norm_gain[1], params.norm_bias[1]
    )
    grad_second, gain_two, bias_two = last_back(grad_memory)
    first, first_back = jax.vjp(
        norm_apply, stash.first_sum, params.norm_gain[0], params.norm_bias[0]
    )
    activated, gelu_back = jax.vjp(activate, stash.inner)
    grad_branch = lower(grad_second)
    grad_inner = lower(gelu_back(right_transposed(grad_branch, params.ffn_out[0]))[0])
    grad_first_sum, gain_one, bias_one = first_back(
        grad_second + right_transposed(grad_inner, params.ffn_in[0])
    )
    grad_attention = lower(grad_first_sum)
    grad_mixed = lower(right_transposed(grad_attention, params.attn_out[0]))
    probs, grad_scores, grad_query = attend_back(
        query, pairs[:, :width], pairs[:, width:], valid, heads, stash.log_total, grad_mixed
    )
    start = jnp.int32(0)
    own = lax.psum_scatter(
        key_terms(
            column_block(grad_scores, start, lax.axis_size("seq") * rows),
            column_block(probs, start, lax.axis_size("seq") * rows),
            query,
            grad_mixed,
            heads,
        ).astype(jnp.bfloat16),
        "seq",
        scatter_dimension=0,
        tiled=True,
    ).astype(jnp.float32)
    grad_key = lower(own[:, :width])
    grad_value = lower(own[:, width:])
    grad_query = lower(grad_query)
    mixed_in = lower(source.astype(jnp.float32) + position.astype(jnp.float32))
    grad_source = (
        grad_first_sum
        + scale * right_transposed(grad_query, params.attn[0, 0])
        + right_transposed(grad_key, params.attn[0, 1])
        + right_transposed(grad_value, params.attn[0, 2])
    )
    grads = dict(
        attn=jnp.stack(
            [
                scale * left_transposed(mixed_in, grad_query),
                left_transposed(mixed_in, grad_key),
                left_transposed(source, grad_value),
            ]
        ),
        attn_out=left_transposed(stash.mixed, grad_attention),
        attn_bias=jnp.stack(
            [scale * column_sum(grad_query), column_sum(grad_value), column_sum(grad_attention)]
        ),
        ffn_in=left_transposed(lower(first), grad_inner),
        ffn_in_bias=column_sum(grad_inner),
        ffn_out=left_transposed(lower(activated), grad_branch),
        ffn_out_bias=column_sum(grad_branch),
        norm_gain=jnp.stack([gain_one, gain_two]),
        norm_bias=jnp.stack([bias_one, bias_two]),
    )
    return (grad_source, grads)


def decoder_step(
    target, points, memory, position, valid, grad_output, params, heads, scale, cross_scale
):
    width = target.shape[1]
    rows = memory.shape[0]
    attn = params.attn
    attn_bias = params.attn_bias
    cross = params.cross
    sine = lower(sine_embed(points, width))
    target_low = lower(target)
    self_in = lower(target + params.query_embed)
    query = lower((product(self_in, attn[1, 0]) + attn_bias[1, 0]) * scale)
    key = lower(product(self_in, attn[1, 1]))
    value = lower(product(target_low, attn[1, 2]) + attn_bias[1, 1])
    everyone = jnp.arange(target.shape[0]) >= 0
    mixed, log_self = attend(query, key, value, everyone, heads)
    mixed = lower(mixed)
    first_sum = target + product(mixed, params.attn_out[1]) + attn_bias[1, 2]
    first, first_back = jax.vjp(
        norm_apply, first_sum, params.norm_gain[2], params.norm_bias[2]
    )
    first_low = lower(first)
    content_key = lower(product(memory, cross[2]))
    place_key = lower(product(position, cross[3]))
    cross_value = lower(product(memory, cross[4]) + attn_bias[2, 1])
    triple = lax.all_gather(
        jnp.concatenate([content_key, place_key, cross_value], axis=1), "seq", axis=0, tiled=True
    )
    content_key = triple[:, :width]
    place_key = triple[:, width : 2 * width]
    cross_value = triple[:, 2 * width :]
    content_query = lower((product(first_low, cross[0]) + attn_bias[2, 0]) * cross_scale)
    place_query = lower(product(sine, cross[1]) * cross_scale)
    joined_query = join_heads(content_query, place_query, heads)
    joined_key = join_heads(content_key, place_key, heads)
    own_start = lax.axis_index("seq") * rows
    cross_mixed, log_cross = attend(joined_query, joined_key, cross_value, valid, heads)
    cross_mixed = lower(cross_mixed)
    second_sum = first + product(cross_mixed, params.attn_out[2]) + attn_bias[2, 2]
    second, second_back = jax.vjp(
        norm_apply, second_sum, params.norm_gain[3], params.norm_bias[3]
    )
    second_low = lower(second)
    inner = product(second_low, params.ffn_in[1]) + params.ffn_in_bias[1]
    activated, gelu_back = jax.vjp(activate, inner)
    activated_low = lower(activated)
    third_sum = second + product(activated_low, params.ffn_out[1]) + params.ffn_out_bias[1]
    output, third_back = jax.vjp(
        norm_apply, third_sum, params.norm_gain[4], params.norm_bias[4]
    )
    grad_third, gain_five, bias_five = third_back(grad_output)
    grad_branch = lower(grad_third)
    grad_inner = lower(gelu_back(right_transposed(grad_branch, params.ffn_out[1]))[0])
    grad_second_sum, gain_four, bias_four = second_back(
        grad_third + right_transposed(grad_inner, params.ffn_in[1])
    )
    grad_cross_out = lower(grad_second_sum)
    grad_cross_mixed = lower(right_transposed(grad_cross_out, params.attn_out[2]))
    cross_probs, cross_scores, grad_joined = attend_back(
        joined_query, joined_key, cross_value, valid, heads, log_cross, grad_cross_mixed
    )
    own = key_terms(
        column_block(cross_scores, own_start, rows),
        column_block(cross_probs, own_start, rows),
        joined_query,
        grad_cross_mixed,
        heads,
    )
    grad_content_key, grad_place_key = part_heads(own[:, : 2 * width], heads)
    grad_content_key = lower(grad_content_key)
    grad_place_key = lower(grad_place_key)
    grad_cross_value = lower(own[:, 2 * width :])
    grad_memory = right_transposed(grad_content_key, cross[2]) + right_transposed(
        grad_cross_value, cross[4]
    )
    grad_content_query, grad_place_query = part_heads(grad_joined, heads)
    grad_content_query = lower(grad_content_query)
    grad_place_query = lower(grad_place_query)
    grad_first = grad_second_sum + cross_scale * right_transposed(grad_content_query, cross[0])
    grad_first_sum, gain_three, bias_three = first_back(grad_first)
    grad_self_out = lower(grad_first_sum)
    grad_mixed = lower(right_transposed(grad_self_out, params.attn_out[1]))
    self_probs, self_scores, grad_query = attend_back(
        query, key, value, everyone, heads, log_self, grad_mixed
    )
    pair = key_terms(self_scores, self_probs, query, grad_mixed, heads)
    grad_key = lower(pair[:, :width])
    grad_value = lower(pair[:, width:])
    grad_query = lower(grad_query)
    grad_self_in = scale * right_transposed(grad_query, attn[1, 0]) + right_transposed(
        grad_key, attn[1, 1]
    )
    grad_target = grad_first_sum + grad_self_in + right_transposed(grad_value, attn[1, 2])
    grads = dict(
        attn=jnp.stack(
            [
                scale * left_transposed(self_in, grad_query),
                left_transposed(self_in, grad_key),
                left_transposed(target_low, grad_value),
            ]
        ),
        attn_out=jnp.stack(
            [left_transposed(mixed, grad_self_out), left_transposed(cross_mixed, grad_cross_out)]
        ),
        attn_bias=jnp.stack(
            [
                jnp.stack(
                    [
                        scale * column_sum(grad_query),
                        column_sum(grad_value),
                        column_sum(grad_self_out),
                    ]
                ),
                jnp.stack(
                    [
                        cross_scale * column_sum(grad_content_query),
                        column_sum(grad_cross_value),
                        column_sum(grad_cross_out),
                    ]
                ),
            ]
        ),
        cross=jnp.stack(
            [
                cross_scale * left_transposed(first_low, grad_content_query),
                cross_scale * left_transposed(sine, grad_place_query),
                left_transposed(memory, grad_content_key),
                left_transposed(position, grad_place_key),
                left_transposed(memory, grad_cross_value),
            ]
        ),
        ffn_in=left_transposed(second_low, grad_inner),
        ffn_in_bias=column_sum(grad_inner),
        ffn_out=left_transposed(activated_low, grad_branch),
        ffn_out_bias=column_sum(grad_branch),
        norm_gain=jnp.stack([gain_three, gain_four, gain_five]),
        norm_bias=jnp.stack([bias_three, bias_four, bias_five]),
        query_embed=grad_self_in,
    )
    return (output, grad_target, lower(grad_memory), grads)


def encoder_zeros(width, inner_width):
    return dict(
        attn=jnp.zeros((3, width, width), jnp.float32),
        attn_out=jnp.zeros((width, width), jnp.float32),
        attn_bias=jnp.zeros((3, width), jnp.float32),
        ffn_in=jnp.zeros((width, inner_width), jnp.float32),
        ffn_in_bias=jnp.zeros((inner_width,), jnp.float32),
        ffn_out=jnp.zeros((inner_width, width), jnp.float32),
        ffn_out_bias=jnp.zeros((width,), jnp.float32),
        norm_gain=jnp.zeros((2, width), jnp.float32),
        norm_bias=jnp.zeros((2, width), jnp.float32),
    )


def decoder_zeros(width, inner_width, queries):
    return dict(
        attn=jnp.zeros((3, width, width), jnp.float32),
        attn_out=jnp.zeros((2, width, width), jnp.float32),
        attn_bias=jnp.zeros((2, 3, width), jnp.float32),
        cross=jnp.zeros((5, width, width), jnp.float32),
        ffn_in=jnp.zeros((width, inner_width), jnp.float32),
        ffn_in_bias=jnp.zeros((inner_width,), jnp.float32),
        ffn_out=jnp.zeros((inner_width, width), jnp.float32),
        ffn_out_bias=jnp.zeros((width,), jnp.float32),
        norm_gain=jnp.zeros((3, width), jnp.float32),
        norm_bias=jnp.zeros((3, width), jnp.float32),
        query_embed=jnp.zeros((queries, width), jnp.float32),
    )


def share_decoder(grads, share, key_share):
    scaled = {name: grads[name] * share for name in grads}
    factor = jnp.array([share, share, key_share, key_share, key_share], jnp.float32)
    scaled["cross"] = grads["cross"] * factor[:, None, None]
    bias_factor = jnp.array([[share, share, share], [share, key_share, share]], jnp.float32)
    scaled["attn_bias"] = grads["attn_bias"] * bias_factor[:, :, None]
    return scaled


def assemble(encoder, decoder):
    encoder = SimpleNamespace(**encoder)
    decoder = SimpleNamespace(**decoder)
    return (
        jnp.stack([encoder.attn, decoder.attn]),
        jnp.concatenate([encoder.attn_out[None], decoder.attn_out]),
        jnp.concatenate([encoder.attn_bias[None], decoder.attn_bias]),
        decoder.cross,
        jnp.stack([encoder.ffn_in, decoder.ffn_in]),
        jnp.stack([encoder.ffn_in_bias, decoder.ffn_in_bias]),
        jnp.stack([encoder.ffn_out, decoder.ffn_out]),
        jnp.stack([encoder.ffn_out_bias, decoder.ffn_out_bias]),
        jnp.concatenate([encoder.norm_gain, decoder.norm_gain]),
        jnp.concatenate([encoder.norm_bias, decoder.norm_bias]),
        decoder.query_embed,
    )


def select_tree(flag, chosen, other):
    return jax.tree.map(lambda first, second: jnp.where(flag, first, second), chosen, other)


def per_device(
    source,
    position,
    lengths,
    target,
    points,
    grad_output,
    attn,
    attn_out,
    attn_bias,
    cross,
    ffn_in,
    ffn_in_bias,
    ffn_out,
    ffn_out_bias,
    norm_gain,
    norm_bias,
    query_embed,
):
    params = SimpleNamespace(
        attn=attn,
        attn_out=attn_out,
        attn_bias=attn_bias,
        cross=cross,
        ffn_in=ffn_in,
        ffn_in_bias=ffn_in_bias,
        ffn_out=ffn_out,
        ffn_out_bias=ffn_out_bias,
        norm_gain=norm_gain,
        norm_bias=norm_bias,
        query_embed=query_embed,
    )
    batches, rows, width = source.shape
    heads = HEADS
    head = width // heads
    scale = head ** (-0.5)
    cross_scale = (2 * head) ** (-0.5)
    queries = target.shape[1]
    inner_width = ffn_in.shape[2]
    seq_count = lax.axis_size("seq")
    positions = jnp.arange(rows * seq_count)
    section = lax.axis_index("section")
    state = dict(
        enc=encoder_zeros(width, inner_width),
        dec=decoder_zeros(width, inner_width, queries),
        stash=dict(
            query=jnp.zeros((batches, rows, width), jnp.bfloat16),
            pairs=jnp.zeros((batches, rows * seq_count, 2 * width), jnp.bfloat16),
            log_total=jnp.zeros((batches, heads, rows, 1), jnp.float32),
            mixed=jnp.zeros((batches, rows, width), jnp.bfloat16),
            first_sum=jnp.zeros((batches, rows, width), jnp.float32),
            inner=jnp.zeros((batches, rows, inner_width), jnp.float32),
            second_sum=jnp.zeros((batches, rows, width), jnp.float32),
        ),
        source=jnp.zeros((batches, rows, width), jnp.float32),
        decoded=jnp.zeros((batches, 2, queries, width), jnp.float32),
    )
    arrived_start = jnp.zeros((rows, width), jnp.bfloat16)
    stored_start = jnp.zeros((batches, rows, width), jnp.bfloat16)

    def tick_step(carry, tick):
        current, incoming, stored = carry
        enc_batch = jnp.minimum(tick, batches - 1)
        dec_batch = jnp.maximum(tick - 1, 0)
        enc_active = jnp.logical_and(section == 0, tick < batches)
        dec_active = jnp.logical_and(section == 1, tick > 0)
        enc_valid = positions < lengths[enc_batch]
        memory, stash = encoder_forward(
            source[enc_batch], position[enc_batch], enc_valid, params, heads, scale
        )
        new_stash = {
            name: lax.dynamic_update_index_in_dim(current["stash"][name], stash[name], enc_batch, 0)
            for name in stash
        }
        dec_valid = positions < lengths[dec_batch]
        output, grad_target, grad_memory, grads = decoder_step(
            target[dec_batch],
            points[dec_batch],
            incoming,
            position[dec_batch],
            dec_valid,
            grad_output[dec_batch],
            params,
            heads,
            scale,
            cross_scale,
        )
        new_dec = jax.tree.map(jnp.add, current["dec"], grads)
        new_decoded = lax.dynamic_update_index_in_dim(
            current["decoded"], jnp.stack([output, grad_target]), dec_batch, 0
        )
        updated = dict(current)
        updated["stash"] = select_tree(enc_active, new_stash, current["stash"])
        updated["dec"] = select_tree(dec_active, new_dec, current["dec"])
        updated["decoded"] = jnp.where(dec_active, new_decoded, current["decoded"])
        outgoing = jnp.where(
            enc_active, memory, jnp.where(dec_active, grad_memory, jnp.zeros_like(memory))
        )
        arrived = swapped(outgoing, "section", 0)
        stored = jnp.where(
            tick > 0, lax.dynamic_update_index_in_dim(stored, arrived, dec_batch, 0), stored
        )
        return ((updated, arrived, stored), None)

    (state, _, stored), _ = lax.scan(
        tick_step, (state, arrived_start, stored_start), jnp.arange(batches + 1)
    )

    def back_step(current, batch):
        valid = positions < lengths[batch]
        stash = {name: current["stash"][name][batch] for name in current["stash"]}
        grad_source, grads = encoder_backward(
            stash,
            source[batch],
            position[batch],
            valid,
            stored[batch].astype(jnp.float32),
            params,
            heads,
            scale,
        )
        active = section == 0
        updated = dict(current)
        updated["enc"] = select_tree(
            active, jax.tree.map(jnp.add, current["enc"], grads), current["enc"]
        )
        updated["source"] = jnp.where(
            active,
            lax.dynamic_update_index_in_dim(current["source"], grad_source, batch, 0),
            current["source"],
        )
        return (updated, None)

    state, _ = lax.scan(back_step, state, jnp.arange(batches))
    share = 1.0 / seq_count
    key_share = 1.0
    encoder = state["enc"]
    decoder = share_decoder(state["dec"], share, key_share)
    half = batches // 2
    source_upper = state["source"][half:]
    decoded_lower = state["decoded"][:half]
    parts = assemble(encoder, decoder)
    summed = lax.psum(
        (
            parts[0],
            parts[1],
            parts[2],
            parts[3],
            parts[4],
            parts[5],
            parts[6],
            parts[7],
            parts[8],
            parts[9],
            parts[10],
        ),
        ("dp", "section", "seq"),
    )
    other_source, other_decoded = (
        swapped(source_upper.astype(jnp.bfloat16), "section", 0).astype(source_upper.dtype),
        swapped(decoded_lower.astype(jnp.bfloat16), "section", 0).astype(decoded_lower.dtype),
    )
    grad_source = jnp.where(section == 0, state["source"][:half], other_source)
    decoded = jnp.where(section == 0, other_decoded, state["decoded"][half:])
    return (
        decoded[:, 0],
        grad_source,
        decoded[:, 1],
        summed[0],
        summed[1],
        summed[2],
        summed[3],
        summed[4],
        summed[5],
        summed[6],
        summed[7],
        summed[8],
        summed[9],
        summed[10],
    )


BF16 = jnp.bfloat16
F32 = jnp.float32


def dot_nn(left, right):
    return lax.dot_general(left, right, (((1,), (0,)), ((), ())), preferred_element_type=F32)


def dot_nt(left, right):
    return lax.dot_general(left, right, (((1,), (1,)), ((), ())), preferred_element_type=F32)


def dot_tn(left, right):
    return lax.dot_general(left, right, (((0,), (0,)), ((), ())), preferred_element_type=F32)


def rows_sum(value):
    return jnp.sum(value.astype(F32), axis=0, keepdims=True)


def norm_parts(value):
    center = value - jnp.mean(value, axis=-1, keepdims=True)
    scale = lax.rsqrt(jnp.mean(center * center, axis=-1, keepdims=True) + EPSILON)
    return center * scale, scale


def norm_back(grad, unit, scale, gain):
    scaled = grad * gain
    inner = jnp.mean(scaled * unit, axis=-1, keepdims=True)
    back = scale * (scaled - jnp.mean(scaled, axis=-1, keepdims=True) - unit * inner)
    return back, rows_sum(grad * unit), rows_sum(grad)


def gelu_parts(value):
    root = math.sqrt(2.0 / math.pi)
    square = value * value
    bend = jnp.tanh(root * value * (1.0 + 0.044715 * square))
    half = 0.5 * (1.0 + bend)
    slope = half + 0.5 * value * (1.0 - bend * bend) * (root * (1.0 + 3.0 * 0.044715 * square))
    return value * half, slope


def head_mask(width, index):
    lane = lax.broadcasted_iota(jnp.int32, (1, width), 1)
    size = width // HEADS
    inside = jnp.logical_and(lane >= index * size, lane < (index + 1) * size)
    return jnp.where(inside, 1.0, 0.0).astype(BF16)


def attend_heads(pairs, values, bias):
    width = values.shape[1]
    count = pairs[0][0].shape[0]
    column = lax.broadcasted_iota(jnp.int32, (count, 128), 1)
    mixed = jnp.zeros((count, width), F32)
    logs = jnp.zeros((count, 128), F32)
    for head in range(HEADS):
        mask = head_mask(width, head)
        scores = bias
        for queries, keys in pairs:
            scores = scores + dot_nt(queries * mask, keys)
        highest = jnp.max(scores, axis=-1, keepdims=True)
        weights = jnp.exp(scores - highest)
        total = jnp.sum(weights, axis=-1, keepdims=True)
        probs = (weights * (1.0 / total)).astype(BF16)
        mixed = mixed + dot_nn(probs, values * mask)
        logs = jnp.where(column == head, highest + jnp.log(total), logs)
    return mixed, logs


def attend_heads_back(pairs, values, bias, logs, grad_mixed, key_refs, value_ref):
    width = values.shape[1]
    size = width // HEADS
    turned_grad = grad_mixed.T
    turned_queries = [queries.T for queries, _ in pairs]
    grads = [jnp.zeros(queries.shape, F32) for queries, _ in pairs]
    for head in range(HEADS):
        mask = head_mask(width, head)
        log = logs[:, head : head + 1]
        scores = bias
        for queries, keys in pairs:
            scores = scores + dot_nt(queries * mask, keys)
        probs = jnp.exp(scores - log)
        grad_probs = dot_nt(grad_mixed * mask, values)
        inner = jnp.sum(probs * grad_probs, axis=-1, keepdims=True)
        grad_scores = (probs * (grad_probs - inner)).astype(BF16)
        part = slice(head * size, (head + 1) * size)
        value_ref[part, :] = dot_nn(turned_grad[part, :], probs.astype(BF16))
        for index, (queries, keys) in enumerate(pairs):
            key_refs[index][part, :] = dot_nn(turned_queries[index][part, :], grad_scores)
            grads[index] = grads[index] + dot_nn(grad_scores, keys * mask)
    return grads


def place_in_pair():
    return lax.axis_index("section"), lax.axis_index("seq")


def rows_at(half, count):
    return pl.ds(pl.multiple_of(half * count, count), count)


def token_bias(lengths, image, rows):
    seq = lax.axis_index("seq")
    lane = lax.broadcasted_iota(jnp.int32, (1, rows), 1)
    length = lengths[image]
    parts = [jnp.where((seq ^ bit) * rows + lane < length, 0.0, NEGATIVE) for bit in range(4)]
    return jnp.concatenate(parts, axis=1)


def query_bias(queries, padded):
    lane = lax.broadcasted_iota(jnp.int32, (1, padded), 1)
    return jnp.where(lane < queries, 0.0, NEGATIVE)


def put_halves(scratch, own, other):
    half = place_in_pair()[0]
    size = scratch.shape[0] // 2
    scratch[rows_at(half, size)] = own
    scratch[rows_at(1 - half, size)] = other
    return scratch[...]


def fetch(source, target, semaphore):
    copy = pltpu.make_async_copy(source, target, semaphore)
    copy.start()
    return copy


ENTERED, TARGET, KEY, VALUE, MINE, QUERY, MIXED = ((0, 2), (2, 4), (4, 6), (6, 8), (8, 9), (9, 10), (10, 11))
SUM, FIRST, LOGS = ((0, 1), (1, 2), (2, 3))


def kept_part(ref, part, own):
    return ref.at[part[0] * own : part[1] * own, :]


def pack_kernel(source, position, mine_o, near_o, far_o, farthest_o):
    width = source.shape[2]
    rows = near_o.shape[0]
    half, image = place_in_pair()
    part = rows_at(half, rows)
    for array, columns in ((source, slice(0, width)), (position, slice(width, 2 * width))):
        mine_o[:, columns] = array[image]
        for bit, out in ((1, near_o), (2, far_o), (3, farthest_o)):
            out[:, columns] = array[image ^ bit, part, :]


def stack_kernel(*refs):
    size = refs[0].shape[0]
    for index, ref in enumerate(refs[:-1]):
        refs[-1][index * size : (index + 1) * size, :] = ref[...]


def self_forward_kernel(
    scale, own, target, embed, attn, attn_bias, attn_out, gain, shift,
    low_o, full_o,
    arrived_s, target_s, embed_s, semaphore,
):
    width = embed.shape[1]
    padded = 2 * own
    queries = embed.shape[0]
    half, image = place_in_pair()
    copy = fetch(target.at[image], arrived_s, semaphore)
    embed_s[:queries] = embed[...]
    for scratch in (embed_s, target_s):
        scratch[queries:] = jnp.zeros((padded - queries, width), F32)
    copy.wait()
    target_s[:queries] = arrived_s[...]
    mine = rows_at(half, own)
    whole = target_s[...]
    own_target = target_s[mine]
    entered = (whole + embed_s[...]).astype(BF16)
    low = whole.astype(BF16)
    own_entered = (own_target + embed_s[mine]).astype(BF16)
    query = ((dot_nn(own_entered, attn[0]) + attn_bias[1, 0:1]) * scale).astype(BF16)
    key = dot_nn(entered, attn[1]).astype(BF16)
    value = (dot_nn(low, attn[2]) + attn_bias[1, 1:2]).astype(BF16)
    mixed, logs = attend_heads([(query, key)], value, query_bias(queries, padded))
    mixed = mixed.astype(BF16)
    first_sum = own_target + dot_nn(mixed, attn_out[...]) + attn_bias[1, 2:3]
    unit, _ = norm_parts(first_sum)
    parts = ((ENTERED, entered), (TARGET, low), (KEY, key), (VALUE, value), (MINE, own_entered), (QUERY, query), (MIXED, mixed))
    for part, values in parts:
        kept_part(low_o, part, own)[...] = values
    kept_part(full_o, SUM, own)[...] = first_sum
    kept_part(full_o, FIRST, own)[...] = unit * gain[2:3] + shift[2:3]
    full_o[LOGS[0] * own :, :128] = logs
    full_o[LOGS[0] * own :, 128:] = jnp.zeros((own, width - 128), F32)


def cross_query_kernel(
    cross_scale, own, points, full_d, tokens, period, cross, attn_bias,
    sine_o, content_o, place_o, place_key_o,
    points_s, spots_s,
):
    width = full_d.shape[1]
    first = kept_part(full_d, FIRST, own)
    half, image = place_in_pair()
    points_s[...] = jnp.zeros(points_s.shape, F32)
    points_s[: points.shape[1], : points.shape[2]] = points[image]
    spots_s[...] = points_s[...].T
    place_key_o[...] = dot_nn(tokens[:, width:], cross[3]).astype(BF16)
    content_o[...] = ((dot_nn(first[...].astype(BF16), cross[0]) + attn_bias[2, 0:1]) * cross_scale).astype(BF16)
    spots = spots_s[rows_at(half, own)]
    lane = lax.broadcasted_iota(jnp.int32, (1, width), 1)
    angle = jnp.where(lane < width // 2, spots[:, 1:2], spots[:, 0:1]) * (2.0 * math.pi) / period[...]
    sine = jnp.where(lane % 2 == 0, jnp.sin(angle), jnp.cos(angle)).astype(BF16)
    sine_o[...] = sine
    place_o[...] = (dot_nn(sine, cross[1]) * cross_scale).astype(BF16)


def encoder_forward_kernel(
    scale, lengths, chunk, arrived, others, attn, attn_bias, attn_out, ffn_in, ffn_in_bias, ffn_out, ffn_out_bias, gain, shift,
    query_o, key_o, value_o, mixed_o, logs_o, sum_o, second_o, memory_o, tokens_o,
):
    own, width = query_o.shape
    rows = chunk.shape[0]
    half = place_in_pair()[0]
    tokens_o[:rows, :] = chunk[...]
    part = rows // 2
    for index in range(3):
        source_rows = slice(index * part, (index + 1) * part)
        for place, ref in ((half, arrived), (1 - half, others)):
            tokens_o[pl.ds(pl.multiple_of((index + 1) * rows + place * part, part), part), :] = ref[source_rows, :]
    tokens = tokens_o[...]
    mine = tokens_o[rows_at(half, own)].astype(F32)
    own_source = mine[:, :width]
    own_entered = (own_source + mine[:, width:]).astype(BF16)
    source = tokens[:, :width]
    position = tokens[:, width:]
    bias = token_bias(lengths, place_in_pair()[1], rows)
    entered = (source.astype(F32) + position.astype(F32)).astype(BF16)
    query = ((dot_nn(own_entered, attn[0]) + attn_bias[0, 0:1]) * scale).astype(BF16)
    key = dot_nn(entered, attn[1]).astype(BF16)
    value = (dot_nn(source, attn[2]) + attn_bias[0, 1:2]).astype(BF16)
    mixed, logs = attend_heads([(query, key)], value, bias)
    mixed = mixed.astype(BF16)
    first_sum = own_source + dot_nn(mixed, attn_out[...]) + attn_bias[0, 2:3]
    unit, _ = norm_parts(first_sum)
    first = unit * gain[0:1] + shift[0:1]
    first_low = first.astype(BF16)
    second_sum = first + ffn_out_bias[0:1]
    inner_width = ffn_in.shape[1]
    for start in range(0, inner_width, width):
        part = slice(start, start + width)
        active, _ = gelu_parts(dot_nn(first_low, ffn_in[:, part]) + ffn_in_bias[0:1, part])
        second_sum = second_sum + dot_nn(active.astype(BF16), ffn_out[part, :])
    unit, _ = norm_parts(second_sum)
    query_o[...] = query
    key_o[...] = key
    value_o[...] = value
    mixed_o[...] = mixed
    logs_o[...] = logs
    sum_o[...] = first_sum
    second_o[...] = second_sum
    memory_o[...] = (unit * gain[1:2] + shift[1:2]).astype(BF16)


def cross_forward_kernel(
    lengths, memory_own, memory_other, place_key, full_d, content, place, grad_output,
    cross, attn_bias, attn_out, ffn_in, ffn_in_bias, ffn_out, ffn_out_bias, gain, shift,
    output_o, key_o, value_o, logs_o, grad_o, grad_mixed_o, keep_o, send_o, out_o, small_o,
    active_s, slope_s, piece_s, grad_s, arrived_s, memory_s, semaphore,
):
    own, width = content.shape
    first = kept_part(full_d, FIRST, own)
    queries = arrived_s.shape[0]
    half, image = place_in_pair()
    copy = fetch(grad_output.at[image], arrived_s, semaphore)
    bias = token_bias(lengths, image, memory_own.shape[0] // 2)
    memory = put_halves(memory_s, memory_own[...], memory_other[...])
    key = dot_nn(memory, cross[2]).astype(BF16)
    value = (dot_nn(memory, cross[4]) + attn_bias[2, 1:2]).astype(BF16)
    mixed, logs = attend_heads([(content[...], key), (place[...], place_key[...])], value, bias)
    mixed = mixed.astype(BF16)
    key_o[...] = key
    value_o[...] = value
    logs_o[...] = logs
    second_sum = first[...] + dot_nn(mixed, attn_out[...]) + attn_bias[2, 2:3]
    second_unit, second_scale = norm_parts(second_sum)
    second = second_unit * gain[3:4] + shift[3:4]
    second_low = second.astype(BF16)
    third_sum = second + ffn_out_bias[1:2]
    inner_width = ffn_in.shape[1]
    for start in range(0, inner_width, width):
        part = slice(start, start + width)
        active, slope = gelu_parts(dot_nn(second_low, ffn_in[:, part]) + ffn_in_bias[1:2, part])
        active = active.astype(BF16)
        active_s[:, part] = active
        slope_s[:, part] = slope
        third_sum = third_sum + dot_nn(active, ffn_out[part, :])
    unit, scale = norm_parts(third_sum)
    output_o[...] = (unit * gain[4:5] + shift[4:5]).astype(output_o.dtype)
    copy.wait()
    grad_s[:queries] = arrived_s[...]
    grad_s[queries:] = jnp.zeros((grad_s.shape[0] - queries, width), F32)
    grad_third, gain_five, shift_five = norm_back(grad_s[rows_at(half, own)], unit, scale, gain[4:5])
    branch = grad_third.astype(BF16)
    grad_second = grad_third
    for index, start in enumerate(range(0, inner_width, width)):
        part = slice(start, start + width)
        grad_inner = (dot_nt(branch, ffn_out[part, :]) * slope_s[:, part]).astype(BF16)
        grad_second = grad_second + dot_nt(grad_inner, ffn_in[:, part])
        piece_s[part, :] = dot_tn(second_low, grad_inner).astype(BF16)
        piece_s[inner_width + start : inner_width + start + width, :] = dot_tn(active_s[:, part], branch).astype(BF16)
        small_o[index : index + 1, :] = rows_sum(grad_inner)
    spread(piece_s, keep_o, send_o)
    grad_second_sum, gain_four, shift_four = norm_back(grad_second, second_unit, second_scale, gain[3:4])
    cross_out = grad_second_sum.astype(BF16)
    grad_o[...] = grad_second_sum
    grad_mixed_o[...] = dot_nt(cross_out, attn_out[...]).astype(BF16)
    out_o[...] = dot_tn(mixed, cross_out).astype(BF16)
    base = inner_width // width
    rest = [rows_sum(branch), gain_four, gain_five, shift_four, shift_five, rows_sum(cross_out)]
    for index, row in enumerate(rest):
        small_o[base + index : base + index + 1, :] = row
    small_o[base + len(rest) :, :] = jnp.zeros((small_o.shape[0] - base - len(rest), width), F32)


def cross_back_kernel(
    lengths, key, value, place_key, content, place, logs, grad_mixed, cross,
    memory_own_o, memory_other_o, grad_key_o, grad_place_key_o, grad_value_o, grad_content_o, grad_place_o,
    key_s, place_s, value_s, grad_s,
):
    own = memory_own_o.shape[0]
    bias = token_bias(lengths, place_in_pair()[1], own // 2)
    grad_content, grad_place = attend_heads_back(
        [(content[...], key[...]), (place[...], place_key[...])],
        value[...], bias, logs[...], grad_mixed[...], [key_s, place_s], value_s,
    )
    grad_key = key_s[...].T.astype(BF16)
    grad_value = value_s[...].T.astype(BF16)
    grad_memory = dot_nt(grad_key, cross[2]) + dot_nt(grad_value, cross[4])
    grad_s[...] = grad_memory
    half = place_in_pair()[0]
    memory_own_o[...] = grad_s[rows_at(half, own)]
    memory_other_o[...] = grad_s[rows_at(1 - half, own)].astype(BF16)
    grad_key_o[...] = grad_key
    grad_value_o[...] = grad_value
    grad_place_key_o[...] = place_s[...].T.astype(BF16)
    grad_content_o[...] = grad_content.astype(BF16)
    grad_place_o[...] = grad_place.astype(BF16)


def self_back_kernel(
    scale, cross_scale, queries,
    low_d, full_d, sine, grad_second_sum,
    memory_own, memory_other, tokens, grad_key, grad_place_key, grad_value, grad_content, grad_place, cross_out, small_c,
    attn, attn_out, cross, gain, shift,
    target_own_o, target_other_o, grads_o,
    key_s, value_s, rows_s, memory_s,
):
    own, width = sine.shape
    padded = 2 * own
    low = lambda part: kept_part(low_d, part, own)[...]
    logs = full_d[LOGS[0] * own :, :128]
    half = place_in_pair()[0]
    mine, other = rows_at(half, own), rows_at(1 - half, own)
    unit, norm_scale = norm_parts(kept_part(full_d, SUM, own)[...])
    first_low = (unit * gain[2:3] + shift[2:3]).astype(BF16)
    grad_first = grad_second_sum[...] + cross_scale * dot_nt(grad_content[...], cross[...])
    grad_first_sum, gain_three, shift_three = norm_back(grad_first, unit, norm_scale, gain[2:3])
    branch = grad_first_sum.astype(BF16)
    grad_mixed = dot_nt(branch, attn_out[...]).astype(BF16)
    (grad_query,) = attend_heads_back(
        [(low(QUERY), low(KEY))], low(VALUE), query_bias(queries, padded), logs, grad_mixed, [key_s], value_s
    )
    grad_query = grad_query.astype(BF16)
    self_key = key_s[...].T.astype(BF16)
    self_value = value_s[...].T.astype(BF16)
    from_query = scale * dot_nt(grad_query, attn[0])
    from_key = dot_nt(self_key, attn[1])
    from_value = dot_nt(self_value, attn[2])
    rows_s[...] = from_key + from_value
    target_own_o[...] = rows_s[mine] + grad_first_sum + from_query
    target_other_o[...] = rows_s[other].astype(BF16)
    rows_s[...] = from_key
    rows_s[mine] += from_query
    position = tokens[:, width:]
    memory = put_halves(memory_s, memory_own[...], memory_other[...])
    small = [
        scale * rows_sum(grad_query),
        rows_sum(self_value),
        rows_sum(branch),
        cross_scale * rows_sum(grad_content[...]),
        rows_sum(grad_value[...]),
        gain_three,
        shift_three,
        jnp.zeros((9, width), F32),
    ]
    grads = [
        scale * dot_tn(low(MINE), grad_query),
        dot_tn(low(ENTERED), self_key),
        dot_tn(low(TARGET), self_value),
        dot_tn(low(MIXED), branch),
        cross_scale * dot_tn(first_low, grad_content[...]),
        cross_scale * dot_tn(sine[...], grad_place[...]),
        dot_tn(memory, grad_key[...]),
        dot_tn(position, grad_place_key[...]),
        dot_tn(memory, grad_value[...]),
        cross_out[...],
        rows_s[...],
        small_c[...],
        jnp.concatenate(small, axis=0),
    ]
    fill(grads_o, grads)


def encoder_ffn_back_kernel(
    grad_own, grad_other, first_sum, second_sum, mixed, attn_out, ffn_in, ffn_in_bias, ffn_out, gain, shift,
    grad_o, grad_mixed_o, keep_o, send_o, out_o, small_o,
    piece_s,
):
    width = first_sum.shape[1]
    inner_width = ffn_in.shape[1]
    grad_memory = (grad_own[...] + grad_other[...].astype(F32)).astype(BF16).astype(F32)
    second_unit, second_scale = norm_parts(second_sum[...])
    grad_second, gain_two, shift_two = norm_back(grad_memory, second_unit, second_scale, gain[1:2])
    branch = grad_second.astype(BF16)
    unit, scale = norm_parts(first_sum[...])
    first_low = (unit * gain[0:1] + shift[0:1]).astype(BF16)
    grad_first = grad_second
    for index, start in enumerate(range(0, inner_width, width)):
        part = slice(start, start + width)
        active, slope = gelu_parts(dot_nn(first_low, ffn_in[:, part]) + ffn_in_bias[0:1, part])
        grad_inner = (dot_nt(branch, ffn_out[part, :]) * slope).astype(BF16)
        grad_first = grad_first + dot_nt(grad_inner, ffn_in[:, part])
        piece_s[part, :] = dot_tn(first_low, grad_inner).astype(BF16)
        piece_s[inner_width + start : inner_width + start + width, :] = dot_tn(active.astype(BF16), branch).astype(BF16)
        small_o[index : index + 1, :] = rows_sum(grad_inner)
    spread(piece_s, keep_o, send_o)
    grad_first_sum, gain_one, shift_one = norm_back(grad_first, unit, scale, gain[0:1])
    attention = grad_first_sum.astype(BF16)
    out_o[...] = dot_tn(mixed[...], attention).astype(BF16)
    grad_o[...] = grad_first_sum
    grad_mixed_o[...] = dot_nt(attention, attn_out[...]).astype(BF16)
    base = inner_width // width
    rest = [rows_sum(branch), gain_one, gain_two, shift_one, shift_two, rows_sum(attention)]
    for index, row in enumerate(rest):
        small_o[base + index : base + index + 1, :] = row
    small_o[base + len(rest) :, :] = jnp.zeros((small_o.shape[0] - base - len(rest), width), F32)


def encoder_attention_back_kernel(
    scale, lengths, tokens, query, key, value, logs, grad_first_sum, grad_mixed, encoder_out, small_e, decoder_grads, attn,
    source_o, source_low_o, keep_o, send_o,
    key_s, value_s, piece_s, source_s, tokens_s,
):
    own, width = query.shape
    rows = tokens.shape[0] // 4
    bias = token_bias(lengths, place_in_pair()[1], rows)
    (grad_query,) = attend_heads_back(
        [(query[...], key[...])], value[...], bias, logs[...], grad_mixed[...], [key_s], value_s
    )
    grad_query = grad_query.astype(BF16)
    grad_key = key_s[...].T.astype(BF16)
    grad_value = value_s[...].T.astype(BF16)
    from_query = grad_first_sum[...] + scale * dot_nt(grad_query, attn[0])
    grad_source = dot_nt(grad_key, attn[1]) + dot_nt(grad_value, attn[2])
    mine = rows_at(place_in_pair()[0], own)
    source_s[...] = grad_source
    source_s[mine] += from_query
    source_o[...] = source_s[...]
    source_low_o[...] = source_s[...].astype(BF16)
    source = tokens[:, :width]
    entered = (source.astype(F32) + tokens[:, width:].astype(F32)).astype(BF16)
    tokens_s[...] = entered
    grads = [
        scale * dot_tn(tokens_s[mine], grad_query),
        dot_tn(entered, grad_key),
        dot_tn(source, grad_value),
        encoder_out[...],
        small_e[...],
        jnp.concatenate([scale * rows_sum(grad_query), rows_sum(grad_value), jnp.zeros((14, width), F32)], axis=0),
        decoder_grads[...],
    ]
    fill(piece_s, grads)
    spread(piece_s, keep_o, send_o)


PARTS = 16


def place_code(core):
    spot = lax.axis_index("dp")
    low, high = spot % 2, spot // 2
    swap = core == 1
    first, second = jnp.where(swap, high, low), jnp.where(swap, low, high)
    return first * 4 + second * 2 + lax.axis_index("seq") % 2


def fill(piece, grads):
    start = 0
    for grad in grads:
        piece[start : start + grad.shape[0], :] = grad.astype(BF16)
        start += grad.shape[0]
    if start < piece.shape[0]:
        piece[start:, :] = jnp.zeros((piece.shape[0] - start, piece.shape[1]), BF16)


def spread(piece, keep_o, send_o):
    half = PARTS // 2
    count = piece.shape[0] // PARTS
    me = lax.axis_index("section")
    for core, out in ((me, keep_o), (1 - me, send_o)):
        code = place_code(core)
        for slot in range(half):
            out[slot * count : (slot + 1) * count, :] = piece[rows_at(core * half + (slot ^ code), count), :]


def added(first, second):
    return (first.astype(F32) + second.astype(F32)).astype(BF16)


def add_whole_kernel(own, arrived, out):
    out[...] = added(own[...], arrived[...])


def add_split_kernel(own, arrived, keep_o, send_o):
    size = keep_o.shape[0]
    keep_o[...] = added(own[:size, :], arrived[:size, :])
    send_o[...] = added(own[size:, :], arrived[size:, :])


def join_kernel(near, far, out):
    size = near.shape[0]
    out[:size, :] = near[...]
    out[size:, :] = far[...]


def crossed(block, axis, bit):
    return lax.ppermute(block, axis, [(index, index ^ bit) for index in range(lax.axis_size(axis))])


def crossed_plane(block, step):
    pairs = []
    for spot in range(lax.axis_size("dp")):
        for core in range(2):
            pairs.append((spot * 2 + core, (spot ^ (1 if core == step else 2)) * 2 + core))
    return lax.ppermute(block, ("dp", "section"), pairs)


def reduce_steps(keep, send):
    size, width = keep.shape
    low = lambda rows: ((rows, width), BF16)
    moves = [
        lambda block: crossed(block, "section", 1),
        lambda block: crossed_plane(block, 0),
        lambda block: crossed_plane(block, 1),
        lambda block: crossed(block, "seq", 1),
        lambda block: crossed(block, "seq", 2),
    ]
    for move in moves[:3]:
        after, micros = yield keep
        size //= 2
        keep, send = run(add_split_kernel, [low(size)] * 2, [keep, move(send)], after=after, micros=micros)
    after, micros = yield keep
    (total,) = run(add_whole_kernel, [low(size)], [keep, moves[3](send)], after=after, micros=micros)
    after, micros = yield total
    (total,) = run(add_whole_kernel, [low(size)], [total, moves[4](total)], after=after, micros=micros)
    for move in reversed(moves[1:4]):
        after, micros = yield total
        size *= 2
        (total,) = run(join_kernel, [low(size)], [total, move(total)], after=after, micros=micros)
    yield total, moves[0](total)


class Piece:
    def __init__(self, keep, send):
        self.steps = reduce_steps(keep, send)
        next(self.steps)

    def step(self, *after, micros=0.1):
        return self.steps.send((after, micros))

    def finish(self, *after, micros=0.1):
        result = self.step(*after, micros=micros)
        while not isinstance(result, tuple):
            result = self.step(micros=micros)
        return result


def part_rows(near, far, start, rows, write):
    half = PARTS // 2
    count = near.shape[0] // half
    me = lax.axis_index("section")
    for part in range(start // count, -(-(start + rows) // count)):
        core = part // half
        slot = (part % half) ^ place_code(core)
        for ref, here in ((near, me == core), (far, me != core)):

            @pl.when(here)
            def _():
                write(part * count - start, ref[rows_at(slot, count), :].astype(F32))


def ffn_result_kernel(*refs):
    near, far = refs[:2]
    in_o, out_o = refs[-2:]
    inner_width, width = out_o.shape

    def write_in(offset, values):
        for start in range(0, values.shape[0], width):
            block = (offset + start) // width
            row = (offset + start) % width
            part = values[start : start + width]
            in_o[row : row + part.shape[0], block * width : (block + 1) * width] = part

    def write_out(offset, values):
        out_o[offset : offset + values.shape[0], :] = values

    part_rows(near, far, 0, inner_width, write_in)
    part_rows(near, far, inner_width, inner_width, write_out)


def rest_result_kernel(
    padded, near, far, attn_o, out_o, attn_bias_o, cross_o, ffn_in_bias_o, ffn_out_bias_o, gain_o, shift_o, embed_o, piece_s
):
    width = gain_o.shape[1]

    def write(offset, values):
        piece_s[offset : offset + values.shape[0], :] = values

    part_rows(near, far, 0, piece_s.shape[0], write)
    encoder = 4 * width
    decoder = encoder + 32
    late = decoder + 10 * width + padded
    block = lambda start, index: piece_s[start + index * width : start + (index + 1) * width, :]
    for index in range(3):
        attn_o[0, index] = block(0, index)
        attn_o[1, index] = block(decoder, index)
    out_o[0] = block(0, 3)
    out_o[1] = block(decoder, 3)
    out_o[2] = block(decoder, 9)
    for index in range(5):
        cross_o[index] = block(decoder, 4 + index)
    embed_o[...] = piece_s[decoder + 10 * width : decoder + 10 * width + embed_o.shape[0], :]
    row = lambda start: piece_s[start : start + 1, :]
    blocks = ffn_in_bias_o.shape[1] // width
    row_e = lambda index: row(encoder + index)
    row_a = lambda index: row(encoder + 16 + index)
    row_c = lambda index: row(late + index)
    row_d = lambda index: row(late + 16 + index)
    bias = [
        row_a(0), row_a(1), row_e(blocks + 5),
        row_d(0), row_d(1), row_d(2),
        row_d(3), row_d(4), row_c(blocks + 5),
    ]
    for index, values in enumerate(bias):
        attn_bias_o[index // 3, index % 3 : index % 3 + 1, :] = values
    for index in range(blocks):
        part = slice(index * width, (index + 1) * width)
        ffn_in_bias_o[0:1, part] = row_e(index)
        ffn_in_bias_o[1:2, part] = row_c(index)
    ffn_out_bias_o[0:1, :] = row_e(blocks)
    ffn_out_bias_o[1:2, :] = row_c(blocks)
    for index, out in ((1, gain_o), (3, shift_o)):
        rows = [row_e(blocks + index), row_e(blocks + index + 1), row_d(5 + index // 2)]
        rows += [row_c(blocks + index), row_c(blocks + index + 1)]
        for place, values in enumerate(rows):
            out[place : place + 1, :] = values


def is_home():
    return lax.axis_index("seq") // 2 == lax.axis_index("section")


def sent_far(block):
    pairs = []
    for core in range(2):
        for spot in range(4):
            if spot // 2 == core:
                pairs.append((core * 4 + spot, core * 4 + (spot ^ 2)))
    return lax.ppermute(block, ("section", "seq"), pairs)


def queries_pack_kernel(output, target_own, target_arrived, out):
    own = output.shape[0]
    out[:own, :] = output[...]
    out[own:, :] = (target_own[...] + target_arrived[...].astype(F32)).astype(BF16)


def chosen_kernel(home, arrived, out):
    @pl.when(is_home())
    def _():
        out[...] = home[...]

    @pl.when(jnp.logical_not(is_home()))
    def _():
        out[...] = arrived[...]


def queries_result_kernel(mine, near, output_o, target_o, rows_s):
    own = mine.shape[0] // 4
    core = lax.axis_index("section")
    spot = lax.axis_index("seq") % 2
    for index, out in enumerate((output_o, target_o)):
        for image, ref in ((spot, mine), (1 - spot, near)):
            for half in range(2):
                start = (2 * half + index) * own
                place = core if half == 0 else 1 - core
                rows_s[image, rows_at(place, own), :] = ref[start : start + own, :].astype(F32)
        out[...] = rows_s[:, : out.shape[1], :]


def source_sum_kernel(own, arrived, keep_o, send_o):
    size = keep_o.shape[0]
    total = own[...] + arrived[...].astype(F32)
    keep_o[...] = total[:size]
    send_o[...] = total[size:].astype(BF16)


def source_pair_kernel(home, arrived, keep_o, send_o):
    rows = keep_o.shape[0]

    @pl.when(is_home())
    def _():
        keep_o[...] = home[:rows, :]
        send_o[...] = home[rows:, :].astype(BF16)

    @pl.when(jnp.logical_not(is_home()))
    def _():
        keep_o[...] = arrived[:rows, :].astype(F32)
        send_o[...] = arrived[rows:, :]


def source_result_kernel(mine, near, out_o):
    spot = lax.axis_index("seq") % 2
    out_o[spot] = mine[...]
    out_o[1 - spot] = near[...].astype(F32)


def whole_spec(shape):
    return pl.BlockSpec(shape, lambda step: (0,) * len(shape))


def part_spec(shape, index):
    return pl.BlockSpec((None,) + shape[1:], lambda step: (index,) + (0,) * (len(shape) - 1))


def run(kernel, outs, operands, scratch=(), micros=1.0, limit=16, after=(), hold=()):
    arrays, specs, places = [], [], []
    for operand in operands:
        array, extra = operand if isinstance(operand, tuple) else (operand, None)
        spec = extra if isinstance(extra, pl.BlockSpec) else pl.BlockSpec(memory_space=pltpu.VMEM)
        arrays.append(array)
        specs.append(spec)
        places.append(extra if isinstance(extra, int) else None)

    def body(*refs):
        parts = [ref if place is None else ref.at[place] for ref, place in zip(refs, places)]
        kernel(*parts, *refs[len(places) + len(after) + len(hold) :])

    return pl.pallas_call(
        body,
        name=getattr(kernel, "func", kernel).__name__,
        out_shape=[jax.ShapeDtypeStruct(shape, dtype) for shape, dtype in outs],
        in_specs=specs + [pl.BlockSpec(memory_space=pl.ANY)] * len(after) + [pl.BlockSpec(memory_space=pltpu.VMEM)] * len(hold),
        out_specs=[pl.BlockSpec(memory_space=pltpu.VMEM) for _ in outs],
        scratch_shapes=[pltpu.VMEM(*item) if isinstance(item, tuple) else item for item in scratch],
        compiler_params=pltpu.CompilerParams(vmem_limit_bytes=limit * 1024 * 1024),
        cost_estimate=pl.CostEstimate(flops=int(micros * 1.15e9), bytes_accessed=1024, transcendentals=0),
    )(*arrays, *after, *hold)


def run_parts(kernel, outs, operands, scratch=(), aliases=None, micros=2.0, after=()):
    arrays, specs = [], []
    for operand in operands:
        array, spec = operand if isinstance(operand, tuple) else (operand, whole_spec(operand.shape))
        arrays.append(array)
        specs.append(spec)
    count = len(specs) + len(after)

    def body(*refs):
        kernel(*refs[: len(specs)], *refs[count : count + len(outs)], *refs[count + len(outs) + 1 :])
        refs[count + len(outs)][...] = jnp.zeros((8, 128), F32)

    return pl.pallas_call(
        body,
        name=getattr(kernel, "func", kernel).__name__,
        grid=(1,),
        out_shape=[jax.ShapeDtypeStruct(out[0], out[1]) for out in outs] + [jax.ShapeDtypeStruct((8, 128), F32)],
        in_specs=specs + [pl.BlockSpec(memory_space=pl.ANY)] * len(after),
        out_specs=[out[2] if len(out) > 2 else whole_spec(out[0]) for out in outs] + [whole_spec((8, 128))],
        scratch_shapes=[pltpu.VMEM(shape, dtype) for shape, dtype in scratch],
        input_output_aliases=aliases or {},
        compiler_params=pltpu.CompilerParams(vmem_limit_bytes=24 * 1024 * 1024),
        cost_estimate=pl.CostEstimate(flops=int(micros * 1.15e9), bytes_accessed=1024, transcendentals=0),
    )(*arrays, *after)


def traded(block, bit):
    return crossed(block, "seq", bit)


def with_pair(block):
    return crossed(block, "section", 1)


BEFORE = "d"
AFTER = "edqwperwdewdeswtdewedweewhDEuw"


def paired_device(
    source, position, lengths, target, points, grad_output,
    attn, attn_out, attn_bias, cross, ffn_in, ffn_in_bias, ffn_out, ffn_out_bias, norm_gain, norm_bias, query_embed,
):
    batches, rows, width = source.shape
    queries = target.shape[1]
    inner_width = ffn_in.shape[2]
    images = batches // lax.axis_size("section")
    tokens = rows * lax.axis_size("seq")
    half_tokens = tokens // 2
    half_queries = -(-queries // 32) * 16
    padded = 2 * half_queries
    head = width // HEADS
    scale = head ** (-0.5)
    cross_scale = (2 * head) ** (-0.5)
    wide = lambda count: ((count, 2 * width), BF16)
    chunk, *parts = run(pack_kernel, [wide(rows)] + [wide(rows // 2)] * 3, [source, position])
    parts = [traded(part, bit + 1) for bit, part in enumerate(parts)]

    column = np.arange(width) % (width // 2)
    period = (10000.0 ** ((2 * (column // 2)).astype(np.float32) / np.float32(width // 2))).astype(np.float32)[None]
    lengths = (lengths, pl.BlockSpec(memory_space=pltpu.SMEM))
    low = lambda count, columns=width: ((count, columns), BF16)
    full = lambda count, columns=width: ((count, columns), F32)
    part = lambda array, index: (array, index)

    elsewhere = lambda array: (array, pl.BlockSpec(memory_space=pl.ANY))
    copied = pltpu.SemaphoreType.DMA
    lanes = -(-padded // 128) * 128

    low_d, full_d = run(
        functools.partial(self_forward_kernel, scale, half_queries),
        [low(11 * half_queries), full(3 * half_queries)],
        [elsewhere(target), query_embed, part(attn, 1), attn_bias, part(attn_out, 1), norm_gain, norm_bias],
        [full(queries), full(padded), full(padded), copied], micros=12.0,
    )

    (arrived,) = run(stack_kernel, [wide(3 * rows // 2)], parts, after=[low_d], hold=[ffn_in, ffn_out])
    query_e, key_e, value_e, mixed_e, logs_e, sum_e, second_e, memory, token_rows = run(
        functools.partial(encoder_forward_kernel, scale),
        [low(half_tokens), low(tokens), low(tokens), low(half_tokens), full(half_tokens, 128),
         full(half_tokens), full(half_tokens), low(half_tokens), wide(tokens)],
        [lengths, chunk, arrived, with_pair(arrived), part(attn, 0), attn_bias, part(attn_out, 0),
         part(ffn_in, 0), ffn_in_bias, part(ffn_out, 0), ffn_out_bias, norm_gain, norm_bias], micros=21.0, after=[low_d],
    )

    sine, content, place_query, place_key = run(
        functools.partial(cross_query_kernel, cross_scale, half_queries),
        [low(half_queries), low(half_queries), low(half_queries), low(tokens)],
        [points.transpose(0, 2, 1), full_d, token_rows, jnp.asarray(period), cross, attn_bias],
        [full(8, lanes), full(lanes, 8)], micros=6.0, after=[mixed_e],
    )
    memory_other = with_pair(memory)
    piece = lambda rows: [low(rows // 2)] * 2
    output_half, cross_key, cross_value, logs_c, grad_second_sum, grad_cross_mixed, keep_d, send_d, out_c, small_c = run(
        cross_forward_kernel,
        [low(half_queries), low(tokens), low(tokens), full(half_queries, 128), full(half_queries), low(half_queries),
         *piece(2 * inner_width), low(width), full(16)],
        [lengths, memory, memory_other, place_key, full_d, content, place_query, elsewhere(grad_output),
         cross, attn_bias, part(attn_out, 2), part(ffn_in, 1), ffn_in_bias, part(ffn_out, 1), ffn_out_bias, norm_gain, norm_bias],
        [low(half_queries, inner_width), full(half_queries, inner_width), low(2 * inner_width), full(padded), full(queries), low(tokens), copied],
        micros=30.0,
    )
    piece_d = Piece(keep_d, send_d)

    memory_grad_own, memory_grad_other, grad_key, grad_place_key, grad_value, grad_content, grad_place = run(
        cross_back_kernel,
        [full(half_tokens), low(half_tokens), low(tokens), low(tokens), low(tokens), low(half_queries), low(half_queries)],
        [lengths, cross_key, cross_value, place_key, content, place_query, logs_c, grad_cross_mixed, cross],
        [full(width, tokens)] * 3 + [full(tokens)],
        micros=21.0,
    )
    memory_grad_partner = with_pair(memory_grad_other)

    count_d = 10 * width + padded + 32
    target_own, target_other, grads_d = run(
        functools.partial(self_back_kernel, scale, cross_scale, queries),
        [full(half_queries), low(half_queries), low(count_d)],
        [low_d, full_d, sine, grad_second_sum, memory, memory_other, token_rows,
         grad_key, grad_place_key, grad_value, grad_content, grad_place, out_c, small_c,
         part(attn, 1), part(attn_out, 1), part(cross, 0), norm_gain, norm_bias],
        [full(width, padded), full(width, padded), full(padded), low(tokens)], micros=18.0, after=[piece_d.step()],
    )

    grad_first_sum, grad_mixed, keep_e, send_e, out_e, small_e = run(
        encoder_ffn_back_kernel,
        [full(half_tokens), low(half_tokens), *piece(2 * inner_width), low(width), full(16)],
        [memory_grad_own, memory_grad_partner, sum_e, second_e, mixed_e, part(attn_out, 0),
         part(ffn_in, 0), ffn_in_bias, part(ffn_out, 0), norm_gain, norm_bias],
        [low(2 * inner_width)], micros=21.0, after=[grads_d, piece_d.step()],
    )
    piece_e = Piece(keep_e, send_e)

    count_w = -(-(4 * width + 32 + count_d) // (16 * PARTS)) * 16 * PARTS
    source_full, source_low, keep_w, send_w = run(
        functools.partial(encoder_attention_back_kernel, scale),
        [full(tokens), low(tokens), *piece(count_w)],
        [lengths, token_rows, query_e, key_e, value_e, logs_e, grad_first_sum, grad_mixed, out_e, small_e, grads_d, part(attn, 0)],
        [full(width, tokens), full(width, tokens), low(count_w), full(tokens), low(tokens)],
        micros=21.0, after=[{"d": piece_d, "e": piece_e}[step].step() for step in BEFORE],
    )
    piece_w = Piece(keep_w, send_w)

    def kept(shape, index):
        return (shape, F32, part_spec(shape, index))

    pieces = dict(d=piece_d, e=piece_e, w=piece_w)
    sums = {}
    packed_halves = [output_half, target_own, with_pair(target_other)]
    mark = keep_w
    for step in AFTER:
        if step in pieces:
            result = pieces[step].step(mark, micros=6.0)
            if isinstance(result, tuple):
                sums[step] = result
                result = result[0]
            mark = result
        elif step == "q":
            (halves,) = run(queries_pack_kernel, [low(2 * half_queries)], packed_halves, after=[mark], micros=6.0)
            mark = halves
        elif step == "r":
            (halves,) = run(join_kernel, [low(4 * half_queries)], [halves, with_pair(halves)], after=[mark], micros=6.0)
            mark = halves
        elif step == "h":
            (halves,) = run(chosen_kernel, [low(4 * half_queries)], [halves, sent_far(halves)], after=[mark], micros=6.0)
            mark = halves
        elif step == "u":
            decoder_output, grad_target, mark = run_parts(
                queries_result_kernel, [((images, queries, width), F32)] * 2, [halves, traded(halves, 1)],
                [((images, padded, width), F32)], after=[mark],
            )
        elif step == "p":
            source_home, source_far = run(
                source_sum_kernel, [full(half_tokens), low(half_tokens)], [source_full, with_pair(source_low)], after=[mark], micros=6.0
            )
            mark = source_home
        elif step == "s":
            source_mine, source_near = run(
                source_pair_kernel, [full(rows), low(rows)], [source_home, sent_far(source_far)], after=[mark], micros=6.0
            )
            mark = source_mine
        elif step == "t":
            grad_source, mark = run_parts(
                source_result_kernel, [((images, rows, width), F32)], [source_mine, traded(source_near, 1)], after=[mark]
            )
        elif step == "D":
            *grad_ffn, mark = run_parts(
                ffn_result_kernel, [kept(ffn_in.shape, 1), kept(ffn_out.shape, 1)], sums["d"], after=[mark]
            )
        elif step == "E":
            before = [(array, pl.BlockSpec(memory_space=pl.ANY)) for array in grad_ffn]
            *grad_ffn, mark = run_parts(
                ffn_result_kernel, [kept(ffn_in.shape, 0), kept(ffn_out.shape, 0)], [*sums["e"], *before], aliases={2: 0, 3: 1}, after=[mark]
            )
    grad_ffn_in, grad_ffn_out = grad_ffn
    rest = (attn, attn_out, attn_bias, cross, ffn_in_bias, ffn_out_bias, norm_gain, norm_bias, query_embed)
    *grads, _ = run_parts(
        functools.partial(rest_result_kernel, padded), [(array.shape, F32) for array in rest],
        sums["w"], [full(count_w)]
    )
    grad_attn, grad_attn_out, grad_attn_bias, grad_cross, grad_ffn_in_bias, grad_ffn_out_bias, grad_gain, grad_shift, grad_embed = grads
    return (
        decoder_output, grad_source, grad_target, grad_attn, grad_attn_out, grad_attn_bias, grad_cross,
        grad_ffn_in, grad_ffn_in_bias, grad_ffn_out, grad_ffn_out_bias, grad_gain, grad_shift, grad_embed,
    )


def chosen_plan(*args):
    batches = args[0].shape[0]
    sections = lax.axis_size("section")
    paired = sections == 2 and batches == lax.axis_size("seq") == lax.axis_size("dp") == 4
    return (paired_device if paired else per_device)(*args)


def solution(mesh):
    placed = (
        P("dp", "seq", None),
        P("dp", "seq", None),
        P("dp"),
        P("dp", None, None),
        P("dp", None, None),
        P("dp", None, None),
        P(),
        P(),
        P(),
        P(),
        P(),
        P(),
        P(),
        P(),
        P(),
        P(),
        P(),
    )
    return jax.shard_map(
        chosen_plan,
        mesh=mesh,
        in_specs=placed,
        out_specs=(
            P(("dp", "section"), None, None),
            P(("dp", "section"), "seq", None),
            P(("dp", "section"), None, None),
            P(),
            P(),
            P(),
            P(),
            P(),
            P(),
            P(),
            P(),
            P(),
            P(),
            P(),
        ),
        check_vma=False,
    )
```

```python
import functools
import math
from types import SimpleNamespace

import jax
import jax.numpy as jnp
import numpy as np
from jax import lax
from jax.experimental import pallas as pl
from jax.experimental.pallas import tpu as pltpu
from jax.sharding import PartitionSpec as P

HEADS = 8


EPSILON = 1e-05
NEGATIVE = -1e30


def swapped(block, axis, bit):
    count = lax.axis_size(axis)
    route = []
    for low in range(count):
        high = low | 1 << bit
        if high != low and high < count:
            route += [(low, high), (high, low)]
    return lax.ppermute(block, axis, route)


def lower(value):
    return value.astype(jnp.bfloat16)


def product(left, right):
    return jnp.dot(left, right, preferred_element_type=jnp.float32)


def left_transposed(left, right):
    return lax.dot_general(
        left, right, (((0,), (0,)), ((), ())), preferred_element_type=jnp.float32
    )


def right_transposed(left, right):
    return lax.dot_general(
        left, right, (((1,), (1,)), ((), ())), preferred_element_type=jnp.float32
    )


def column_sum(value):
    return jnp.sum(value.astype(jnp.float32), axis=0)


def norm_apply(value, gain, shift):
    center = value - jnp.mean(value, axis=-1, keepdims=True)
    scale = lax.rsqrt(jnp.mean(center * center, axis=-1, keepdims=True) + EPSILON)
    return center * scale * gain + shift


def activate(value):
    return jax.nn.gelu(value)


def sine_embed(points, width):
    half_width = width // 2
    column = jnp.arange(half_width)
    period = 10000.0 ** ((2 * (column // 2)).astype(jnp.float32) / half_width)

    def embed(coordinate):
        angle = coordinate[..., None] * (2.0 * math.pi) / period
        return jnp.where(column % 2 == 0, jnp.sin(angle), jnp.cos(angle))

    return jnp.concatenate([embed(points[..., 1]), embed(points[..., 0])], axis=-1)


def split_heads(value, heads):
    return value.reshape(value.shape[0], heads, value.shape[1] // heads)


def join_heads(first, second, heads):
    joined = jnp.concatenate([split_heads(first, heads), split_heads(second, heads)], axis=2)
    return joined.reshape(first.shape[0], 2 * first.shape[1])


def part_heads(value, heads):
    count = value.shape[0]
    split = split_heads(value, heads)
    middle = split.shape[2] // 2
    return (split[:, :, :middle].reshape(count, -1), split[:, :, middle:].reshape(count, -1))


def column_block(value, start, count):
    return lax.dynamic_slice_in_dim(value, start, count, 2)


def score_heads(queries, keys, heads):
    return jnp.einsum(
        "qhd,khd->hqk",
        split_heads(queries, heads),
        split_heads(keys, heads),
        preferred_element_type=jnp.float32,
    )


def mix_heads(probs, values, heads):
    mixed = jnp.einsum(
        "hqk,khd->qhd", probs, split_heads(values, heads), preferred_element_type=jnp.float32
    )
    return mixed.reshape(mixed.shape[0], -1)


def attend(queries, keys, values, valid, heads):
    masked = jnp.where(valid, score_heads(queries, keys, heads), NEGATIVE)
    highest = jnp.max(masked, axis=-1, keepdims=True)
    weights = jnp.where(valid, jnp.exp(masked - highest), 0.0)
    totals = jnp.sum(weights, axis=-1, keepdims=True)
    return (mix_heads(lower(weights / totals), values, heads), highest + jnp.log(totals))


def attend_back(queries, keys, values, valid, heads, log_total, grad_mixed):
    probs = jnp.where(valid, jnp.exp(score_heads(queries, keys, heads) - log_total), 0.0)
    grad_probs = score_heads(grad_mixed, values, heads)
    inner = jnp.sum(probs * grad_probs, axis=-1, keepdims=True)
    grad_scores = lower(probs * (grad_probs - inner))
    return (lower(probs), grad_scores, mix_heads(grad_scores, keys, heads))


def key_terms(grad_scores, probs, queries, grad_mixed, heads):
    grad_keys = jnp.einsum(
        "hqk,qhd->khd", grad_scores, split_heads(queries, heads), preferred_element_type=jnp.float32
    )
    grad_values = jnp.einsum(
        "hqk,qhd->khd", probs, split_heads(grad_mixed, heads), preferred_element_type=jnp.float32
    )
    count = grad_keys.shape[0]
    return jnp.concatenate([grad_keys.reshape(count, -1), grad_values.reshape(count, -1)], axis=1)


def encoder_forward(source, position, valid, params, heads, scale):
    width = source.shape[1]
    source_f = source.astype(jnp.float32)
    mixed_in = lower(source_f + position.astype(jnp.float32))
    query = lower((product(mixed_in, params.attn[0, 0]) + params.attn_bias[0, 0]) * scale)
    key = lower(product(mixed_in, params.attn[0, 1]))
    value = lower(product(source, params.attn[0, 2]) + params.attn_bias[0, 1])
    pairs = lax.all_gather(jnp.concatenate([key, value], axis=1), "seq", axis=0, tiled=True)
    mixed, log_total = attend(query, pairs[:, :width], pairs[:, width:], valid, heads)
    mixed = lower(mixed)
    first_sum = source_f + product(mixed, params.attn_out[0]) + params.attn_bias[0, 2]
    first = norm_apply(first_sum, params.norm_gain[0], params.norm_bias[0])
    inner = product(lower(first), params.ffn_in[0]) + params.ffn_in_bias[0]
    second_sum = (
        first + product(lower(activate(inner)), params.ffn_out[0]) + params.ffn_out_bias[0]
    )
    memory = norm_apply(second_sum, params.norm_gain[1], params.norm_bias[1])
    stash = dict(
        query=query,
        pairs=pairs,
        log_total=log_total,
        mixed=mixed,
        first_sum=first_sum,
        inner=inner,
        second_sum=second_sum,
    )
    return (lower(memory), stash)


def encoder_backward(kept, source, position, valid, grad_memory, params, heads, scale):
    stash = SimpleNamespace(**kept)
    width = source.shape[1]
    rows = source.shape[0]
    query = stash.query
    pairs = stash.pairs
    _, last_back = jax.vjp(
        norm_apply, stash.second_sum, params.norm_gain[1], params.norm_bias[1]
    )
    grad_second, gain_two, bias_two = last_back(grad_memory)
    first, first_back = jax.vjp(
        norm_apply, stash.first_sum, params.norm_gain[0], params.norm_bias[0]
    )
    activated, gelu_back = jax.vjp(activate, stash.inner)
    grad_branch = lower(grad_second)
    grad_inner = lower(gelu_back(right_transposed(grad_branch, params.ffn_out[0]))[0])
    grad_first_sum, gain_one, bias_one = first_back(
        grad_second + right_transposed(grad_inner, params.ffn_in[0])
    )
    grad_attention = lower(grad_first_sum)
    grad_mixed = lower(right_transposed(grad_attention, params.attn_out[0]))
    probs, grad_scores, grad_query = attend_back(
        query, pairs[:, :width], pairs[:, width:], valid, heads, stash.log_total, grad_mixed
    )
    start = jnp.int32(0)
    own = lax.psum_scatter(
        key_terms(
            column_block(grad_scores, start, lax.axis_size("seq") * rows),
            column_block(probs, start, lax.axis_size("seq") * rows),
            query,
            grad_mixed,
            heads,
        ).astype(jnp.bfloat16),
        "seq",
        scatter_dimension=0,
        tiled=True,
    ).astype(jnp.float32)
    grad_key = lower(own[:, :width])
    grad_value = lower(own[:, width:])
    grad_query = lower(grad_query)
    mixed_in = lower(source.astype(jnp.float32) + position.astype(jnp.float32))
    grad_source = (
        grad_first_sum
        + scale * right_transposed(grad_query, params.attn[0, 0])
        + right_transposed(grad_key, params.attn[0, 1])
        + right_transposed(grad_value, params.attn[0, 2])
    )
    grads = dict(
        attn=jnp.stack(
            [
                scale * left_transposed(mixed_in, grad_query),
                left_transposed(mixed_in, grad_key),
                left_transposed(source, grad_value),
            ]
        ),
        attn_out=left_transposed(stash.mixed, grad_attention),
        attn_bias=jnp.stack(
            [scale * column_sum(grad_query), column_sum(grad_value), column_sum(grad_attention)]
        ),
        ffn_in=left_transposed(lower(first), grad_inner),
        ffn_in_bias=column_sum(grad_inner),
        ffn_out=left_transposed(lower(activated), grad_branch),
        ffn_out_bias=column_sum(grad_branch),
        norm_gain=jnp.stack([gain_one, gain_two]),
        norm_bias=jnp.stack([bias_one, bias_two]),
    )
    return (grad_source, grads)


def decoder_step(
    target, points, memory, position, valid, grad_output, params, heads, scale, cross_scale
):
    width = target.shape[1]
    rows = memory.shape[0]
    attn = params.attn
    attn_bias = params.attn_bias
    cross = params.cross
    sine = lower(sine_embed(points, width))
    target_low = lower(target)
    self_in = lower(target + params.query_embed)
    query = lower((product(self_in, attn[1, 0]) + attn_bias[1, 0]) * scale)
    key = lower(product(self_in, attn[1, 1]))
    value = lower(product(target_low, attn[1, 2]) + attn_bias[1, 1])
    everyone = jnp.arange(target.shape[0]) >= 0
    mixed, log_self = attend(query, key, value, everyone, heads)
    mixed = lower(mixed)
    first_sum = target + product(mixed, params.attn_out[1]) + attn_bias[1, 2]
    first, first_back = jax.vjp(
        norm_apply, first_sum, params.norm_gain[2], params.norm_bias[2]
    )
    first_low = lower(first)
    content_key = lower(product(memory, cross[2]))
    place_key = lower(product(position, cross[3]))
    cross_value = lower(product(memory, cross[4]) + attn_bias[2, 1])
    triple = lax.all_gather(
        jnp.concatenate([content_key, place_key, cross_value], axis=1), "seq", axis=0, tiled=True
    )
    content_key = triple[:, :width]
    place_key = triple[:, width : 2 * width]
    cross_value = triple[:, 2 * width :]
    content_query = lower((product(first_low, cross[0]) + attn_bias[2, 0]) * cross_scale)
    place_query = lower(product(sine, cross[1]) * cross_scale)
    joined_query = join_heads(content_query, place_query, heads)
    joined_key = join_heads(content_key, place_key, heads)
    own_start = lax.axis_index("seq") * rows
    cross_mixed, log_cross = attend(joined_query, joined_key, cross_value, valid, heads)
    cross_mixed = lower(cross_mixed)
    second_sum = first + product(cross_mixed, params.attn_out[2]) + attn_bias[2, 2]
    second, second_back = jax.vjp(
        norm_apply, second_sum, params.norm_gain[3], params.norm_bias[3]
    )
    second_low = lower(second)
    inner = product(second_low, params.ffn_in[1]) + params.ffn_in_bias[1]
    activated, gelu_back = jax.vjp(activate, inner)
    activated_low = lower(activated)
    third_sum = second + product(activated_low, params.ffn_out[1]) + params.ffn_out_bias[1]
    output, third_back = jax.vjp(
        norm_apply, third_sum, params.norm_gain[4], params.norm_bias[4]
    )
    grad_third, gain_five, bias_five = third_back(grad_output)
    grad_branch = lower(grad_third)
    grad_inner = lower(gelu_back(right_transposed(grad_branch, params.ffn_out[1]))[0])
    grad_second_sum, gain_four, bias_four = second_back(
        grad_third + right_transposed(grad_inner, params.ffn_in[1])
    )
    grad_cross_out = lower(grad_second_sum)
    grad_cross_mixed = lower(right_transposed(grad_cross_out, params.attn_out[2]))
    cross_probs, cross_scores, grad_joined = attend_back(
        joined_query, joined_key, cross_value, valid, heads, log_cross, grad_cross_mixed
    )
    own = key_terms(
        column_block(cross_scores, own_start, rows),
        column_block(cross_probs, own_start, rows),
        joined_query,
        grad_cross_mixed,
        heads,
    )
    grad_content_key, grad_place_key = part_heads(own[:, : 2 * width], heads)
    grad_content_key = lower(grad_content_key)
    grad_place_key = lower(grad_place_key)
    grad_cross_value = lower(own[:, 2 * width :])
    grad_memory = right_transposed(grad_content_key, cross[2]) + right_transposed(
        grad_cross_value, cross[4]
    )
    grad_content_query, grad_place_query = part_heads(grad_joined, heads)
    grad_content_query = lower(grad_content_query)
    grad_place_query = lower(grad_place_query)
    grad_first = grad_second_sum + cross_scale * right_transposed(grad_content_query, cross[0])
    grad_first_sum, gain_three, bias_three = first_back(grad_first)
    grad_self_out = lower(grad_first_sum)
    grad_mixed = lower(right_transposed(grad_self_out, params.attn_out[1]))
    self_probs, self_scores, grad_query = attend_back(
        query, key, value, everyone, heads, log_self, grad_mixed
    )
    pair = key_terms(self_scores, self_probs, query, grad_mixed, heads)
    grad_key = lower(pair[:, :width])
    grad_value = lower(pair[:, width:])
    grad_query = lower(grad_query)
    grad_self_in = scale * right_transposed(grad_query, attn[1, 0]) + right_transposed(
        grad_key, attn[1, 1]
    )
    grad_target = grad_first_sum + grad_self_in + right_transposed(grad_value, attn[1, 2])
    grads = dict(
        attn=jnp.stack(
            [
                scale * left_transposed(self_in, grad_query),
                left_transposed(self_in, grad_key),
                left_transposed(target_low, grad_value),
            ]
        ),
        attn_out=jnp.stack(
            [left_transposed(mixed, grad_self_out), left_transposed(cross_mixed, grad_cross_out)]
        ),
        attn_bias=jnp.stack(
            [
                jnp.stack(
                    [
                        scale * column_sum(grad_query),
                        column_sum(grad_value),
                        column_sum(grad_self_out),
                    ]
                ),
                jnp.stack(
                    [
                        cross_scale * column_sum(grad_content_query),
                        column_sum(grad_cross_value),
                        column_sum(grad_cross_out),
                    ]
                ),
            ]
        ),
        cross=jnp.stack(
            [
                cross_scale * left_transposed(first_low, grad_content_query),
                cross_scale * left_transposed(sine, grad_place_query),
                left_transposed(memory, grad_content_key),
                left_transposed(position, grad_place_key),
                left_transposed(memory, grad_cross_value),
            ]
        ),
        ffn_in=left_transposed(second_low, grad_inner),
        ffn_in_bias=column_sum(grad_inner),
        ffn_out=left_transposed(activated_low, grad_branch),
        ffn_out_bias=column_sum(grad_branch),
        norm_gain=jnp.stack([gain_three, gain_four, gain_five]),
        norm_bias=jnp.stack([bias_three, bias_four, bias_five]),
        query_embed=grad_self_in,
    )
    return (output, grad_target, lower(grad_memory), grads)


def encoder_zeros(width, inner_width):
    return dict(
        attn=jnp.zeros((3, width, width), jnp.float32),
        attn_out=jnp.zeros((width, width), jnp.float32),
        attn_bias=jnp.zeros((3, width), jnp.float32),
        ffn_in=jnp.zeros((width, inner_width), jnp.float32),
        ffn_in_bias=jnp.zeros((inner_width,), jnp.float32),
        ffn_out=jnp.zeros((inner_width, width), jnp.float32),
        ffn_out_bias=jnp.zeros((width,), jnp.float32),
        norm_gain=jnp.zeros((2, width), jnp.float32),
        norm_bias=jnp.zeros((2, width), jnp.float32),
    )


def decoder_zeros(width, inner_width, queries):
    return dict(
        attn=jnp.zeros((3, width, width), jnp.float32),
        attn_out=jnp.zeros((2, width, width), jnp.float32),
        attn_bias=jnp.zeros((2, 3, width), jnp.float32),
        cross=jnp.zeros((5, width, width), jnp.float32),
        ffn_in=jnp.zeros((width, inner_width), jnp.float32),
        ffn_in_bias=jnp.zeros((inner_width,), jnp.float32),
        ffn_out=jnp.zeros((inner_width, width), jnp.float32),
        ffn_out_bias=jnp.zeros((width,), jnp.float32),
        norm_gain=jnp.zeros((3, width), jnp.float32),
        norm_bias=jnp.zeros((3, width), jnp.float32),
        query_embed=jnp.zeros((queries, width), jnp.float32),
    )


def share_decoder(grads, share, key_share):
    scaled = {name: grads[name] * share for name in grads}
    factor = jnp.array([share, share, key_share, key_share, key_share], jnp.float32)
    scaled["cross"] = grads["cross"] * factor[:, None, None]
    bias_factor = jnp.array([[share, share, share], [share, key_share, share]], jnp.float32)
    scaled["attn_bias"] = grads["attn_bias"] * bias_factor[:, :, None]
    return scaled


def assemble(encoder, decoder):
    encoder = SimpleNamespace(**encoder)
    decoder = SimpleNamespace(**decoder)
    return (
        jnp.stack([encoder.attn, decoder.attn]),
        jnp.concatenate([encoder.attn_out[None], decoder.attn_out]),
        jnp.concatenate([encoder.attn_bias[None], decoder.attn_bias]),
        decoder.cross,
        jnp.stack([encoder.ffn_in, decoder.ffn_in]),
        jnp.stack([encoder.ffn_in_bias, decoder.ffn_in_bias]),
        jnp.stack([encoder.ffn_out, decoder.ffn_out]),
        jnp.stack([encoder.ffn_out_bias, decoder.ffn_out_bias]),
        jnp.concatenate([encoder.norm_gain, decoder.norm_gain]),
        jnp.concatenate([encoder.norm_bias, decoder.norm_bias]),
        decoder.query_embed,
    )


def select_tree(flag, chosen, other):
    return jax.tree.map(lambda first, second: jnp.where(flag, first, second), chosen, other)


def per_device(
    source,
    position,
    lengths,
    target,
    points,
    grad_output,
    attn,
    attn_out,
    attn_bias,
    cross,
    ffn_in,
    ffn_in_bias,
    ffn_out,
    ffn_out_bias,
    norm_gain,
    norm_bias,
    query_embed,
):
    params = SimpleNamespace(
        attn=attn,
        attn_out=attn_out,
        attn_bias=attn_bias,
        cross=cross,
        ffn_in=ffn_in,
        ffn_in_bias=ffn_in_bias,
        ffn_out=ffn_out,
        ffn_out_bias=ffn_out_bias,
        norm_gain=norm_gain,
        norm_bias=norm_bias,
        query_embed=query_embed,
    )
    batches, rows, width = source.shape
    heads = HEADS
    head = width // heads
    scale = head ** (-0.5)
    cross_scale = (2 * head) ** (-0.5)
    queries = target.shape[1]
    inner_width = ffn_in.shape[2]
    seq_count = lax.axis_size("seq")
    positions = jnp.arange(rows * seq_count)
    section = lax.axis_index("section")
    state = dict(
        enc=encoder_zeros(width, inner_width),
        dec=decoder_zeros(width, inner_width, queries),
        stash=dict(
            query=jnp.zeros((batches, rows, width), jnp.bfloat16),
            pairs=jnp.zeros((batches, rows * seq_count, 2 * width), jnp.bfloat16),
            log_total=jnp.zeros((batches, heads, rows, 1), jnp.float32),
            mixed=jnp.zeros((batches, rows, width), jnp.bfloat16),
            first_sum=jnp.zeros((batches, rows, width), jnp.float32),
            inner=jnp.zeros((batches, rows, inner_width), jnp.float32),
            second_sum=jnp.zeros((batches, rows, width), jnp.float32),
        ),
        source=jnp.zeros((batches, rows, width), jnp.float32),
        decoded=jnp.zeros((batches, 2, queries, width), jnp.float32),
    )
    arrived_start = jnp.zeros((rows, width), jnp.bfloat16)
    stored_start = jnp.zeros((batches, rows, width), jnp.bfloat16)

    def tick_step(carry, tick):
        current, incoming, stored = carry
        enc_batch = jnp.minimum(tick, batches - 1)
        dec_batch = jnp.maximum(tick - 1, 0)
        enc_active = jnp.logical_and(section == 0, tick < batches)
        dec_active = jnp.logical_and(section == 1, tick > 0)
        enc_valid = positions < lengths[enc_batch]
        memory, stash = encoder_forward(
            source[enc_batch], position[enc_batch], enc_valid, params, heads, scale
        )
        new_stash = {
            name: lax.dynamic_update_index_in_dim(current["stash"][name], stash[name], enc_batch, 0)
            for name in stash
        }
        dec_valid = positions < lengths[dec_batch]
        output, grad_target, grad_memory, grads = decoder_step(
            target[dec_batch],
            points[dec_batch],
            incoming,
            position[dec_batch],
            dec_valid,
            grad_output[dec_batch],
            params,
            heads,
            scale,
            cross_scale,
        )
        new_dec = jax.tree.map(jnp.add, current["dec"], grads)
        new_decoded = lax.dynamic_update_index_in_dim(
            current["decoded"], jnp.stack([output, grad_target]), dec_batch, 0
        )
        updated = dict(current)
        updated["stash"] = select_tree(enc_active, new_stash, current["stash"])
        updated["dec"] = select_tree(dec_active, new_dec, current["dec"])
        updated["decoded"] = jnp.where(dec_active, new_decoded, current["decoded"])
        outgoing = jnp.where(
            enc_active, memory, jnp.where(dec_active, grad_memory, jnp.zeros_like(memory))
        )
        arrived = swapped(outgoing, "section", 0)
        stored = jnp.where(
            tick > 0, lax.dynamic_update_index_in_dim(stored, arrived, dec_batch, 0), stored
        )
        return ((updated, arrived, stored), None)

    (state, _, stored), _ = lax.scan(
        tick_step, (state, arrived_start, stored_start), jnp.arange(batches + 1)
    )

    def back_step(current, batch):
        valid = positions < lengths[batch]
        stash = {name: current["stash"][name][batch] for name in current["stash"]}
        grad_source, grads = encoder_backward(
            stash,
            source[batch],
            position[batch],
            valid,
            stored[batch].astype(jnp.float32),
            params,
            heads,
            scale,
        )
        active = section == 0
        updated = dict(current)
        updated["enc"] = select_tree(
            active, jax.tree.map(jnp.add, current["enc"], grads), current["enc"]
        )
        updated["source"] = jnp.where(
            active,
            lax.dynamic_update_index_in_dim(current["source"], grad_source, batch, 0),
            current["source"],
        )
        return (updated, None)

    state, _ = lax.scan(back_step, state, jnp.arange(batches))
    share = 1.0 / seq_count
    key_share = 1.0
    encoder = state["enc"]
    decoder = share_decoder(state["dec"], share, key_share)
    half = batches // 2
    source_upper = state["source"][half:]
    decoded_lower = state["decoded"][:half]
    parts = assemble(encoder, decoder)
    summed = lax.psum(
        (
            parts[0],
            parts[1],
            parts[2],
            parts[3],
            parts[4],
            parts[5],
            parts[6],
            parts[7],
            parts[8],
            parts[9],
            parts[10],
        ),
        ("dp", "section", "seq"),
    )
    other_source, other_decoded = (
        swapped(source_upper.astype(jnp.bfloat16), "section", 0).astype(source_upper.dtype),
        swapped(decoded_lower.astype(jnp.bfloat16), "section", 0).astype(decoded_lower.dtype),
    )
    grad_source = jnp.where(section == 0, state["source"][:half], other_source)
    decoded = jnp.where(section == 0, other_decoded, state["decoded"][half:])
    return (
        decoded[:, 0],
        grad_source,
        decoded[:, 1],
        summed[0],
        summed[1],
        summed[2],
        summed[3],
        summed[4],
        summed[5],
        summed[6],
        summed[7],
        summed[8],
        summed[9],
        summed[10],
    )


BF16 = jnp.bfloat16
F32 = jnp.float32


def dot_nn(left, right):
    return lax.dot_general(left, right, (((1,), (0,)), ((), ())), preferred_element_type=F32)


def dot_nt(left, right):
    return lax.dot_general(left, right, (((1,), (1,)), ((), ())), preferred_element_type=F32)


def dot_tn(left, right):
    return lax.dot_general(left, right, (((0,), (0,)), ((), ())), preferred_element_type=F32)


def rows_sum(value):
    return jnp.sum(value.astype(F32), axis=0, keepdims=True)


def norm_parts(value):
    center = value - jnp.mean(value, axis=-1, keepdims=True)
    scale = lax.rsqrt(jnp.mean(center * center, axis=-1, keepdims=True) + EPSILON)
    return center * scale, scale


def norm_back(grad, unit, scale, gain):
    scaled = grad * gain
    inner = jnp.mean(scaled * unit, axis=-1, keepdims=True)
    back = scale * (scaled - jnp.mean(scaled, axis=-1, keepdims=True) - unit * inner)
    return back, rows_sum(grad * unit), rows_sum(grad)


def gelu_parts(value):
    root = math.sqrt(2.0 / math.pi)
    square = value * value
    bend = jnp.tanh(root * value * (1.0 + 0.044715 * square))
    half = 0.5 * (1.0 + bend)
    slope = half + 0.5 * value * (1.0 - bend * bend) * (root * (1.0 + 3.0 * 0.044715 * square))
    return value * half, slope


def head_mask(width, index):
    lane = lax.broadcasted_iota(jnp.int32, (1, width), 1)
    size = width // HEADS
    inside = jnp.logical_and(lane >= index * size, lane < (index + 1) * size)
    return jnp.where(inside, 1.0, 0.0).astype(BF16)


def attend_heads(pairs, values, bias):
    width = values.shape[1]
    count = pairs[0][0].shape[0]
    column = lax.broadcasted_iota(jnp.int32, (count, 128), 1)
    mixed = jnp.zeros((count, width), F32)
    logs = jnp.zeros((count, 128), F32)
    for head in range(HEADS):
        mask = head_mask(width, head)
        scores = bias
        for queries, keys in pairs:
            scores = scores + dot_nt(queries * mask, keys)
        highest = jnp.max(scores, axis=-1, keepdims=True)
        weights = jnp.exp(scores - highest)
        total = jnp.sum(weights, axis=-1, keepdims=True)
        probs = (weights * (1.0 / total)).astype(BF16)
        mixed = mixed + dot_nn(probs, values * mask)
        logs = jnp.where(column == head, highest + jnp.log(total), logs)
    return mixed, logs


def attend_heads_back(pairs, values, bias, logs, grad_mixed, key_refs, value_ref):
    width = values.shape[1]
    size = width // HEADS
    turned_grad = grad_mixed.T
    turned_queries = [queries.T for queries, _ in pairs]
    grads = [jnp.zeros(queries.shape, F32) for queries, _ in pairs]
    for head in range(HEADS):
        mask = head_mask(width, head)
        log = logs[:, head : head + 1]
        scores = bias
        for queries, keys in pairs:
            scores = scores + dot_nt(queries * mask, keys)
        probs = jnp.exp(scores - log)
        grad_probs = dot_nt(grad_mixed * mask, values)
        inner = jnp.sum(probs * grad_probs, axis=-1, keepdims=True)
        grad_scores = (probs * (grad_probs - inner)).astype(BF16)
        part = slice(head * size, (head + 1) * size)
        value_ref[part, :] = dot_nn(turned_grad[part, :], probs.astype(BF16))
        for index, (queries, keys) in enumerate(pairs):
            key_refs[index][part, :] = dot_nn(turned_queries[index][part, :], grad_scores)
            grads[index] = grads[index] + dot_nn(grad_scores, keys * mask)
    return grads


def place_in_pair():
    return lax.axis_index("section"), lax.axis_index("seq")


def rows_at(half, count):
    return pl.ds(pl.multiple_of(half * count, count), count)


def token_bias(lengths, image, rows):
    seq = lax.axis_index("seq")
    lane = lax.broadcasted_iota(jnp.int32, (1, rows), 1)
    length = lengths[image]
    parts = [jnp.where((seq ^ bit) * rows + lane < length, 0.0, NEGATIVE) for bit in range(4)]
    return jnp.concatenate(parts, axis=1)


def query_bias(queries, padded):
    lane = lax.broadcasted_iota(jnp.int32, (1, padded), 1)
    return jnp.where(lane < queries, 0.0, NEGATIVE)


def put_halves(scratch, own, other):
    half = place_in_pair()[0]
    size = scratch.shape[0] // 2
    scratch[rows_at(half, size)] = own
    scratch[rows_at(1 - half, size)] = other
    return scratch[...]


def fetch(source, target, semaphore):
    copy = pltpu.make_async_copy(source, target, semaphore)
    copy.start()
    return copy


ENTERED, TARGET, KEY, VALUE, MINE, QUERY, MIXED = ((0, 2), (2, 4), (4, 6), (6, 8), (8, 9), (9, 10), (10, 11))
SUM, FIRST, LOGS = ((0, 1), (1, 2), (2, 3))


def kept_part(ref, part, own):
    return ref.at[part[0] * own : part[1] * own, :]


def pack_kernel(source, position, mine_o, near_o, far_o, farthest_o):
    width = source.shape[2]
    rows = near_o.shape[0]
    half, image = place_in_pair()
    part = rows_at(half, rows)
    for array, columns in ((source, slice(0, width)), (position, slice(width, 2 * width))):
        mine_o[:, columns] = array[image]
        for bit, out in ((1, near_o), (2, far_o), (3, farthest_o)):
            out[:, columns] = array[image ^ bit, part, :]


def stack_kernel(*refs):
    size = refs[0].shape[0]
    for index, ref in enumerate(refs[:-1]):
        refs[-1][index * size : (index + 1) * size, :] = ref[...]


def self_forward_kernel(
    scale, own, target, embed, attn, attn_bias, attn_out, gain, shift,
    low_o, full_o,
    arrived_s, target_s, embed_s, semaphore,
):
    width = embed.shape[1]
    padded = 2 * own
    queries = embed.shape[0]
    half, image = place_in_pair()
    copy = fetch(target.at[image], arrived_s, semaphore)
    embed_s[:queries] = embed[...]
    for scratch in (embed_s, target_s):
        scratch[queries:] = jnp.zeros((padded - queries, width), F32)
    copy.wait()
    target_s[:queries] = arrived_s[...]
    mine = rows_at(half, own)
    whole = target_s[...]
    own_target = target_s[mine]
    entered = (whole + embed_s[...]).astype(BF16)
    low = whole.astype(BF16)
    own_entered = (own_target + embed_s[mine]).astype(BF16)
    query = ((dot_nn(own_entered, attn[0]) + attn_bias[1, 0:1]) * scale).astype(BF16)
    key = dot_nn(entered, attn[1]).astype(BF16)
    value = (dot_nn(low, attn[2]) + attn_bias[1, 1:2]).astype(BF16)
    mixed, logs = attend_heads([(query, key)], value, query_bias(queries, padded))
    mixed = mixed.astype(BF16)
    first_sum = own_target + dot_nn(mixed, attn_out[...]) + attn_bias[1, 2:3]
    unit, _ = norm_parts(first_sum)
    parts = ((ENTERED, entered), (TARGET, low), (KEY, key), (VALUE, value), (MINE, own_entered), (QUERY, query), (MIXED, mixed))
    for part, values in parts:
        kept_part(low_o, part, own)[...] = values
    kept_part(full_o, SUM, own)[...] = first_sum
    kept_part(full_o, FIRST, own)[...] = unit * gain[2:3] + shift[2:3]
    full_o[LOGS[0] * own :, :128] = logs
    full_o[LOGS[0] * own :, 128:] = jnp.zeros((own, width - 128), F32)


def cross_query_kernel(
    cross_scale, own, points, full_d, tokens, period, cross, attn_bias,
    sine_o, content_o, place_o, place_key_o,
    points_s, spots_s,
):
    width = full_d.shape[1]
    first = kept_part(full_d, FIRST, own)
    half, image = place_in_pair()
    points_s[...] = jnp.zeros(points_s.shape, F32)
    points_s[: points.shape[1], : points.shape[2]] = points[image]
    spots_s[...] = points_s[...].T
    place_key_o[...] = dot_nn(tokens[:, width:], cross[3]).astype(BF16)
    content_o[...] = ((dot_nn(first[...].astype(BF16), cross[0]) + attn_bias[2, 0:1]) * cross_scale).astype(BF16)
    spots = spots_s[rows_at(half, own)]
    lane = lax.broadcasted_iota(jnp.int32, (1, width), 1)
    angle = jnp.where(lane < width // 2, spots[:, 1:2], spots[:, 0:1]) * (2.0 * math.pi) / period[...]
    sine = jnp.where(lane % 2 == 0, jnp.sin(angle), jnp.cos(angle)).astype(BF16)
    sine_o[...] = sine
    place_o[...] = (dot_nn(sine, cross[1]) * cross_scale).astype(BF16)


def encoder_forward_kernel(
    scale, lengths, chunk, arrived, others, attn, attn_bias, attn_out, ffn_in, ffn_in_bias, ffn_out, ffn_out_bias, gain, shift,
    query_o, key_o, value_o, mixed_o, logs_o, sum_o, second_o, memory_o, tokens_o,
):
    own, width = query_o.shape
    rows = chunk.shape[0]
    half = place_in_pair()[0]
    tokens_o[:rows, :] = chunk[...]
    part = rows // 2
    for index in range(3):
        source_rows = slice(index * part, (index + 1) * part)
        for place, ref in ((half, arrived), (1 - half, others)):
            tokens_o[pl.ds(pl.multiple_of((index + 1) * rows + place * part, part), part), :] = ref[source_rows, :]
    tokens = tokens_o[...]
    mine = tokens_o[rows_at(half, own)].astype(F32)
    own_source = mine[:, :width]
    own_entered = (own_source + mine[:, width:]).astype(BF16)
    source = tokens[:, :width]
    position = tokens[:, width:]
    bias = token_bias(lengths, place_in_pair()[1], rows)
    entered = (source.astype(F32) + position.astype(F32)).astype(BF16)
    query = ((dot_nn(own_entered, attn[0]) + attn_bias[0, 0:1]) * scale).astype(BF16)
    key = dot_nn(entered, attn[1]).astype(BF16)
    value = (dot_nn(source, attn[2]) + attn_bias[0, 1:2]).astype(BF16)
    mixed, logs = attend_heads([(query, key)], value, bias)
    mixed = mixed.astype(BF16)
    first_sum = own_source + dot_nn(mixed, attn_out[...]) + attn_bias[0, 2:3]
    unit, _ = norm_parts(first_sum)
    first = unit * gain[0:1] + shift[0:1]
    first_low = first.astype(BF16)
    second_sum = first + ffn_out_bias[0:1]
    inner_width = ffn_in.shape[1]
    for start in range(0, inner_width, width):
        part = slice(start, start + width)
        active, _ = gelu_parts(dot_nn(first_low, ffn_in[:, part]) + ffn_in_bias[0:1, part])
        second_sum = second_sum + dot_nn(active.astype(BF16), ffn_out[part, :])
    unit, _ = norm_parts(second_sum)
    query_o[...] = query
    key_o[...] = key
    value_o[...] = value
    mixed_o[...] = mixed
    logs_o[...] = logs
    sum_o[...] = first_sum
    second_o[...] = second_sum
    memory_o[...] = (unit * gain[1:2] + shift[1:2]).astype(BF16)


def cross_forward_kernel(
    lengths, memory_own, memory_other, place_key, full_d, content, place, grad_output,
    cross, attn_bias, attn_out, ffn_in, ffn_in_bias, ffn_out, ffn_out_bias, gain, shift,
    output_o, key_o, value_o, logs_o, grad_o, grad_mixed_o, keep_o, send_o, out_o, small_o,
    active_s, slope_s, piece_s, grad_s, arrived_s, memory_s, semaphore,
):
    own, width = content.shape
    first = kept_part(full_d, FIRST, own)
    queries = arrived_s.shape[0]
    half, image = place_in_pair()
    copy = fetch(grad_output.at[image], arrived_s, semaphore)
    bias = token_bias(lengths, image, memory_own.shape[0] // 2)
    memory = put_halves(memory_s, memory_own[...], memory_other[...])
    key = dot_nn(memory, cross[2]).astype(BF16)
    value = (dot_nn(memory, cross[4]) + attn_bias[2, 1:2]).astype(BF16)
    mixed, logs = attend_heads([(content[...], key), (place[...], place_key[...])], value, bias)
    mixed = mixed.astype(BF16)
    key_o[...] = key
    value_o[...] = value
    logs_o[...] = logs
    second_sum = first[...] + dot_nn(mixed, attn_out[...]) + attn_bias[2, 2:3]
    second_unit, second_scale = norm_parts(second_sum)
    second = second_unit * gain[3:4] + shift[3:4]
    second_low = second.astype(BF16)
    third_sum = second + ffn_out_bias[1:2]
    inner_width = ffn_in.shape[1]
    for start in range(0, inner_width, width):
        part = slice(start, start + width)
        active, slope = gelu_parts(dot_nn(second_low, ffn_in[:, part]) + ffn_in_bias[1:2, part])
        active = active.astype(BF16)
        active_s[:, part] = active
        slope_s[:, part] = slope
        third_sum = third_sum + dot_nn(active, ffn_out[part, :])
    unit, scale = norm_parts(third_sum)
    output_o[...] = (unit * gain[4:5] + shift[4:5]).astype(output_o.dtype)
    copy.wait()
    grad_s[:queries] = arrived_s[...]
    grad_s[queries:] = jnp.zeros((grad_s.shape[0] - queries, width), F32)
    grad_third, gain_five, shift_five = norm_back(grad_s[rows_at(half, own)], unit, scale, gain[4:5])
    branch = grad_third.astype(BF16)
    grad_second = grad_third
    for index, start in enumerate(range(0, inner_width, width)):
        part = slice(start, start + width)
        grad_inner = (dot_nt(branch, ffn_out[part, :]) * slope_s[:, part]).astype(BF16)
        grad_second = grad_second + dot_nt(grad_inner, ffn_in[:, part])
        piece_s[part, :] = dot_tn(second_low, grad_inner).astype(BF16)
        piece_s[inner_width + start : inner_width + start + width, :] = dot_tn(active_s[:, part], branch).astype(BF16)
        small_o[index : index + 1, :] = rows_sum(grad_inner)
    spread(piece_s, keep_o, send_o)
    grad_second_sum, gain_four, shift_four = norm_back(grad_second, second_unit, second_scale, gain[3:4])
    cross_out = grad_second_sum.astype(BF16)
    grad_o[...] = grad_second_sum
    grad_mixed_o[...] = dot_nt(cross_out, attn_out[...]).astype(BF16)
    out_o[...] = dot_tn(mixed, cross_out).astype(BF16)
    base = inner_width // width
    rest = [rows_sum(branch), gain_four, gain_five, shift_four, shift_five, rows_sum(cross_out)]
    for index, row in enumerate(rest):
        small_o[base + index : base + index + 1, :] = row
    small_o[base + len(rest) :, :] = jnp.zeros((small_o.shape[0] - base - len(rest), width), F32)


def cross_back_kernel(
    lengths, key, value, place_key, content, place, logs, grad_mixed, cross,
    memory_own_o, memory_other_o, grad_key_o, grad_place_key_o, grad_value_o, grad_content_o, grad_place_o,
    key_s, place_s, value_s, grad_s,
):
    own = memory_own_o.shape[0]
    bias = token_bias(lengths, place_in_pair()[1], own // 2)
    grad_content, grad_place = attend_heads_back(
        [(content[...], key[...]), (place[...], place_key[...])],
        value[...], bias, logs[...], grad_mixed[...], [key_s, place_s], value_s,
    )
    grad_key = key_s[...].T.astype(BF16)
    grad_value = value_s[...].T.astype(BF16)
    grad_memory = dot_nt(grad_key, cross[2]) + dot_nt(grad_value, cross[4])
    grad_s[...] = grad_memory
    half = place_in_pair()[0]
    memory_own_o[...] = grad_s[rows_at(half, own)]
    memory_other_o[...] = grad_s[rows_at(1 - half, own)].astype(BF16)
    grad_key_o[...] = grad_key
    grad_value_o[...] = grad_value
    grad_place_key_o[...] = place_s[...].T.astype(BF16)
    grad_content_o[...] = grad_content.astype(BF16)
    grad_place_o[...] = grad_place.astype(BF16)


def self_back_kernel(
    scale, cross_scale, queries,
    low_d, full_d, sine, grad_second_sum,
    memory_own, memory_other, tokens, grad_key, grad_place_key, grad_value, grad_content, grad_place, cross_out, small_c,
    attn, attn_out, cross, gain, shift,
    target_own_o, target_other_o, grads_o,
    key_s, value_s, rows_s, memory_s,
):
    own, width = sine.shape
    padded = 2 * own
    low = lambda part: kept_part(low_d, part, own)[...]
    logs = full_d[LOGS[0] * own :, :128]
    half = place_in_pair()[0]
    mine, other = rows_at(half, own), rows_at(1 - half, own)
    unit, norm_scale = norm_parts(kept_part(full_d, SUM, own)[...])
    first_low = (unit * gain[2:3] + shift[2:3]).astype(BF16)
    grad_first = grad_second_sum[...] + cross_scale * dot_nt(grad_content[...], cross[...])
    grad_first_sum, gain_three, shift_three = norm_back(grad_first, unit, norm_scale, gain[2:3])
    branch = grad_first_sum.astype(BF16)
    grad_mixed = dot_nt(branch, attn_out[...]).astype(BF16)
    (grad_query,) = attend_heads_back(
        [(low(QUERY), low(KEY))], low(VALUE), query_bias(queries, padded), logs, grad_mixed, [key_s], value_s
    )
    grad_query = grad_query.astype(BF16)
    self_key = key_s[...].T.astype(BF16)
    self_value = value_s[...].T.astype(BF16)
    from_query = scale * dot_nt(grad_query, attn[0])
    from_key = dot_nt(self_key, attn[1])
    from_value = dot_nt(self_value, attn[2])
    rows_s[...] = from_key + from_value
    target_own_o[...] = rows_s[mine] + grad_first_sum + from_query
    target_other_o[...] = rows_s[other].astype(BF16)
    rows_s[...] = from_key
    rows_s[mine] += from_query
    position = tokens[:, width:]
    memory = put_halves(memory_s, memory_own[...], memory_other[...])
    small = [
        scale * rows_sum(grad_query),
        rows_sum(self_value),
        rows_sum(branch),
        cross_scale * rows_sum(grad_content[...]),
        rows_sum(grad_value[...]),
        gain_three,
        shift_three,
        jnp.zeros((9, width), F32),
    ]
    grads = [
        scale * dot_tn(low(MINE), grad_query),
        dot_tn(low(ENTERED), self_key),
        dot_tn(low(TARGET), self_value),
        dot_tn(low(MIXED), branch),
        cross_scale * dot_tn(first_low, grad_content[...]),
        cross_scale * dot_tn(sine[...], grad_place[...]),
        dot_tn(memory, grad_key[...]),
        dot_tn(position, grad_place_key[...]),
        dot_tn(memory, grad_value[...]),
        cross_out[...],
        rows_s[...],
        small_c[...],
        jnp.concatenate(small, axis=0),
    ]
    fill(grads_o, grads)


def encoder_ffn_back_kernel(
    grad_own, grad_other, first_sum, second_sum, mixed, attn_out, ffn_in, ffn_in_bias, ffn_out, gain, shift,
    grad_o, grad_mixed_o, keep_o, send_o, out_o, small_o,
    piece_s,
):
    width = first_sum.shape[1]
    inner_width = ffn_in.shape[1]
    grad_memory = (grad_own[...] + grad_other[...].astype(F32)).astype(BF16).astype(F32)
    second_unit, second_scale = norm_parts(second_sum[...])
    grad_second, gain_two, shift_two = norm_back(grad_memory, second_unit, second_scale, gain[1:2])
    branch = grad_second.astype(BF16)
    unit, scale = norm_parts(first_sum[...])
    first_low = (unit * gain[0:1] + shift[0:1]).astype(BF16)
    grad_first = grad_second
    for index, start in enumerate(range(0, inner_width, width)):
        part = slice(start, start + width)
        active, slope = gelu_parts(dot_nn(first_low, ffn_in[:, part]) + ffn_in_bias[0:1, part])
        grad_inner = (dot_nt(branch, ffn_out[part, :]) * slope).astype(BF16)
        grad_first = grad_first + dot_nt(grad_inner, ffn_in[:, part])
        piece_s[part, :] = dot_tn(first_low, grad_inner).astype(BF16)
        piece_s[inner_width + start : inner_width + start + width, :] = dot_tn(active.astype(BF16), branch).astype(BF16)
        small_o[index : index + 1, :] = rows_sum(grad_inner)
    spread(piece_s, keep_o, send_o)
    grad_first_sum, gain_one, shift_one = norm_back(grad_first, unit, scale, gain[0:1])
    attention = grad_first_sum.astype(BF16)
    out_o[...] = dot_tn(mixed[...], attention).astype(BF16)
    grad_o[...] = grad_first_sum
    grad_mixed_o[...] = dot_nt(attention, attn_out[...]).astype(BF16)
    base = inner_width // width
    rest = [rows_sum(branch), gain_one, gain_two, shift_one, shift_two, rows_sum(attention)]
    for index, row in enumerate(rest):
        small_o[base + index : base + index + 1, :] = row
    small_o[base + len(rest) :, :] = jnp.zeros((small_o.shape[0] - base - len(rest), width), F32)


def encoder_attention_back_kernel(
    scale, lengths, tokens, query, key, value, logs, grad_first_sum, grad_mixed, encoder_out, small_e, decoder_grads, attn,
    source_o, source_low_o, keep_o, send_o,
    key_s, value_s, piece_s, source_s, tokens_s,
):
    own, width = query.shape
    rows = tokens.shape[0] // 4
    bias = token_bias(lengths, place_in_pair()[1], rows)
    (grad_query,) = attend_heads_back(
        [(query[...], key[...])], value[...], bias, logs[...], grad_mixed[...], [key_s], value_s
    )
    grad_query = grad_query.astype(BF16)
    grad_key = key_s[...].T.astype(BF16)
    grad_value = value_s[...].T.astype(BF16)
    from_query = grad_first_sum[...] + scale * dot_nt(grad_query, attn[0])
    grad_source = dot_nt(grad_key, attn[1]) + dot_nt(grad_value, attn[2])
    mine = rows_at(place_in_pair()[0], own)
    source_s[...] = grad_source
    source_s[mine] += from_query
    source_o[...] = source_s[...]
    source_low_o[...] = source_s[...].astype(BF16)
    source = tokens[:, :width]
    entered = (source.astype(F32) + tokens[:, width:].astype(F32)).astype(BF16)
    tokens_s[...] = entered
    grads = [
        scale * dot_tn(tokens_s[mine], grad_query),
        dot_tn(entered, grad_key),
        dot_tn(source, grad_value),
        encoder_out[...],
        small_e[...],
        jnp.concatenate([scale * rows_sum(grad_query), rows_sum(grad_value), jnp.zeros((14, width), F32)], axis=0),
        decoder_grads[...],
    ]
    fill(piece_s, grads)
    spread(piece_s, keep_o, send_o)


PARTS = 16


def place_code(core):
    spot = lax.axis_index("dp")
    low, high = spot % 2, spot // 2
    swap = core == 1
    first, second = jnp.where(swap, high, low), jnp.where(swap, low, high)
    return first * 4 + second * 2 + lax.axis_index("seq") % 2


def fill(piece, grads):
    start = 0
    for grad in grads:
        piece[start : start + grad.shape[0], :] = grad.astype(BF16)
        start += grad.shape[0]
    if start < piece.shape[0]:
        piece[start:, :] = jnp.zeros((piece.shape[0] - start, piece.shape[1]), BF16)


def spread(piece, keep_o, send_o):
    half = PARTS // 2
    count = piece.shape[0] // PARTS
    me = lax.axis_index("section")
    for core, out in ((me, keep_o), (1 - me, send_o)):
        code = place_code(core)
        for slot in range(half):
            out[slot * count : (slot + 1) * count, :] = piece[rows_at(core * half + (slot ^ code), count), :]


def added(first, second):
    return (first.astype(F32) + second.astype(F32)).astype(BF16)


def add_whole_kernel(own, arrived, out):
    out[...] = added(own[...], arrived[...])


def add_split_kernel(own, arrived, keep_o, send_o):
    size = keep_o.shape[0]
    keep_o[...] = added(own[:size, :], arrived[:size, :])
    send_o[...] = added(own[size:, :], arrived[size:, :])


def join_kernel(near, far, out):
    size = near.shape[0]
    out[:size, :] = near[...]
    out[size:, :] = far[...]


def crossed(block, axis, bit):
    return lax.ppermute(block, axis, [(index, index ^ bit) for index in range(lax.axis_size(axis))])


def crossed_plane(block, step):
    pairs = []
    for spot in range(lax.axis_size("dp")):
        for core in range(2):
            pairs.append((spot * 2 + core, (spot ^ (1 if core == step else 2)) * 2 + core))
    return lax.ppermute(block, ("dp", "section"), pairs)


def reduce_steps(keep, send):
    size, width = keep.shape
    low = lambda rows: ((rows, width), BF16)
    moves = [
        lambda block: crossed(block, "section", 1),
        lambda block: crossed_plane(block, 0),
        lambda block: crossed_plane(block, 1),
        lambda block: crossed(block, "seq", 1),
        lambda block: crossed(block, "seq", 2),
    ]
    for move in moves[:3]:
        after, micros = yield keep
        size //= 2
        keep, send = run(add_split_kernel, [low(size)] * 2, [keep, move(send)], after=after, micros=micros)
    after, micros = yield keep
    (total,) = run(add_whole_kernel, [low(size)], [keep, moves[3](send)], after=after, micros=micros)
    after, micros = yield total
    (total,) = run(add_whole_kernel, [low(size)], [total, moves[4](total)], after=after, micros=micros)
    for move in reversed(moves[1:4]):
        after, micros = yield total
        size *= 2
        (total,) = run(join_kernel, [low(size)], [total, move(total)], after=after, micros=micros)
    yield total, moves[0](total)


class Piece:
    def __init__(self, keep, send):
        self.steps = reduce_steps(keep, send)
        next(self.steps)

    def step(self, *after, micros=0.1):
        return self.steps.send((after, micros))

    def finish(self, *after, micros=0.1):
        result = self.step(*after, micros=micros)
        while not isinstance(result, tuple):
            result = self.step(micros=micros)
        return result


def part_rows(near, far, start, rows, write):
    half = PARTS // 2
    count = near.shape[0] // half
    me = lax.axis_index("section")
    for part in range(start // count, -(-(start + rows) // count)):
        core = part // half
        slot = (part % half) ^ place_code(core)
        for ref, here in ((near, me == core), (far, me != core)):

            @pl.when(here)
            def _():
                write(part * count - start, ref[rows_at(slot, count), :].astype(F32))


def ffn_result_kernel(*refs):
    near, far = refs[:2]
    in_o, out_o = refs[-2:]
    inner_width, width = out_o.shape

    def write_in(offset, values):
        for start in range(0, values.shape[0], width):
            block = (offset + start) // width
            row = (offset + start) % width
            part = values[start : start + width]
            in_o[row : row + part.shape[0], block * width : (block + 1) * width] = part

    def write_out(offset, values):
        out_o[offset : offset + values.shape[0], :] = values

    part_rows(near, far, 0, inner_width, write_in)
    part_rows(near, far, inner_width, inner_width, write_out)


def rest_result_kernel(
    padded, near, far, attn_o, out_o, attn_bias_o, cross_o, ffn_in_bias_o, ffn_out_bias_o, gain_o, shift_o, embed_o, piece_s
):
    width = gain_o.shape[1]

    def write(offset, values):
        piece_s[offset : offset + values.shape[0], :] = values

    part_rows(near, far, 0, piece_s.shape[0], write)
    encoder = 4 * width
    decoder = encoder + 32
    late = decoder + 10 * width + padded
    block = lambda start, index: piece_s[start + index * width : start + (index + 1) * width, :]
    for index in range(3):
        attn_o[0, index] = block(0, index)
        attn_o[1, index] = block(decoder, index)
    out_o[0] = block(0, 3)
    out_o[1] = block(decoder, 3)
    out_o[2] = block(decoder, 9)
    for index in range(5):
        cross_o[index] = block(decoder, 4 + index)
    embed_o[...] = piece_s[decoder + 10 * width : decoder + 10 * width + embed_o.shape[0], :]
    row = lambda start: piece_s[start : start + 1, :]
    blocks = ffn_in_bias_o.shape[1] // width
    row_e = lambda index: row(encoder + index)
    row_a = lambda index: row(encoder + 16 + index)
    row_c = lambda index: row(late + index)
    row_d = lambda index: row(late + 16 + index)
    bias = [
        row_a(0), row_a(1), row_e(blocks + 5),
        row_d(0), row_d(1), row_d(2),
        row_d(3), row_d(4), row_c(blocks + 5),
    ]
    for index, values in enumerate(bias):
        attn_bias_o[index // 3, index % 3 : index % 3 + 1, :] = values
    for index in range(blocks):
        part = slice(index * width, (index + 1) * width)
        ffn_in_bias_o[0:1, part] = row_e(index)
        ffn_in_bias_o[1:2, part] = row_c(index)
    ffn_out_bias_o[0:1, :] = row_e(blocks)
    ffn_out_bias_o[1:2, :] = row_c(blocks)
    for index, out in ((1, gain_o), (3, shift_o)):
        rows = [row_e(blocks + index), row_e(blocks + index + 1), row_d(5 + index // 2)]
        rows += [row_c(blocks + index), row_c(blocks + index + 1)]
        for place, values in enumerate(rows):
            out[place : place + 1, :] = values


def is_home():
    return lax.axis_index("seq") // 2 == lax.axis_index("section")


def sent_far(block):
    pairs = []
    for core in range(2):
        for spot in range(4):
            if spot // 2 == core:
                pairs.append((core * 4 + spot, core * 4 + (spot ^ 2)))
    return lax.ppermute(block, ("section", "seq"), pairs)


def queries_pack_kernel(output, target_own, target_arrived, out):
    own = output.shape[0]
    out[:own, :] = output[...]
    out[own:, :] = (target_own[...] + target_arrived[...].astype(F32)).astype(BF16)


def chosen_kernel(home, arrived, out):
    @pl.when(is_home())
    def _():
        out[...] = home[...]

    @pl.when(jnp.logical_not(is_home()))
    def _():
        out[...] = arrived[...]


def queries_result_kernel(mine, near, output_o, target_o, rows_s):
    own = mine.shape[0] // 4
    core = lax.axis_index("section")
    spot = lax.axis_index("seq") % 2
    for index, out in enumerate((output_o, target_o)):
        for image, ref in ((spot, mine), (1 - spot, near)):
            for half in range(2):
                start = (2 * half + index) * own
                place = core if half == 0 else 1 - core
                rows_s[image, rows_at(place, own), :] = ref[start : start + own, :].astype(F32)
        out[...] = rows_s[:, : out.shape[1], :]


def source_sum_kernel(own, arrived, keep_o, send_o):
    size = keep_o.shape[0]
    total = own[...] + arrived[...].astype(F32)
    keep_o[...] = total[:size]
    send_o[...] = total[size:].astype(BF16)


def source_pair_kernel(home, arrived, keep_o, send_o):
    rows = keep_o.shape[0]

    @pl.when(is_home())
    def _():
        keep_o[...] = home[:rows, :]
        send_o[...] = home[rows:, :].astype(BF16)

    @pl.when(jnp.logical_not(is_home()))
    def _():
        keep_o[...] = arrived[:rows, :].astype(F32)
        send_o[...] = arrived[rows:, :]


def source_result_kernel(mine, near, out_o):
    spot = lax.axis_index("seq") % 2
    out_o[spot] = mine[...]
    out_o[1 - spot] = near[...].astype(F32)


def whole_spec(shape):
    return pl.BlockSpec(shape, lambda step: (0,) * len(shape))


def part_spec(shape, index):
    return pl.BlockSpec((None,) + shape[1:], lambda step: (index,) + (0,) * (len(shape) - 1))


def run(kernel, outs, operands, scratch=(), micros=1.0, limit=16, after=(), hold=()):
    arrays, specs, places = [], [], []
    for operand in operands:
        array, extra = operand if isinstance(operand, tuple) else (operand, None)
        spec = extra if isinstance(extra, pl.BlockSpec) else pl.BlockSpec(memory_space=pltpu.VMEM)
        arrays.append(array)
        specs.append(spec)
        places.append(extra if isinstance(extra, int) else None)

    def body(*refs):
        parts = [ref if place is None else ref.at[place] for ref, place in zip(refs, places)]
        kernel(*parts, *refs[len(places) + len(after) + len(hold) :])

    return pl.pallas_call(
        body,
        name=getattr(kernel, "func", kernel).__name__,
        out_shape=[jax.ShapeDtypeStruct(shape, dtype) for shape, dtype in outs],
        in_specs=specs + [pl.BlockSpec(memory_space=pl.ANY)] * len(after) + [pl.BlockSpec(memory_space=pltpu.VMEM)] * len(hold),
        out_specs=[pl.BlockSpec(memory_space=pltpu.VMEM) for _ in outs],
        scratch_shapes=[pltpu.VMEM(*item) if isinstance(item, tuple) else item for item in scratch],
        compiler_params=pltpu.CompilerParams(vmem_limit_bytes=limit * 1024 * 1024),
        cost_estimate=pl.CostEstimate(flops=int(micros * 1.15e9), bytes_accessed=1024, transcendentals=0),
    )(*arrays, *after, *hold)


def run_parts(kernel, outs, operands, scratch=(), aliases=None, micros=2.0, after=()):
    arrays, specs = [], []
    for operand in operands:
        array, spec = operand if isinstance(operand, tuple) else (operand, whole_spec(operand.shape))
        arrays.append(array)
        specs.append(spec)
    count = len(specs) + len(after)

    def body(*refs):
        kernel(*refs[: len(specs)], *refs[count : count + len(outs)], *refs[count + len(outs) + 1 :])
        refs[count + len(outs)][...] = jnp.zeros((8, 128), F32)

    return pl.pallas_call(
        body,
        name=getattr(kernel, "func", kernel).__name__,
        grid=(1,),
        out_shape=[jax.ShapeDtypeStruct(out[0], out[1]) for out in outs] + [jax.ShapeDtypeStruct((8, 128), F32)],
        in_specs=specs + [pl.BlockSpec(memory_space=pl.ANY)] * len(after),
        out_specs=[out[2] if len(out) > 2 else whole_spec(out[0]) for out in outs] + [whole_spec((8, 128))],
        scratch_shapes=[pltpu.VMEM(shape, dtype) for shape, dtype in scratch],
        input_output_aliases=aliases or {},
        compiler_params=pltpu.CompilerParams(vmem_limit_bytes=24 * 1024 * 1024),
        cost_estimate=pl.CostEstimate(flops=int(micros * 1.15e9), bytes_accessed=1024, transcendentals=0),
    )(*arrays, *after)


def traded(block, bit):
    return crossed(block, "seq", bit)


def with_pair(block):
    return crossed(block, "section", 1)


BEFORE = "d"
AFTER = "edqwperwdewdeswtdewedweewhDEuw"


def paired_device(
    source, position, lengths, target, points, grad_output,
    attn, attn_out, attn_bias, cross, ffn_in, ffn_in_bias, ffn_out, ffn_out_bias, norm_gain, norm_bias, query_embed,
):
    batches, rows, width = source.shape
    queries = target.shape[1]
    inner_width = ffn_in.shape[2]
    images = batches // lax.axis_size("section")
    tokens = rows * lax.axis_size("seq")
    half_tokens = tokens // 2
    half_queries = -(-queries // 32) * 16
    padded = 2 * half_queries
    head = width // HEADS
    scale = head ** (-0.5)
    cross_scale = (2 * head) ** (-0.5)
    wide = lambda count: ((count, 2 * width), BF16)
    chunk, *parts = run(pack_kernel, [wide(rows)] + [wide(rows // 2)] * 3, [source, position])
    parts = [traded(part, bit + 1) for bit, part in enumerate(parts)]

    column = np.arange(width) % (width // 2)
    period = (10000.0 ** ((2 * (column // 2)).astype(np.float32) / np.float32(width // 2))).astype(np.float32)[None]
    lengths = (lengths, pl.BlockSpec(memory_space=pltpu.SMEM))
    low = lambda count, columns=width: ((count, columns), BF16)
    full = lambda count, columns=width: ((count, columns), F32)
    part = lambda array, index: (array, index)

    elsewhere = lambda array: (array, pl.BlockSpec(memory_space=pl.ANY))
    copied = pltpu.SemaphoreType.DMA
    lanes = -(-padded // 128) * 128

    low_d, full_d = run(
        functools.partial(self_forward_kernel, scale, half_queries),
        [low(11 * half_queries), full(3 * half_queries)],
        [elsewhere(target), query_embed, part(attn, 1), attn_bias, part(attn_out, 1), norm_gain, norm_bias],
        [full(queries), full(padded), full(padded), copied], micros=12.0,
    )

    (arrived,) = run(stack_kernel, [wide(3 * rows // 2)], parts, after=[low_d], hold=[ffn_in, ffn_out])
    query_e, key_e, value_e, mixed_e, logs_e, sum_e, second_e, memory, token_rows = run(
        functools.partial(encoder_forward_kernel, scale),
        [low(half_tokens), low(tokens), low(tokens), low(half_tokens), full(half_tokens, 128),
         full(half_tokens), full(half_tokens), low(half_tokens), wide(tokens)],
        [lengths, chunk, arrived, with_pair(arrived), part(attn, 0), attn_bias, part(attn_out, 0),
         part(ffn_in, 0), ffn_in_bias, part(ffn_out, 0), ffn_out_bias, norm_gain, norm_bias], micros=21.0, after=[low_d],
    )

    sine, content, place_query, place_key = run(
        functools.partial(cross_query_kernel, cross_scale, half_queries),
        [low(half_queries), low(half_queries), low(half_queries), low(tokens)],
        [points.transpose(0, 2, 1), full_d, token_rows, jnp.asarray(period), cross, attn_bias],
        [full(8, lanes), full(lanes, 8)], micros=6.0, after=[mixed_e],
    )
    memory_other = with_pair(memory)
    piece = lambda rows: [low(rows // 2)] * 2
    output_half, cross_key, cross_value, logs_c, grad_second_sum, grad_cross_mixed, keep_d, send_d, out_c, small_c = run(
        cross_forward_kernel,
        [low(half_queries), low(tokens), low(tokens), full(half_queries, 128), full(half_queries), low(half_queries),
         *piece(2 * inner_width), low(width), full(16)],
        [lengths, memory, memory_other, place_key, full_d, content, place_query, elsewhere(grad_output),
         cross, attn_bias, part(attn_out, 2), part(ffn_in, 1), ffn_in_bias, part(ffn_out, 1), ffn_out_bias, norm_gain, norm_bias],
        [low(half_queries, inner_width), full(half_queries, inner_width), low(2 * inner_width), full(padded), full(queries), low(tokens), copied],
        micros=30.0,
    )
    piece_d = Piece(keep_d, send_d)

    memory_grad_own, memory_grad_other, grad_key, grad_place_key, grad_value, grad_content, grad_place = run(
        cross_back_kernel,
        [full(half_tokens), low(half_tokens), low(tokens), low(tokens), low(tokens), low(half_queries), low(half_queries)],
        [lengths, cross_key, cross_value, place_key, content, place_query, logs_c, grad_cross_mixed, cross],
        [full(width, tokens)] * 3 + [full(tokens)],
        micros=21.0,
    )
    memory_grad_partner = with_pair(memory_grad_other)

    count_d = 10 * width + padded + 32
    target_own, target_other, grads_d = run(
        functools.partial(self_back_kernel, scale, cross_scale, queries),
        [full(half_queries), low(half_queries), low(count_d)],
        [low_d, full_d, sine, grad_second_sum, memory, memory_other, token_rows,
         grad_key, grad_place_key, grad_value, grad_content, grad_place, out_c, small_c,
         part(attn, 1), part(attn_out, 1), part(cross, 0), norm_gain, norm_bias],
        [full(width, padded), full(width, padded), full(padded), low(tokens)], micros=18.0, after=[piece_d.step()],
    )

    grad_first_sum, grad_mixed, keep_e, send_e, out_e, small_e = run(
        encoder_ffn_back_kernel,
        [full(half_tokens), low(half_tokens), *piece(2 * inner_width), low(width), full(16)],
        [memory_grad_own, memory_grad_partner, sum_e, second_e, mixed_e, part(attn_out, 0),
         part(ffn_in, 0), ffn_in_bias, part(ffn_out, 0), norm_gain, norm_bias],
        [low(2 * inner_width)], micros=21.0, after=[grads_d, piece_d.step()],
    )
    piece_e = Piece(keep_e, send_e)

    count_w = -(-(4 * width + 32 + count_d) // (16 * PARTS)) * 16 * PARTS
    source_full, source_low, keep_w, send_w = run(
        functools.partial(encoder_attention_back_kernel, scale),
        [full(tokens), low(tokens), *piece(count_w)],
        [lengths, token_rows, query_e, key_e, value_e, logs_e, grad_first_sum, grad_mixed, out_e, small_e, grads_d, part(attn, 0)],
        [full(width, tokens), full(width, tokens), low(count_w), full(tokens), low(tokens)],
        micros=21.0, after=[{"d": piece_d, "e": piece_e}[step].step() for step in BEFORE],
    )
    piece_w = Piece(keep_w, send_w)

    def kept(shape, index):
        return (shape, F32, part_spec(shape, index))

    pieces = dict(d=piece_d, e=piece_e, w=piece_w)
    sums = {}
    packed_halves = [output_half, target_own, with_pair(target_other)]
    mark = keep_w
    short = {AFTER.rindex("e"): 0.1, AFTER.rindex("w", 0, -1): 3.0}
    for place, step in enumerate(AFTER):
        if step in pieces:
            result = pieces[step].step(mark, micros=short.get(place, 6.0))
            if isinstance(result, tuple):
                sums[step] = result
                result = result[0]
            mark = result
        elif step == "q":
            (halves,) = run(queries_pack_kernel, [low(2 * half_queries)], packed_halves, after=[mark], micros=6.0)
            mark = halves
        elif step == "r":
            (halves,) = run(join_kernel, [low(4 * half_queries)], [halves, with_pair(halves)], after=[mark], micros=6.0)
            mark = halves
        elif step == "h":
            (halves,) = run(chosen_kernel, [low(4 * half_queries)], [halves, sent_far(halves)], after=[mark], micros=6.0)
            mark = halves
        elif step == "u":
            decoder_output, grad_target, mark = run_parts(
                queries_result_kernel, [((images, queries, width), F32)] * 2, [halves, traded(halves, 1)],
                [((images, padded, width), F32)], after=[mark],
            )
        elif step == "p":
            source_home, source_far = run(
                source_sum_kernel, [full(half_tokens), low(half_tokens)], [source_full, with_pair(source_low)], after=[mark], micros=6.0
            )
            mark = source_home
        elif step == "s":
            source_mine, source_near = run(
                source_pair_kernel, [full(rows), low(rows)], [source_home, sent_far(source_far)], after=[mark], micros=6.0
            )
            mark = source_mine
        elif step == "t":
            grad_source, mark = run_parts(
                source_result_kernel, [((images, rows, width), F32)], [source_mine, traded(source_near, 1)], after=[mark]
            )
        elif step == "D":
            *grad_ffn, mark = run_parts(
                ffn_result_kernel, [kept(ffn_in.shape, 1), kept(ffn_out.shape, 1)], sums["d"], after=[mark]
            )
        elif step == "E":
            before = [(array, pl.BlockSpec(memory_space=pl.ANY)) for array in grad_ffn]
            *grad_ffn, mark = run_parts(
                ffn_result_kernel, [kept(ffn_in.shape, 0), kept(ffn_out.shape, 0)], [*sums["e"], *before], aliases={2: 0, 3: 1}, after=[mark]
            )
    grad_ffn_in, grad_ffn_out = grad_ffn
    rest = (attn, attn_out, attn_bias, cross, ffn_in_bias, ffn_out_bias, norm_gain, norm_bias, query_embed)
    *grads, _ = run_parts(
        functools.partial(rest_result_kernel, padded), [(array.shape, F32) for array in rest],
        sums["w"], [full(count_w)]
    )
    grad_attn, grad_attn_out, grad_attn_bias, grad_cross, grad_ffn_in_bias, grad_ffn_out_bias, grad_gain, grad_shift, grad_embed = grads
    return (
        decoder_output, grad_source, grad_target, grad_attn, grad_attn_out, grad_attn_bias, grad_cross,
        grad_ffn_in, grad_ffn_in_bias, grad_ffn_out, grad_ffn_out_bias, grad_gain, grad_shift, grad_embed,
    )


def chosen_plan(*args):
    batches = args[0].shape[0]
    sections = lax.axis_size("section")
    paired = sections == 2 and batches == lax.axis_size("seq") == lax.axis_size("dp") == 4
    return (paired_device if paired else per_device)(*args)


def solution(mesh):
    placed = (
        P("dp", "seq", None),
        P("dp", "seq", None),
        P("dp"),
        P("dp", None, None),
        P("dp", None, None),
        P("dp", None, None),
        P(),
        P(),
        P(),
        P(),
        P(),
        P(),
        P(),
        P(),
        P(),
        P(),
        P(),
    )
    return jax.shard_map(
        chosen_plan,
        mesh=mesh,
        in_specs=placed,
        out_specs=(
            P(("dp", "section"), None, None),
            P(("dp", "section"), "seq", None),
            P(("dp", "section"), None, None),
            P(),
            P(),
            P(),
            P(),
            P(),
            P(),
            P(),
            P(),
            P(),
            P(),
            P(),
        ),
        check_vma=False,
    )
```
